256 devices in a mesh: gz: 16 (over y, x), gy: 2 (over z_lo), af: 8 (over z_hi, core).
Axes of the slice: x: 4, y: 4, z: 8 (z_hi: 4, z_lo: 2; z = z_hi * 2 + z_lo), core: 2. Of those that a mesh axis runs over, the one named last changes fastest.
Arguments:
- features: bfloat16 [256, 32, 1024], P('af', 'gz', 'gy'), may hold values from -6 to 6
- filters: bfloat16 [3, 3, 3, 256, 256], P(None, None, None, 'af'), may hold values from -0.078125 to 0.078125
- cotangent: bfloat16 [256, 32, 1024], P('af', 'gz', 'gy'), may hold values from -6 to 6
Outputs:
- response: bfloat16 [256, 32, 1024], P('af', 'gz', 'gy')
- input_grad: bfloat16 [256, 32, 1024], P('af', 'gz', 'gy')
- filter_grad: float32 [3, 3, 3, 256, 256], P(None, None, None, 'af')
The draws below stay inside these ranges and needn't reach their ends.
All inputs are finite; a program needn't handle non-finite values.
Results may differ from the reference program's by a relative error of at most 0.0013.
Values may be sent and summed in bfloat16 or wider, within the bound.
A program may use at most 64 MiB of HBM per device.

```python
import jax
import jax.numpy as jnp

C = 256
WIDTH = 64
DEPTH = 32
HEIGHT = 16
NCELLS = 32768


def shard_levels(own_key, extent, cuts, low, top_value):
    def one(axis_at, shards_of):
        heights = jax.random.uniform(jax.random.fold_in(jax.random.fold_in(own_key, 6), axis_at), (shards_of,), jnp.float32, low / len(cuts), top_value / len(cuts))
        return jnp.repeat(jnp.exp(heights), extent[axis_at] // shards_of).reshape((-1,) + (1,) * (len(extent) - axis_at - 1))

    gain = one(*cuts[0])
    for cut in cuts[1:]:
        gain = gain * one(*cut)
    return gain


def normal_values(rng, extent, deviation, limit, pieces=(), kind=jnp.bfloat16):
    values = deviation * jax.random.normal(rng, extent, jnp.float32)
    if pieces:
        values = values * shard_levels(rng, extent, pieces, -0.22, 0.18)
    return jnp.clip(values, -limit, limit).astype(kind)


def setup_inputs(seed: int = 0) -> dict:
    key_list = jax.random.split(jax.random.key(seed), 4)
    features = normal_values(key_list[0], (C, DEPTH, HEIGHT * WIDTH), 1.0, 6.0, ((0, 8), (1, 16), (2, 2)))
    filters = normal_values(key_list[1], (3, 3, 3, C, C), (27 * C) ** -0.5, 0.078125, ((3, 8),))
    cotangent = normal_values(key_list[2], (C, DEPTH, HEIGHT * WIDTH), 1.0, 6.0, ((0, 8), (1, 16), (2, 2)))
    return {"features": features, "filters": filters, "cotangent": cotangent}


def shifted(padded, offs, depth, height, width):
    a, b, c = offs
    return padded[:, 1 + a:1 + a + depth, 1 + b:1 + b + height, 1 + c:1 + c + width]

def reference(features, filters, cotangent):
    chans = features.shape[0]
    depth = DEPTH
    height = HEIGHT
    width = WIDTH
    field = features.astype(jnp.float32).reshape(chans, depth, height, width)
    grads = cotangent.astype(jnp.float32).reshape(chans, depth, height, width)
    taps = filters.astype(jnp.float32)
    field_pad = jnp.pad(field, ((0, 0), (1, 1), (1, 1), (1, 1)))
    grads_pad = jnp.pad(grads, ((0, 0), (1, 1), (1, 1), (1, 1)))
    response = jnp.zeros((chans, depth, height, width), jnp.float32)
    backward = jnp.zeros((chans, depth, height, width), jnp.float32)
    filter_rows = []
    for tz in range(3):
        for ty in range(3):
            for tx in range(3):
                offs = (tz - 1, ty - 1, tx - 1)
                back = (1 - tz, 1 - ty, 1 - tx)
                tap = taps[tz, ty, tx]
                source = shifted(field_pad, offs, depth, height, width)
                response = response + jnp.einsum('oc,cdhw->odhw', tap, source)
                backward = backward + jnp.einsum('oc,odhw->cdhw', tap, shifted(grads_pad, back, depth, height, width))
                filter_rows.append(jnp.einsum('odhw,cdhw->oc', grads, source))
    scale = 1.0 / jnp.sqrt(jnp.float32(NCELLS))
    filter_grad = jnp.stack(filter_rows).reshape(3, 3, 3, chans, chans) * scale
    shape = features.shape
    return (response.reshape(shape).astype(jnp.bfloat16), backward.reshape(shape).astype(jnp.bfloat16), filter_grad)
```

```python
import math

import jax
import jax.numpy as jnp
from jax import lax
from jax.experimental import pallas as pl
from jax.experimental.pallas import tpu as pltpu
from jax.sharding import PartitionSpec as P

MESH = pl.DeviceIdType.MESH
F32 = jnp.float32
BF16 = jnp.bfloat16
WIDTH = 64
PLANE = 512
CELLS = 1024
OWN = 32
C = 256
TAPS = 27
ROWS = TAPS * OWN
CHUNK = ROWS // 4
SPLIT = 112
N_COPIES = 96


def tap_index(a, b, c):
    return ((a + 1) * 3 + (b + 1)) * 3 + (c + 1)


def roll(x, shift):
    return pltpu.roll(x, shift % x.shape[1], 1)


def aligned(start, size, unit):
    return pl.ds(pl.multiple_of(start, unit), size)


class Ring:
    def __init__(self, send, chunk, rows, split, pos, nxt, prv, first, from_prv, from_nxt):
        self.send, self.chunk, self.rows, self.split = send, chunk, rows, split
        self.pos, self.nxt, self.prv = pos, nxt, prv
        self.first, self.from_prv, self.from_nxt = first, from_prv, from_nxt

    def start(self):
        low, high = self.split, self.rows - self.split
        far, up, down = ((self.pos + k) % 4 for k in (2, 1, 3))
        self.far_low = self.send(self.chunk(far, 0, low), self.first.at[pl.ds(0, low)], self.nxt)
        self.far_high = self.send(self.chunk(far, low, high), self.first.at[pl.ds(low, high)], self.prv)
        self.up_high = self.send(self.chunk(up, low, high), self.from_prv.at[pl.ds(low, high)], self.nxt)
        self.down_low = self.send(self.chunk(down, 0, low), self.from_nxt.at[pl.ds(0, low)], self.prv)

    def middle(self):
        low, high = self.split, self.rows - self.split
        up, down = ((self.pos + k) % 4 for k in (1, 3))
        part = self.chunk(up, 0, low)
        self.far_low.wait_recv()
        part[...] += self.first[pl.ds(0, low)]
        self.up_low = self.send(part, self.from_prv.at[pl.ds(0, low)], self.nxt)
        part = self.chunk(down, low, high)
        self.far_high.wait_recv()
        part[...] += self.first[pl.ds(low, high)]
        self.down_high = self.send(part, self.from_nxt.at[pl.ds(low, high)], self.prv)

    def end(self):
        for copy in (self.up_high, self.down_low, self.up_low, self.down_high):
            copy.wait_recv()
        return self.chunk(self.pos, 0, self.rows)[...] + self.from_prv[...] + self.from_nxt[...]


def kernel(
    feat, cot, taps, resp_out, back_out, grad_out,
    field, cot_plane, cot_row, cim,
    back, back_in, back_sum, back_first, back_prv, back_nxt,
    z, core_sum, row_sum, core_in, row_in, row_far_in,
    grad, grad_first, grad_prv, grad_nxt, part, part_in, whole,
    send_sem, recv_sem,
):
    gz = lax.axis_index("gz")
    gy = lax.axis_index("gy")
    af = lax.axis_index("af")
    py, px = gz // 4, gz % 4
    zh, core = af // 2, af % 2

    sibling = (gz, gy, zh * 2 + (1 - core))
    z_next = (gz, gy, ((zh + 1) % 4) * 2 + core)
    z_prev = (gz, gy, ((zh + 3) % 4) * 2 + core)
    d_next, d_prev = (gz + 1) % 16, (gz + 15) % 16
    side = 1 - gy

    def along_x(k, row=gy):
        return (py * 4 + (px + k) % 4, row, af)

    def along_y(k, row=gy):
        return (((py + k) % 4) * 4 + px, row, af)

    started = []

    def send(src, dst, device):
        index = len(started)
        copy = pltpu.make_async_remote_copy(
            src_ref=src, dst_ref=dst, send_sem=send_sem.at[index], recv_sem=recv_sem.at[index],
            device_id=device, device_id_type=MESH,
        )
        copy.start()
        started.append(copy)
        return copy

    partners = [sibling, z_next, z_prev, (d_next, gy, af), (d_prev, gy, af)]
    partners += [(d_next, side, af), (d_prev, side, af), (gz, side, af)]
    for k in (1, 2, 3):
        for along in (along_x, along_y):
            partners += [along(k), along(k, side)]
    barrier = pltpu.get_barrier_semaphore()
    for partner in partners:
        pl.semaphore_signal(barrier, inc=1, device_id=partner, device_id_type=MESH)
    pl.semaphore_wait(barrier, len(partners))

    edge = (1 - gy) * (PLANE - 128)
    low_edge = cot.at[:, aligned(edge, 128, 128)]
    high_edge = cot.at[:, aligned(edge + PLANE, 128, 128)]
    halo = [
        send(cot.at[:, pl.ds(0, PLANE)], cot_plane.at[1], (d_prev, gy, af)),
        send(cot.at[:, pl.ds(PLANE, PLANE)], cot_plane.at[0], (d_next, gy, af)),
        send(low_edge, cot_row.at[1], (gz, side, af)),
        send(high_edge, cot_row.at[2], (gz, side, af)),
        send(low_edge, cot_row.at[3], (d_prev, side, af)),
        send(high_edge, cot_row.at[0], (d_next, side, af)),
    ]

    def block(channels_of, start, count):
        return field.at[aligned(channels_of * OWN + start, count, 16)]

    to_sibling = [send(feat, block(af, 0, OWN), sibling)]
    up_low = send(feat.at[pl.ds(0, 16)], block(af, 0, 16), z_next)
    down_high = send(feat.at[pl.ds(16, 16)], block(af, 16, 16), z_prev)
    up_high = send(feat.at[pl.ds(16, 16)], block(af, 16, 16), z_next)
    down_low = send(feat.at[pl.ds(0, 16)], block(af, 0, 16), z_prev)
    block(af, 0, OWN)[...] = feat[...]

    for copy in halo:
        copy.wait_recv()
    lane = lax.broadcasted_iota(jnp.int32, (OWN, PLANE + 128), 1)
    column = lane % WIDTH
    slab_lane = lax.broadcasted_iota(jnp.int32, (OWN, 128), 1)
    row_side = (slab_lane < WIDTH) == (gy == 0)
    inside = (gz > 0, None, None, gz < 15)
    for e in range(4):
        if e in (1, 2):
            plane = cot[:, pl.ds((e - 1) * PLANE, PLANE)].astype(F32)
        else:
            plane = cot_plane[e // 3].astype(F32)
        rows = jnp.where(row_side, cot_row[e].astype(F32), 0.0)
        base = jnp.concatenate([plane, rows], axis=1)
        if inside[e] is not None:
            base = jnp.where(inside[e], base, 0.0)
        for c in (-1, 0, 1):
            if c == 0:
                moved = base
            else:
                moved = jnp.where(column == (0 if c == 1 else WIDTH - 1), 0.0, roll(base, c))
            tall = roll(moved, WIDTH).astype(BF16)
            moved = moved.astype(BF16)
            for a in (-1, 0, 1):
                d = e - 1 + a
                if d not in (0, 1):
                    continue
                for b in (-1, 0, 1):
                    piece = {-1: tall[:, 128:], 0: moved[:, :PLANE], 1: tall[:, :PLANE]}[b]
                    cim[pl.ds(tap_index(a, b, c) * OWN, OWN), pl.ds(d * PLANE, PLANE)] = piece

    below, above = ((zh + 3) % 4) * 2 + core, ((zh + 1) % 4) * 2 + core
    up_low.wait_recv()
    far_low = send(block(below, 0, 16), block(below, 0, 16), z_next)
    down_high.wait_recv()
    far_high = send(block(above, 16, 16), block(above, 16, 16), z_prev)
    up_high.wait_recv()
    to_sibling.append(send(block(below, 0, OWN), block(below, 0, OWN), sibling))
    down_low.wait_recv()
    to_sibling.append(send(block(above, 0, OWN), block(above, 0, OWN), sibling))

    @pl.loop(0, 4)
    def _(n):
        cols = aligned(n * 256, 256, 256)
        back[:, cols] = lax.dot_general(
            taps[...], cim[:, cols], (((0,), (0,)), ((), ())), preferred_element_type=F32
        )

    back_copies = [
        send(back.at[aligned((2 * k + 1 - core) * OWN, OWN, OWN)], back_in.at[k], sibling)
        for k in range(4)
    ]
    far_low.wait_recv()
    far_high.wait_recv()
    far = ((zh + 2) % 4) * 2 + core
    to_sibling.append(send(block(far, 0, OWN), block(far, 0, OWN), sibling))
    for copy in to_sibling:
        copy.wait_recv()

    @pl.loop(0, 3)
    def _(n):
        rows = aligned(n * 288, 288, 288)
        product = lax.dot_general(
            cim[rows], field[...], (((1,), (1,)), ((), ())), preferred_element_type=F32
        )
        grad[0, rows] = product[:, :128]
        grad[1, rows] = product[:, 128:]

    rings = []
    for half, (pos, along) in enumerate(((px, along_x), (py, along_y))):
        def chunk(i, start, count, half=half):
            return grad.at[half, aligned(i * CHUNK + start, count, 8)]

        ring = Ring(
            send, chunk, CHUNK, SPLIT, pos, along(1), along(3),
            grad_first.at[half], grad_prv.at[half], grad_nxt.at[half],
        )
        ring.start()
        rings.append(ring)

    for k in range(4):
        back_copies[k].wait_recv()
        back_sum[k] = back[aligned((2 * k + core) * OWN, OWN, OWN)] + back_in[k]

    back_ring = Ring(
        send, lambda i, start, count: back_sum.at[i, pl.ds(start, count)], OWN, 16, zh, z_next, z_prev,
        back_first, back_prv, back_nxt,
    )
    back_ring.start()

    @pl.loop(0, 4)
    def _(n):
        cols = aligned(n * 256, 256, 256)
        z[:, cols] = jnp.dot(taps[...], field[:, cols], preferred_element_type=F32)

    for ring in rings:
        ring.middle()

    plane_lane = lane[:, :PLANE]
    plane_column = column[:, :PLANE]
    for e in range(4):
        rows_of = []
        for b in (-1, 0, 1):
            total = None
            for c in (-1, 0, 1):
                term = None
                for a in (-1, 0, 1):
                    d = e - 1 + a
                    if d in (0, 1):
                        value = z[pl.ds(tap_index(a, b, c) * OWN, OWN), pl.ds(d * PLANE, PLANE)]
                        term = value if term is None else term + value
                if c:
                    out = WIDTH - 1 if c == 1 else 0
                    term = jnp.where(plane_column == out, 0.0, roll(term, -c))
                total = term if total is None else total + term
            rows_of.append(roll(total, -b * WIDTH) if b else total)
        before, centre, after = rows_of
        core_sum[e] = (
            centre
            + jnp.where(plane_lane < PLANE - WIDTH, after, 0.0)
            + jnp.where(plane_lane >= WIDTH, before, 0.0)
        )
        outward = jnp.where(gy == 0, before[:, :128], after[:, PLANE - 128:])
        row_sum[e] = jnp.where(row_side, outward, 0.0)

    resp_copies = [
        send(core_sum.at[0], core_in.at[1], (d_prev, gy, af)),
        send(core_sum.at[3], core_in.at[0], (d_next, gy, af)),
        send(row_sum.at[1], row_in.at[0], (gz, side, af)),
        send(row_sum.at[2], row_in.at[1], (gz, side, af)),
        send(row_sum.at[0], row_far_in.at[1], (d_prev, side, af)),
        send(row_sum.at[3], row_far_in.at[0], (d_next, side, af)),
    ]
    back_ring.middle()

    groups = []
    for half, (pos, along) in enumerate(((py, along_y), (px, along_x))):
        part[half, pl.ds(0, CHUNK)] = rings[half].end()
        part[half, pl.ds(CHUNK, 256 - CHUNK)] = jnp.zeros((256 - CHUNK, 128), F32)
        mine = pos * 2 + gy
        others = []
        for step in range(1, 8):
            k, other = step // 2, gy if step % 2 == 0 else side
            there = ((pos + k) % 4) * 2 + other
            others.append((along(k, other), there))
        groups.append((mine, others))

    part_copies = []
    for half, (mine, others) in enumerate(groups):
        part_copies.append([
            send(part.at[half, aligned(there * 32, 32, 32)], part_in.at[half, n], device)
            for n, (device, there) in enumerate(others)
        ])
    scale = 1.0 / math.sqrt(32768.0)
    whole_copies = []
    for half, (mine, others) in enumerate(groups):
        rows = aligned(mine * 32, 32, 32)
        total = part[half, rows]
        for n, copy in enumerate(part_copies[half]):
            copy.wait_recv()
            total = total + part_in[half, n]
        whole[half, rows] = total * scale
        for device, _ in others:
            whole_copies.append(send(whole.at[half, rows], whole.at[half, rows], device))

    for copy in resp_copies:
        copy.wait_recv()
    for d, valid in ((0, gz > 0), (1, gz < 15)):
        total = core_sum[d + 1] + jnp.where(valid, core_in[d], 0.0)
        slab = row_in[d] + jnp.where(valid, row_far_in[d], 0.0)
        slab = jnp.concatenate(
            [
                jnp.where(gy == 1, slab, 0.0),
                jnp.zeros((OWN, PLANE - 256), F32),
                jnp.where(gy == 0, slab, 0.0),
            ],
            axis=1,
        )
        resp_out[:, pl.ds(d * PLANE, PLANE)] = (total + slab).astype(BF16)

    for copy in whole_copies:
        copy.wait_recv()
    final = []
    for half, (pos, along) in enumerate(((px, along_x), (py, along_y))):
        def place(i, start, count, half=half):
            return grad_out.at[aligned(i * CHUNK + start, count, 8), pl.ds(half * 128, 128)]

        low, high = (0, SPLIT), (SPLIT, CHUNK - SPLIT)
        nxt, prv = along(1), along(3)
        copies = []
        for device, (start, count) in ((nxt, low), (prv, high), (nxt, high), (prv, low)):
            copies.append(send(whole.at[half, pl.ds(start, count)], place(pos, start, count), device))
        place(pos, 0, CHUNK)[...] = whole[half, pl.ds(0, CHUNK)]
        final.append((copies, place, pos, nxt, prv, low, high))

    back_out[...] = back_ring.end().astype(BF16)

    last = []
    for copies, place, pos, nxt, prv, low, high in final:
        down, up = (pos + 3) % 4, (pos + 1) % 4
        copies[0].wait_recv()
        last.append(send(place(down, *low), place(down, *low), nxt))
        copies[1].wait_recv()
        last.append(send(place(up, *high), place(up, *high), prv))
        copies[2].wait_recv()
        copies[3].wait_recv()
    for copy in last:
        copy.wait_recv()
    for copy in started:
        copy.wait_send()


def shards(features, filters, cotangent):
    vmem = pl.BlockSpec(memory_space=pltpu.VMEM)
    resp, back, grad = pl.pallas_call(
        kernel,
        out_shape=(
            jax.ShapeDtypeStruct((OWN, CELLS), BF16),
            jax.ShapeDtypeStruct((OWN, CELLS), BF16),
            jax.ShapeDtypeStruct((ROWS, C), F32),
        ),
        in_specs=[vmem] * 3,
        out_specs=(vmem,) * 3,
        scratch_shapes=[
            pltpu.VMEM((C, CELLS), BF16),
            pltpu.VMEM((2, OWN, PLANE), BF16),
            pltpu.VMEM((4, OWN, 128), BF16),
            pltpu.VMEM((ROWS, CELLS), BF16),
            pltpu.VMEM((C, CELLS), F32),
            pltpu.VMEM((4, OWN, CELLS), F32),
            pltpu.VMEM((4, OWN, CELLS), F32),
            pltpu.VMEM((OWN, CELLS), F32),
            pltpu.VMEM((OWN, CELLS), F32),
            pltpu.VMEM((OWN, CELLS), F32),
            pltpu.VMEM((ROWS, CELLS), F32),
            pltpu.VMEM((4, OWN, PLANE), F32),
            pltpu.VMEM((4, OWN, 128), F32),
            pltpu.VMEM((2, OWN, PLANE), F32),
            pltpu.VMEM((2, OWN, 128), F32),
            pltpu.VMEM((2, OWN, 128), F32),
            pltpu.VMEM((2, ROWS, 128), F32),
            pltpu.VMEM((2, CHUNK, 128), F32),
            pltpu.VMEM((2, CHUNK, 128), F32),
            pltpu.VMEM((2, CHUNK, 128), F32),
            pltpu.VMEM((2, 256, 128), F32),
            pltpu.VMEM((2, 7, 32, 128), F32),
            pltpu.VMEM((2, 256, 128), F32),
            pltpu.SemaphoreType.DMA((N_COPIES,)),
            pltpu.SemaphoreType.DMA((N_COPIES,)),
        ],
        compiler_params=pltpu.CompilerParams(
            collective_id=0, has_side_effects=True, vmem_limit_bytes=40 * 1024 * 1024
        ),
    )(
        features.reshape(OWN, CELLS),
        cotangent.reshape(OWN, CELLS),
        filters.reshape(ROWS, C),
    )
    return (
        resp.reshape(features.shape),
        back.reshape(cotangent.shape),
        grad.reshape(filters.shape),
    )


def solution(mesh):
    placed = (P("af", "gz", "gy"), P(None, None, None, "af", None), P("af", "gz", "gy"))
    return jax.shard_map(
        shards,
        mesh=mesh,
        in_specs=placed,
        out_specs=(P("af", "gz", "gy"), P("af", "gz", "gy"), P(None, None, None, "af", None)),
        check_vma=False,
    )
```

```python
import math

import jax
import jax.numpy as jnp
from jax import lax
from jax.experimental import pallas as pl
from jax.experimental.pallas import tpu as pltpu
from jax.sharding import PartitionSpec as P

MESH = pl.DeviceIdType.MESH
F32 = jnp.float32
BF16 = jnp.bfloat16
WIDTH = 64
PLANE = 512
CELLS = 1024
OWN = 32
C = 256
TAPS = 27
ROWS = TAPS * OWN
PADDED = 896
CHUNK = PADDED // 8
N_GROUPS = 32


def tap_index(a, b, c):
    return ((a + 1) * 3 + (b + 1)) * 3 + (c + 1)


def roll(x, shift):
    return pltpu.roll(x, shift % x.shape[1], 1)


def aligned(start, size, unit):
    return pl.ds(pl.multiple_of(start, unit), size)


class Ring:
    def __init__(self, group, chunk, rows, split, pos, nxt, prv, first, both):
        self.group, self.chunk, self.rows, self.split = group, chunk, rows, split
        self.pos, self.nxt, self.prv = pos, nxt, prv
        self.first, self.both = first, both

    def start(self):
        low, high = self.split, self.rows - self.split
        far, up, down = ((self.pos + k) % 4 for k in (2, 1, 3))
        self.early = self.group(self.first)
        self.early.send(self.chunk(far, 0, low), self.first.at[pl.ds(0, low)], self.nxt)
        self.early.send(self.chunk(far, low, high), self.first.at[pl.ds(low, high)], self.prv)
        self.late = self.group(self.both)
        self.late.send(self.chunk(up, low, high), self.both.at[0, pl.ds(low, high)], self.nxt)
        self.late.send(self.chunk(down, 0, low), self.both.at[1, pl.ds(0, low)], self.prv)

    def middle(self):
        low, high = self.split, self.rows - self.split
        up, down = ((self.pos + k) % 4 for k in (1, 3))
        self.early.wait_recv()
        part = self.chunk(up, 0, low)
        part[...] += self.first[pl.ds(0, low)]
        self.late.send(part, self.both.at[0, pl.ds(0, low)], self.nxt)
        part = self.chunk(down, low, high)
        part[...] += self.first[pl.ds(low, high)]
        self.late.send(part, self.both.at[1, pl.ds(low, high)], self.prv)

    def end(self):
        self.late.wait_recv()
        return self.chunk(self.pos, 0, self.rows)[...] + self.both[0] + self.both[1]


def kernel(
    feat, cot, taps, resp_out, back_out, grad_out,
    field, cot_halo, cim,
    back, back_in, back_sum, back_first, back_both,
    z, core_sum, row_sum, resp_in,
    grad, grad_in, part, part_in, whole,
    send_sem, recv_sem,
):
    gz = lax.axis_index("gz")
    gy = lax.axis_index("gy")
    af = lax.axis_index("af")
    py, px = gz // 4, gz % 4
    zh, core = af // 2, af % 2

    sibling = (gz, gy, zh * 2 + (1 - core))
    d_next, d_prev = (gz + 1) % 16, (gz + 15) % 16
    side = 1 - gy

    def along_x(k, row=gy):
        return (py * 4 + (px + k) % 4, row, af)

    def along_y(k, row=gy):
        return (((py + k) % 4) * 4 + px, row, af)

    def along_z(k):
        return (gz, gy, ((zh + k) % 4) * 2 + core)

    groups = []

    class Group:
        def __init__(self, size):
            self.index, self.size = len(groups), size
            groups.append(self)

        def send(self, src, dst, device):
            pltpu.make_async_remote_copy(
                src_ref=src, dst_ref=dst,
                send_sem=send_sem.at[self.index], recv_sem=recv_sem.at[self.index],
                device_id=device, device_id_type=MESH,
            ).start()
            return self

        def wait_recv(self):
            pltpu.make_async_copy(self.size, self.size, recv_sem.at[self.index]).wait()

        def wait_send(self):
            pltpu.make_async_copy(self.size, self.size, send_sem.at[self.index]).wait()

    partners = [sibling, (d_next, gy, af), (d_prev, gy, af)]
    partners += [(d_next, side, af), (d_prev, side, af), (gz, side, af)]
    for k in (1, 2, 3):
        partners.append(along_z(k))
        for along in (along_x, along_y):
            partners += [along(k), along(k, side)]
    barrier = pltpu.get_barrier_semaphore()
    for partner in partners:
        pl.semaphore_signal(barrier, inc=1, device_id=partner, device_id_type=MESH)
    pl.semaphore_wait(barrier, len(partners))

    def block(channels_of):
        return field.at[aligned(channels_of * OWN, OWN, OWN)]

    def relay(k):
        rows = block(((zh + k) % 4) * 2 + core)
        return Group(rows).send(rows, rows, sibling)

    pair = 1 + 2 * (zh % 2)
    from_pair = Group(block(af)).send(feat, block(af), along_z(pair))
    from_sibling = Group(block(af)).send(feat, block(af), sibling)

    edge = (1 - gy) * (PLANE - 128)
    low_edge = cot.at[:, aligned(edge, 128, 128)]
    high_edge = cot.at[:, aligned(edge + PLANE, 128, 128)]

    def halo(n):
        return cot_halo.at[:, pl.ds(2 * PLANE + n * 128, 128)]

    halos = Group(cot_halo)
    halos.send(low_edge, halo(3), (d_prev, side, af))
    halos.send(high_edge, halo(0), (d_next, side, af))
    halos.send(cot.at[:, pl.ds(0, PLANE)], cot_halo.at[:, pl.ds(PLANE, PLANE)], (d_prev, gy, af))
    halos.send(cot.at[:, pl.ds(PLANE, PLANE)], cot_halo.at[:, pl.ds(0, PLANE)], (d_next, gy, af))
    halos.send(low_edge, halo(1), (gz, side, af))
    halos.send(high_edge, halo(2), (gz, side, af))
    from_far = Group(block(af)).send(feat, block(af), along_z(2))
    from_other = Group(block(af)).send(feat, block(af), along_z(4 - pair))
    block(af)[...] = feat[...]

    from_pair.wait_recv()
    pair_relay = relay(pair)

    halos.wait_recv()
    lane = lax.broadcasted_iota(jnp.int32, (OWN, PLANE + 128), 1)
    column = lane % WIDTH
    slab_lane = lax.broadcasted_iota(jnp.int32, (OWN, 128), 1)
    row_side = (slab_lane < WIDTH) == (gy == 0)
    inside = (gz > 0, None, None, gz < 15)
    for e in range(4):
        if e in (1, 2):
            plane = cot[:, pl.ds((e - 1) * PLANE, PLANE)].astype(F32)
        else:
            plane = cot_halo[:, pl.ds((e // 3) * PLANE, PLANE)].astype(F32)
        rows = jnp.where(row_side, halo(e)[...].astype(F32), 0.0)
        base = jnp.concatenate([plane, rows], axis=1)
        if inside[e] is not None:
            base = jnp.where(inside[e], base, 0.0)
        for c in (-1, 0, 1):
            if c == 0:
                moved = base
            else:
                moved = jnp.where(column == (0 if c == 1 else WIDTH - 1), 0.0, roll(base, c))
            tall = roll(moved, WIDTH).astype(BF16)
            moved = moved.astype(BF16)
            for a in (-1, 0, 1):
                d = e - 1 + a
                if d not in (0, 1):
                    continue
                for b in (-1, 0, 1):
                    piece = {-1: tall[:, 128:], 0: moved[:, :PLANE], 1: tall[:, :PLANE]}[b]
                    cim[pl.ds(tap_index(a, b, c) * OWN, OWN), pl.ds(d * PLANE, PLANE)] = piece

    near_lanes = (zh // 2) * 128

    def channels(half):
        return near_lanes if half == 0 else 128 - near_lanes

    def filter_products(half):
        @pl.loop(0, 3)
        def _(n):
            rows = aligned(n * 288, 288, 288)
            grad[half, rows] = lax.dot_general(
                cim[rows], field[aligned(channels(half), 128, 128)],
                (((1,), (1,)), ((), ())), preferred_element_type=F32,
            )
        grad[half, pl.ds(ROWS, PADDED - ROWS)] = jnp.zeros((PADDED - ROWS, 128), F32)

    orders = ((px, along_x, py, along_y), (py, along_y, px, along_x))

    def unit_rows(r, i):
        return aligned(r * 4 * CHUNK + i * CHUNK, CHUNK, 16)

    def scatter(half):
        for r, (pos, along, _, _) in enumerate(orders):
            u = half * 2 + r
            sent = Group(grad_in.at[u])
            for k in (2, 1, 3):
                sent.send(grad.at[half, unit_rows(r, (pos + k) % 4)], grad_in.at[u, k - 1], along(k))
            scattered[u] = sent

    def eight(pos, along):
        others = []
        for step in (5, 4, 3, 2, 7, 6, 1):
            k, row = step // 2, gy if step % 2 == 0 else side
            others.append((step - 1, along(k, row), ((pos + k) % 4) * 2 + row))
        return pos * 2 + gy, others

    def scatter_again(half):
        for r, (pos, _, pos2, along2) in enumerate(orders):
            u = half * 2 + r
            scattered[u].wait_recv()
            part[u, pl.ds(0, CHUNK)] = (
                grad[half, unit_rows(r, pos)] + grad_in[u, 0] + grad_in[u, 1] + grad_in[u, 2]
            )
            part[u, pl.ds(CHUNK, 16)] = jnp.zeros((16, 128), F32)
            sent = Group(part_in.at[u])
            for n, device, there in eight(pos2, along2)[1]:
                sent.send(part.at[u, aligned(there * 16, 16, 16)], part_in.at[u, n], device)
            scattered_again[u] = sent

    def gather(half):
        for r, (_, _, pos2, along2) in enumerate(orders):
            u = half * 2 + r
            mine, others = eight(pos2, along2)
            rows = aligned(mine * 16, 16, 16)
            scattered_again[u].wait_recv()
            total = part[u, rows]
            for n in range(7):
                total = total + part_in[u, n]
            whole[u, rows] = total * (1.0 / math.sqrt(32768.0))
            sent = Group(part_in.at[u])
            for _, device, _ in others:
                sent.send(whole.at[u, rows], whole.at[u, rows], device)
            gathered[u] = sent

    def gather_again(half):
        lanes = aligned(channels(half), 128, 128)
        for r, (pos, along, _, _) in enumerate(orders):
            u = half * 2 + r
            gathered[u].wait_recv()
            sent = Group(grad_in.at[u])
            place = grad_out.at[unit_rows(r, pos), lanes]
            for k in (2, 1, 3):
                sent.send(whole.at[u, pl.ds(0, CHUNK)], place, along(k))
            place[...] = whole[u, pl.ds(0, CHUNK)]
            gathered_again[u] = sent

    scattered, scattered_again, gathered, gathered_again = {}, {}, {}, {}

    from_sibling.wait_recv()
    pair_relay.wait_recv()
    filter_products(0)
    scatter(0)
    from_other.wait_recv()
    other_relay = relay(4 - pair)

    @pl.loop(0, 4)
    def _(n):
        cols = aligned(n * 256, 256, 256)
        back[:, cols] = lax.dot_general(
            taps[...], cim[:, cols], (((0,), (0,)), ((), ())), preferred_element_type=F32
        )

    from_far.wait_recv()
    far_relay = relay(2)
    to_sibling = Group(back_in)
    for k in range(4):
        to_sibling.send(back.at[aligned((2 * k + 1 - core) * OWN, OWN, OWN)], back_in.at[k], sibling)
    other_relay.wait_recv()
    far_relay.wait_recv()
    filter_products(1)
    scatter(1)

    to_sibling.wait_recv()
    for k in range(4):
        back_sum[k] = back[aligned((2 * k + core) * OWN, OWN, OWN)] + back_in[k]

    ring = Ring(
        Group, lambda i, start, count: back_sum.at[i, pl.ds(start, count)], OWN, 16,
        zh, along_z(1), along_z(3), back_first, back_both,
    )
    ring.start()

    @pl.loop(0, 4)
    def _(n):
        cols = aligned(n * 256, 256, 256)
        z[:, cols] = jnp.dot(taps[...], field[:, cols], preferred_element_type=F32)

    scatter_again(0)

    plane_lane = lane[:, :PLANE]
    plane_column = column[:, :PLANE]
    for e in range(4):
        rows_of = []
        for b in (-1, 0, 1):
            total = None
            for c in (-1, 0, 1):
                term = None
                for a in (-1, 0, 1):
                    d = e - 1 + a
                    if d in (0, 1):
                        value = z[pl.ds(tap_index(a, b, c) * OWN, OWN), pl.ds(d * PLANE, PLANE)]
                        term = value if term is None else term + value
                if c:
                    out = WIDTH - 1 if c == 1 else 0
                    term = jnp.where(plane_column == out, 0.0, roll(term, -c))
                total = term if total is None else total + term
            rows_of.append(roll(total, -b * WIDTH) if b else total)
        before, centre, after = rows_of
        core_sum[e] = (
            centre
            + jnp.where(plane_lane < PLANE - WIDTH, after, 0.0)
            + jnp.where(plane_lane >= WIDTH, before, 0.0)
        )
        outward = jnp.where(gy == 0, before[:, :128], after[:, PLANE - 128:])
        row_sum[e] = jnp.where(row_side, outward, 0.0)

    def resp_row(n):
        return resp_in.at[:, pl.ds(2 * PLANE + n * 128, 128)]

    outer = Group(resp_in)
    outer.send(core_sum.at[0], resp_in.at[:, pl.ds(PLANE, PLANE)], (d_prev, gy, af))
    outer.send(core_sum.at[3], resp_in.at[:, pl.ds(0, PLANE)], (d_next, gy, af))
    outer.send(row_sum.at[1], resp_row(0), (gz, side, af))
    outer.send(row_sum.at[2], resp_row(1), (gz, side, af))
    outer.send(row_sum.at[0], resp_row(3), (d_prev, side, af))
    outer.send(row_sum.at[3], resp_row(2), (d_next, side, af))

    scatter_again(1)
    ring.middle()
    gather(0)

    outer.wait_recv()
    for d, valid in ((0, gz > 0), (1, gz < 15)):
        total = core_sum[d + 1] + jnp.where(valid, resp_in[:, pl.ds(d * PLANE, PLANE)], 0.0)
        slab = resp_row(d)[...] + jnp.where(valid, resp_row(2 + d)[...], 0.0)
        slab = jnp.concatenate(
            [
                jnp.where(gy == 1, slab, 0.0),
                jnp.zeros((OWN, PLANE - 256), F32),
                jnp.where(gy == 0, slab, 0.0),
            ],
            axis=1,
        )
        resp_out[:, pl.ds(d * PLANE, PLANE)] = (total + slab).astype(BF16)

    gather(1)
    gather_again(0)
    gather_again(1)
    back_out[...] = ring.end().astype(BF16)
    for u in range(4):
        gathered_again[u].wait_recv()
    for group in groups:
        group.wait_send()


def shards(features, filters, cotangent):
    vmem = pl.BlockSpec(memory_space=pltpu.VMEM)
    resp, back, grad = pl.pallas_call(
        kernel,
        out_shape=(
            jax.ShapeDtypeStruct((OWN, CELLS), BF16),
            jax.ShapeDtypeStruct((OWN, CELLS), BF16),
            jax.ShapeDtypeStruct((PADDED, C), F32),
        ),
        in_specs=[vmem] * 3,
        out_specs=(vmem,) * 3,
        scratch_shapes=[
            pltpu.VMEM((C, CELLS), BF16),
            pltpu.VMEM((OWN, 2 * PLANE + 4 * 128), BF16),
            pltpu.VMEM((ROWS, CELLS), BF16),
            pltpu.VMEM((C, CELLS), F32),
            pltpu.VMEM((4, OWN, CELLS), F32),
            pltpu.VMEM((4, OWN, CELLS), F32),
            pltpu.VMEM((OWN, CELLS), F32),
            pltpu.VMEM((2, OWN, CELLS), F32),
            pltpu.VMEM((ROWS, CELLS), F32),
            pltpu.VMEM((4, OWN, PLANE), F32),
            pltpu.VMEM((4, OWN, 128), F32),
            pltpu.VMEM((OWN, 2 * PLANE + 4 * 128), F32),
            pltpu.VMEM((2, PADDED, 128), F32),
            pltpu.VMEM((4, 3, CHUNK, 128), F32),
            pltpu.VMEM((4, CHUNK + 16, 128), F32),
            pltpu.VMEM((4, 7, 16, 128), F32),
            pltpu.VMEM((4, CHUNK + 16, 128), F32),
            pltpu.SemaphoreType.DMA((N_GROUPS,)),
            pltpu.SemaphoreType.DMA((N_GROUPS,)),
        ],
        compiler_params=pltpu.CompilerParams(
            collective_id=0, has_side_effects=True, vmem_limit_bytes=40 * 1024 * 1024
        ),
    )(
        features.reshape(OWN, CELLS),
        cotangent.reshape(OWN, CELLS),
        filters.reshape(ROWS, C),
    )
    return (
        resp.reshape(features.shape),
        back.reshape(cotangent.shape),
        grad[:ROWS].reshape(filters.shape),
    )


def solution(mesh):
    placed = (P("af", "gz", "gy"), P(None, None, None, "af", None), P("af", "gz", "gy"))
    return jax.shard_map(
        shards,
        mesh=mesh,
        in_specs=placed,
        out_specs=(P("af", "gz", "gy"), P("af", "gz", "gy"), P(None, None, None, "af", None)),
        check_vma=False,
    )
```

```python
import math

import jax
import jax.numpy as jnp
from jax import lax
from jax.experimental import pallas as pl
from jax.experimental.pallas import tpu as pltpu
from jax.sharding import PartitionSpec as P

MESH = pl.DeviceIdType.MESH
F32 = jnp.float32
BF16 = jnp.bfloat16
WIDTH = 64
PLANE = 512
CELLS = 1024
OWN = 32
C = 256
TAPS = 27
ROWS = TAPS * OWN
PADDED = 896
CHUNK = PADDED // 8
N_GROUPS = 32


def tap_index(a, b, c):
    return ((a + 1) * 3 + (b + 1)) * 3 + (c + 1)


def roll(x, shift):
    return pltpu.roll(x, shift % x.shape[1], 1)


def aligned(start, size, unit):
    return pl.ds(pl.multiple_of(start, unit), size)


class Ring:
    def __init__(self, group, chunk, rows, split, pos, nxt, prv, first, both):
        self.group, self.chunk, self.rows, self.split = group, chunk, rows, split
        self.pos, self.nxt, self.prv = pos, nxt, prv
        self.first, self.both = first, both

    def start(self):
        low, high = self.split, self.rows - self.split
        far, up, down = ((self.pos + k) % 4 for k in (2, 1, 3))
        self.early = self.group(self.first)
        self.early.send(self.chunk(far, 0, low), self.first.at[pl.ds(0, low)], self.nxt)
        self.early.send(self.chunk(far, low, high), self.first.at[pl.ds(low, high)], self.prv)
        self.late = self.group(self.both)
        self.late.send(self.chunk(up, low, high), self.both.at[0, pl.ds(low, high)], self.nxt)
        self.late.send(self.chunk(down, 0, low), self.both.at[1, pl.ds(0, low)], self.prv)

    def middle(self):
        low, high = self.split, self.rows - self.split
        up, down = ((self.pos + k) % 4 for k in (1, 3))
        self.early.wait_recv()
        part = self.chunk(up, 0, low)
        part[...] += self.first[pl.ds(0, low)]
        self.late.send(part, self.both.at[0, pl.ds(0, low)], self.nxt)
        part = self.chunk(down, low, high)
        part[...] += self.first[pl.ds(low, high)]
        self.late.send(part, self.both.at[1, pl.ds(low, high)], self.prv)

    def end(self):
        self.late.wait_recv()
        return self.chunk(self.pos, 0, self.rows)[...] + self.both[0] + self.both[1]


def kernel(
    feat_hbm, cot_hbm, taps_hbm, resp_out, back_out, grad_out,
    feat_raw, cot_raw, taps, taps_t, feat, cot, field, cot_halo, cim,
    back, back_in, back_sum, back_first, back_both,
    z, core_sum, row_sum, resp_in,
    grad, grad_in, part, part_in, whole,
    load_sem, send_sem, recv_sem,
):
    loads = [
        pltpu.make_async_copy(src, dst, load_sem.at[n])
        for n, (src, dst) in enumerate(((feat_hbm, feat_raw), (cot_hbm, cot_raw), (taps_hbm, taps)))
    ]
    for load in loads:
        load.start()
    gz = lax.axis_index("gz")
    gy = lax.axis_index("gy")
    af = lax.axis_index("af")
    py, px = gz // 4, gz % 4
    zh, core = af // 2, af % 2

    sibling = (gz, gy, zh * 2 + (1 - core))
    d_next, d_prev = (gz + 1) % 16, (gz + 15) % 16
    side = 1 - gy

    def along_x(k, row=gy):
        return (py * 4 + (px + k) % 4, row, af)

    def along_y(k, row=gy):
        return (((py + k) % 4) * 4 + px, row, af)

    def along_z(k):
        return (gz, gy, ((zh + k) % 4) * 2 + core)

    groups = []

    class Group:
        def __init__(self, size):
            self.index, self.size = len(groups), size
            groups.append(self)

        def send(self, src, dst, device):
            pltpu.make_async_remote_copy(
                src_ref=src, dst_ref=dst,
                send_sem=send_sem.at[self.index], recv_sem=recv_sem.at[self.index],
                device_id=device, device_id_type=MESH,
            ).start()
            return self

        def wait_recv(self):
            pltpu.make_async_copy(self.size, self.size, recv_sem.at[self.index]).wait()

        def wait_send(self):
            pltpu.make_async_copy(self.size, self.size, send_sem.at[self.index]).wait()

    partners = [sibling, (d_next, gy, af), (d_prev, gy, af)]
    partners += [(d_next, side, af), (d_prev, side, af), (gz, side, af)]
    partners += [along_z(1), along_z(3)]
    for k in (1, 2, 3):
        for along in (along_x, along_y):
            partners += [along(k), along(k, side)]
    barrier = pltpu.get_barrier_semaphore()
    for partner in partners:
        pl.semaphore_signal(barrier, inc=1, device_id=partner, device_id_type=MESH)
    for load, raw, flat in zip(loads, (feat_raw, cot_raw), (feat, cot)):
        load.wait()
        for d in (0, 1):
            flat[:, pl.ds(d * PLANE, PLANE)] = raw[:, d, :]
    loads[2].wait()
    taps_t[...] = taps[...].T
    pl.semaphore_wait(barrier, len(partners))

    def block(channels_of):
        return field.at[aligned(channels_of * OWN, OWN, OWN)]

    pair = 1 + 2 * (zh % 2)
    other = 4 - pair
    far = 2

    def owner(k):
        return ((zh + k) % 4) * 2 + core

    def pass_on(rows, device):
        return Group(rows).send(rows, rows, device)

    def half_block(k, start):
        return field.at[aligned(owner(k) * OWN + start, 16, 16)]

    from_pair = Group(block(af)).send(feat, block(af), along_z(pair))
    from_sibling = Group(block(af)).send(feat, block(af), sibling)

    edge = (1 - gy) * (PLANE - 128)
    low_edge = cot.at[:, aligned(edge, 128, 128)]
    high_edge = cot.at[:, aligned(edge + PLANE, 128, 128)]

    def halo(n):
        return cot_halo.at[:, pl.ds(2 * PLANE + n * 128, 128)]

    halos = Group(cot_halo)
    halos.send(low_edge, halo(3), (d_prev, side, af))
    halos.send(high_edge, halo(0), (d_next, side, af))
    halos.send(cot.at[:, pl.ds(0, PLANE)], cot_halo.at[:, pl.ds(PLANE, PLANE)], (d_prev, gy, af))
    halos.send(cot.at[:, pl.ds(PLANE, PLANE)], cot_halo.at[:, pl.ds(0, PLANE)], (d_next, gy, af))
    halos.send(low_edge, halo(1), (gz, side, af))
    halos.send(high_edge, halo(2), (gz, side, af))
    from_other = Group(block(af)).send(feat, block(af), along_z(other))
    block(af)[...] = feat[...]

    from_pair.wait_recv()
    far_by_other = pass_on(half_block(pair, 0), along_z(other))
    pair_relay = pass_on(block(owner(pair)), sibling)

    halos.wait_recv()
    lane = lax.broadcasted_iota(jnp.int32, (OWN, PLANE + 128), 1)
    column = lane % WIDTH
    slab_lane = lax.broadcasted_iota(jnp.int32, (OWN, 128), 1)
    row_side = (slab_lane < WIDTH) == (gy == 0)
    inside = (gz > 0, None, None, gz < 15)
    for e in range(4):
        if e in (1, 2):
            plane = cot[:, pl.ds((e - 1) * PLANE, PLANE)].astype(F32)
        else:
            plane = cot_halo[:, pl.ds((e // 3) * PLANE, PLANE)].astype(F32)
        rows = jnp.where(row_side, halo(e)[...].astype(F32), 0.0)
        base = jnp.concatenate([plane, rows], axis=1)
        if inside[e] is not None:
            base = jnp.where(inside[e], base, 0.0)
        for c in (-1, 0, 1):
            if c == 0:
                moved = base
            else:
                moved = jnp.where(column == (0 if c == 1 else WIDTH - 1), 0.0, roll(base, c))
            tall = roll(moved, WIDTH).astype(BF16)
            moved = moved.astype(BF16)
            for a in (-1, 0, 1):
                d = e - 1 + a
                if d not in (0, 1):
                    continue
                for b in (-1, 0, 1):
                    piece = {-1: tall[:, 128:], 0: moved[:, :PLANE], 1: tall[:, :PLANE]}[b]
                    cim[pl.ds(tap_index(a, b, c) * OWN, OWN), pl.ds(d * PLANE, PLANE)] = piece

    near_lanes = (zh // 2) * 128

    def channels(half):
        return near_lanes if half == 0 else 128 - near_lanes

    def filter_products(half):
        grad[half, pl.ds(0, ROWS)] = lax.dot_general(
            cim[...], field[aligned(channels(half), 128, 128)],
            (((1,), (1,)), ((), ())), preferred_element_type=F32,
        )
        grad[half, pl.ds(ROWS, PADDED - ROWS)] = jnp.zeros((PADDED - ROWS, 128), F32)

    orders = ((px, along_x, py, along_y), (py, along_y, px, along_x))

    def unit_rows(r, i):
        return aligned(r * 4 * CHUNK + i * CHUNK, CHUNK, 16)

    def scatter(half):
        for r, (pos, along, _, _) in enumerate(orders):
            u = half * 2 + r
            sent = Group(grad_in.at[u])
            for k in (2, 1, 3):
                sent.send(grad.at[half, unit_rows(r, (pos + k) % 4)], grad_in.at[u, k - 1], along(k))
            scattered[u] = sent

    def eight(pos, along):
        others = []
        for step in (5, 4, 3, 2, 7, 6, 1):
            k, row = step // 2, gy if step % 2 == 0 else side
            others.append((step - 1, along(k, row), ((pos + k) % 4) * 2 + row))
        return pos * 2 + gy, others

    def scatter_again(half):
        for r, (pos, _, pos2, along2) in enumerate(orders):
            u = half * 2 + r
            scattered[u].wait_recv()
            part[u, pl.ds(0, CHUNK)] = (
                grad[half, unit_rows(r, pos)] + grad_in[u, 0] + grad_in[u, 1] + grad_in[u, 2]
            )
            part[u, pl.ds(CHUNK, 16)] = jnp.zeros((16, 128), F32)
            sent = Group(part_in.at[u])
            for n, device, there in eight(pos2, along2)[1]:
                sent.send(part.at[u, aligned(there * 16, 16, 16)], part_in.at[u, n], device)
            scattered_again[u] = sent

    def gather(half):
        for r, (_, _, pos2, along2) in enumerate(orders):
            u = half * 2 + r
            mine, others = eight(pos2, along2)
            rows = aligned(mine * 16, 16, 16)
            scattered_again[u].wait_recv()
            total = part[u, rows]
            for n in range(7):
                total = total + part_in[u, n]
            whole[u, rows] = total * (1.0 / math.sqrt(32768.0))
            sent = Group(part_in.at[u])
            for _, device, _ in others:
                sent.send(whole.at[u, rows], whole.at[u, rows], device)
            gathered[u] = sent

    def gather_again(half):
        lanes = aligned(channels(half), 128, 128)
        for r, (pos, along, _, _) in enumerate(orders):
            u = half * 2 + r
            gathered[u].wait_recv()
            sent = Group(grad_in.at[u])
            place = grad_out.at[unit_rows(r, pos), lanes]
            for k in (2, 1, 3):
                sent.send(whole.at[u, pl.ds(0, CHUNK)], place, along(k))
            place[...] = whole[u, pl.ds(0, CHUNK)]
            gathered_again[u] = sent

    scattered, scattered_again, gathered, gathered_again = {}, {}, {}, {}

    from_other.wait_recv()
    far_by_pair = pass_on(half_block(other, 16), along_z(pair))
    other_relay = pass_on(block(owner(other)), sibling)
    from_sibling.wait_recv()
    pair_relay.wait_recv()
    filter_products(0)
    scatter(0)

    @pl.loop(0, 4)
    def _(n):
        cols = aligned(n * 256, 256, 256)
        back[:, cols] = lax.dot_general(
            taps_t[...], cim[:, cols], (((1,), (0,)), ((), ())), preferred_element_type=F32
        )

    far_by_other.wait_recv()
    far_by_pair.wait_recv()
    far_relay = pass_on(block(owner(far)), sibling)
    to_sibling = Group(back_in)
    for k in range(4):
        to_sibling.send(back.at[aligned((2 * k + 1 - core) * OWN, OWN, OWN)], back_in.at[k], sibling)
    other_relay.wait_recv()
    far_relay.wait_recv()
    filter_products(1)
    scatter(1)

    @pl.loop(0, 4)
    def _(n):
        cols = aligned(n * 256, 256, 256)
        z[:, cols] = jnp.dot(taps[...], field[:, cols], preferred_element_type=F32)

    scatter_again(0)

    to_sibling.wait_recv()
    for k in range(4):
        back_sum[k] = back[aligned((2 * k + core) * OWN, OWN, OWN)] + back_in[k]

    ring = Ring(
        Group, lambda i, start, count: back_sum.at[i, pl.ds(start, count)], OWN, 16,
        zh, along_z(1), along_z(3), back_first, back_both,
    )
    ring.start()

    plane_lane = lane[:, :PLANE]
    plane_column = column[:, :PLANE]
    for e in range(4):
        rows_of = []
        for b in (-1, 0, 1):
            total = None
            for c in (-1, 0, 1):
                term = None
                for a in (-1, 0, 1):
                    d = e - 1 + a
                    if d in (0, 1):
                        value = z[pl.ds(tap_index(a, b, c) * OWN, OWN), pl.ds(d * PLANE, PLANE)]
                        term = value if term is None else term + value
                if c:
                    out = WIDTH - 1 if c == 1 else 0
                    term = jnp.where(plane_column == out, 0.0, roll(term, -c))
                total = term if total is None else total + term
            rows_of.append(roll(total, -b * WIDTH) if b else total)
        before, centre, after = rows_of
        core_sum[e] = (
            centre
            + jnp.where(plane_lane < PLANE - WIDTH, after, 0.0)
            + jnp.where(plane_lane >= WIDTH, before, 0.0)
        )
        outward = jnp.where(gy == 0, before[:, :128], after[:, PLANE - 128:])
        row_sum[e] = jnp.where(row_side, outward, 0.0)

    def resp_row(n):
        return resp_in.at[:, pl.ds(2 * PLANE + n * 128, 128)]

    outer = Group(resp_in)
    outer.send(core_sum.at[0], resp_in.at[:, pl.ds(PLANE, PLANE)], (d_prev, gy, af))
    outer.send(core_sum.at[3], resp_in.at[:, pl.ds(0, PLANE)], (d_next, gy, af))
    outer.send(row_sum.at[1], resp_row(0), (gz, side, af))
    outer.send(row_sum.at[2], resp_row(1), (gz, side, af))
    outer.send(row_sum.at[0], resp_row(3), (d_prev, side, af))
    outer.send(row_sum.at[3], resp_row(2), (d_next, side, af))

    scatter_again(1)
    gather(0)
    ring.middle()

    outer.wait_recv()
    for d, valid in ((0, gz > 0), (1, gz < 15)):
        total = core_sum[d + 1] + jnp.where(valid, resp_in[:, pl.ds(d * PLANE, PLANE)], 0.0)
        slab = resp_row(d)[...] + jnp.where(valid, resp_row(2 + d)[...], 0.0)
        slab = jnp.concatenate(
            [
                jnp.where(gy == 1, slab, 0.0),
                jnp.zeros((OWN, PLANE - 256), F32),
                jnp.where(gy == 0, slab, 0.0),
            ],
            axis=1,
        )
        resp_out[:, d, :] = (total + slab).astype(BF16)

    gather(1)
    gather_again(0)
    gather_again(1)
    total = ring.end().astype(BF16)
    for d in (0, 1):
        back_out[:, d, :] = total[:, d * PLANE:(d + 1) * PLANE]
    for u in range(4):
        gathered_again[u].wait_recv()
    for group in groups:
        group.wait_send()


def shards(features, filters, cotangent):
    vmem = pl.BlockSpec(memory_space=pltpu.VMEM)
    resp, back, grad = pl.pallas_call(
        kernel,
        out_shape=(
            jax.ShapeDtypeStruct((OWN, 2, PLANE), BF16),
            jax.ShapeDtypeStruct((OWN, 2, PLANE), BF16),
            jax.ShapeDtypeStruct((PADDED, C), F32),
        ),
        in_specs=[pl.BlockSpec(memory_space=pl.ANY)] * 3,
        out_specs=(vmem,) * 3,
        scratch_shapes=[
            pltpu.VMEM((OWN, 2, PLANE), BF16),
            pltpu.VMEM((OWN, 2, PLANE), BF16),
            pltpu.VMEM((ROWS, C), BF16),
            pltpu.VMEM((C, ROWS), BF16),
            pltpu.VMEM((OWN, CELLS), BF16),
            pltpu.VMEM((OWN, CELLS), BF16),
            pltpu.VMEM((C, CELLS), BF16),
            pltpu.VMEM((OWN, 2 * PLANE + 4 * 128), BF16),
            pltpu.VMEM((ROWS, CELLS), BF16),
            pltpu.VMEM((C, CELLS), F32),
            pltpu.VMEM((4, OWN, CELLS), F32),
            pltpu.VMEM((4, OWN, CELLS), F32),
            pltpu.VMEM((OWN, CELLS), F32),
            pltpu.VMEM((2, OWN, CELLS), F32),
            pltpu.VMEM((ROWS, CELLS), F32),
            pltpu.VMEM((4, OWN, PLANE), F32),
            pltpu.VMEM((4, OWN, 128), F32),
            pltpu.VMEM((OWN, 2 * PLANE + 4 * 128), F32),
            pltpu.VMEM((2, PADDED, 128), F32),
            pltpu.VMEM((4, 3, CHUNK, 128), F32),
            pltpu.VMEM((4, CHUNK + 16, 128), F32),
            pltpu.VMEM((4, 7, 16, 128), F32),
            pltpu.VMEM((4, CHUNK + 16, 128), F32),
            pltpu.SemaphoreType.DMA((3,)),
            pltpu.SemaphoreType.DMA((N_GROUPS,)),
            pltpu.SemaphoreType.DMA((N_GROUPS,)),
        ],
        compiler_params=pltpu.CompilerParams(
            collective_id=0, has_side_effects=True, vmem_limit_bytes=60 * 1024 * 1024
        ),
    )(
        features,
        cotangent,
        filters.reshape(ROWS, C),
    )
    return resp, back, grad[:ROWS].reshape(filters.shape)


def solution(mesh):
    placed = (P("af", "gz", "gy"), P(None, None, None, "af", None), P("af", "gz", "gy"))
    return jax.shard_map(
        shards,
        mesh=mesh,
        in_specs=placed,
        out_specs=(P("af", "gz", "gy"), P("af", "gz", "gy"), P(None, None, None, "af", None)),
        check_vma=False,
    )
```

```python
import functools
import math

import jax
import jax.numpy as jnp
from jax import lax
from jax.experimental import pallas as pl
from jax.experimental.pallas import tpu as pltpu
from jax.sharding import PartitionSpec as P

MESH = pl.DeviceIdType.MESH
F32 = jnp.float32
BF16 = jnp.bfloat16
WIDTH = 64
PLANE = 512
CELLS = 1024
OWN = 32
C = 256
TAPS = 27
ROWS = TAPS * OWN
PADDED = 896
CHUNK = PADDED // 8
N_GROUPS = 32


def tap_index(a, b, c):
    return ((a + 1) * 3 + (b + 1)) * 3 + (c + 1)


def roll(x, shift):
    return pltpu.roll(x, shift % x.shape[1], 1)


def aligned(start, size, unit):
    return pl.ds(pl.multiple_of(start, unit), size)


def encode(blocks):
    top = functools.reduce(jnp.maximum, [jnp.abs(block) for block in blocks])
    scale = jnp.maximum(top * 2.0**-15, 1e-30).astype(BF16)
    inverse = 1.0 / scale.astype(F32)
    codes = []
    for block in blocks:
        power = block * inverse
        for _ in range(3):
            power = power * power
        codes.append(jnp.where(block < 0, -power, power).astype(BF16))
    return codes, scale


def decode(codes, scale):
    scale = scale.astype(F32)
    blocks = []
    for code in codes:
        code = code.astype(F32)
        root = lax.rsqrt(lax.rsqrt(jnp.maximum(jnp.abs(code), 2e-38)))
        root = root * lax.rsqrt(root) * scale
        blocks.append(jnp.where(code < 0, -root, root))
    return blocks


def put_rows(ref, value):
    codes, scale = encode([value[i:i + 16] for i in range(0, CHUNK, 16)])
    ref[pl.ds(0, CHUNK)] = jnp.concatenate(codes, axis=0)
    ref[pl.ds(CHUNK, 16)] = scale


def get_rows(ref):
    codes = [ref[pl.ds(i, 16)] for i in range(0, CHUNK, 16)]
    return jnp.concatenate(decode(codes, ref[pl.ds(CHUNK, 16)]), axis=0)


def put_columns(ref, value):
    codes, scale = encode([value[:, i:i + 128] for i in range(0, CELLS, 128)])
    ref[:, pl.ds(0, CELLS)] = jnp.concatenate(codes, axis=1)
    ref[:, pl.ds(CELLS, 128)] = scale


def get_columns(ref):
    codes = [ref[:, pl.ds(i, 128)] for i in range(0, CELLS, 128)]
    return jnp.concatenate(decode(codes, ref[:, pl.ds(CELLS, 128)]), axis=1)


class Ring:
    def __init__(self, group, chunks, pos, nxt, prv, out, first, both):
        self.group, self.chunks, self.pos, self.nxt, self.prv = group, chunks, pos, nxt, prv
        self.out, self.first, self.both = out, first, both

    def part(self, k, half):
        return self.chunks[(self.pos + k) % 4, pl.ds(half * 16, 16)]

    def start(self):
        self.early, self.late = self.group(self.first), self.group(self.both)
        put_columns(self.out.at[0], self.part(2, 0))
        self.early.send(self.out.at[0], self.first.at[0], self.nxt)
        put_columns(self.out.at[1], self.part(2, 1))
        self.early.send(self.out.at[1], self.first.at[1], self.prv)
        put_columns(self.out.at[2], self.part(1, 1))
        self.late.send(self.out.at[2], self.both.at[0, 1], self.nxt)
        put_columns(self.out.at[3], self.part(3, 0))
        self.late.send(self.out.at[3], self.both.at[1, 0], self.prv)

    def middle(self):
        self.early.wait_recv()
        put_columns(self.out.at[4], self.part(1, 0) + get_columns(self.first.at[0]))
        self.late.send(self.out.at[4], self.both.at[0, 0], self.nxt)
        put_columns(self.out.at[5], self.part(3, 1) + get_columns(self.first.at[1]))
        self.late.send(self.out.at[5], self.both.at[1, 1], self.prv)

    def end(self):
        self.late.wait_recv()
        return [
            self.part(0, half) + get_columns(self.both.at[0, half]) + get_columns(self.both.at[1, half])
            for half in (0, 1)
        ]


def kernel(
    feat_hbm, cot_hbm, taps_hbm, resp_out, back_out, grad_out,
    feat_raw, cot_raw, taps, taps_t, feat, cot, field, cot_halo, cim,
    back, back_in, back_sum, back_code, back_first, back_both,
    z, core_sum, row_sum, resp_in,
    grad, grad_code, grad_in, part, part_in, whole, whole_code, whole_in,
    load_sem, send_sem, recv_sem,
):
    loads = [
        pltpu.make_async_copy(src, dst, load_sem.at[n])
        for n, (src, dst) in enumerate(((feat_hbm, feat_raw), (cot_hbm, cot_raw), (taps_hbm, taps)))
    ]
    for load in loads:
        load.start()
    gz = lax.axis_index("gz")
    gy = lax.axis_index("gy")
    af = lax.axis_index("af")
    py, px = gz // 4, gz % 4
    zh, core = af // 2, af % 2

    sibling = (gz, gy, zh * 2 + (1 - core))
    d_next, d_prev = (gz + 1) % 16, (gz + 15) % 16
    side = 1 - gy

    def along_x(k, row=gy):
        return (py * 4 + (px + k) % 4, row, af)

    def along_y(k, row=gy):
        return (((py + k) % 4) * 4 + px, row, af)

    def along_z(k):
        return (gz, gy, ((zh + k) % 4) * 2 + core)

    groups = []

    class Group:
        def __init__(self, size):
            self.index, self.size = len(groups), size
            groups.append(self)

        def send(self, src, dst, device):
            pltpu.make_async_remote_copy(
                src_ref=src, dst_ref=dst,
                send_sem=send_sem.at[self.index], recv_sem=recv_sem.at[self.index],
                device_id=device, device_id_type=MESH,
            ).start()
            return self

        def wait_recv(self):
            pltpu.make_async_copy(self.size, self.size, recv_sem.at[self.index]).wait()

        def wait_send(self):
            pltpu.make_async_copy(self.size, self.size, send_sem.at[self.index]).wait()

    partners = [sibling, (d_next, gy, af), (d_prev, gy, af)]
    partners += [(d_next, side, af), (d_prev, side, af), (gz, side, af)]
    partners += [along_z(1), along_z(3)]
    for k in (1, 2, 3):
        for along in (along_x, along_y):
            partners += [along(k), along(k, side)]
    barrier = pltpu.get_barrier_semaphore()
    for partner in partners:
        pl.semaphore_signal(barrier, inc=1, device_id=partner, device_id_type=MESH)
    for load, raw, flat in zip(loads, (feat_raw, cot_raw), (feat, cot)):
        load.wait()
        for d in (0, 1):
            flat[:, pl.ds(d * PLANE, PLANE)] = raw[:, d, :]
    loads[2].wait()
    taps_t[...] = taps[...].T
    pl.semaphore_wait(barrier, len(partners))

    def block(channels_of):
        return field.at[aligned(channels_of * OWN, OWN, OWN)]

    pair = 1 + 2 * (zh % 2)
    other = 4 - pair
    far = 2

    def owner(k):
        return ((zh + k) % 4) * 2 + core

    def pass_on(rows, device):
        return Group(rows).send(rows, rows, device)

    def half_block(k, start):
        return field.at[aligned(owner(k) * OWN + start, 16, 16)]

    from_pair = Group(block(af)).send(feat, block(af), along_z(pair))
    from_sibling = Group(block(af)).send(feat, block(af), sibling)

    edge = (1 - gy) * (PLANE - 128)
    low_edge = cot.at[:, aligned(edge, 128, 128)]
    high_edge = cot.at[:, aligned(edge + PLANE, 128, 128)]

    def halo(n):
        return cot_halo.at[:, pl.ds(2 * PLANE + n * 128, 128)]

    halos = Group(cot_halo)
    halos.send(low_edge, halo(3), (d_prev, side, af))
    halos.send(high_edge, halo(0), (d_next, side, af))
    halos.send(cot.at[:, pl.ds(0, PLANE)], cot_halo.at[:, pl.ds(PLANE, PLANE)], (d_prev, gy, af))
    halos.send(cot.at[:, pl.ds(PLANE, PLANE)], cot_halo.at[:, pl.ds(0, PLANE)], (d_next, gy, af))
    halos.send(low_edge, halo(1), (gz, side, af))
    halos.send(high_edge, halo(2), (gz, side, af))
    from_other = Group(block(af)).send(feat, block(af), along_z(other))
    block(af)[...] = feat[...]

    from_pair.wait_recv()
    far_by_other = pass_on(half_block(pair, 0), along_z(other))
    pair_relay = pass_on(block(owner(pair)), sibling)

    halos.wait_recv()
    lane = lax.broadcasted_iota(jnp.int32, (OWN, PLANE + 128), 1)
    column = lane % WIDTH
    slab_lane = lax.broadcasted_iota(jnp.int32, (OWN, 128), 1)
    row_side = (slab_lane < WIDTH) == (gy == 0)
    inside = (gz > 0, None, None, gz < 15)
    for e in range(4):
        if e in (1, 2):
            plane = cot[:, pl.ds((e - 1) * PLANE, PLANE)].astype(F32)
        else:
            plane = cot_halo[:, pl.ds((e // 3) * PLANE, PLANE)].astype(F32)
        rows = jnp.where(row_side, halo(e)[...].astype(F32), 0.0)
        base = jnp.concatenate([plane, rows], axis=1)
        if inside[e] is not None:
            base = jnp.where(inside[e], base, 0.0)
        for c in (-1, 0, 1):
            if c == 0:
                moved = base
            else:
                moved = jnp.where(column == (0 if c == 1 else WIDTH - 1), 0.0, roll(base, c))
            tall = roll(moved, WIDTH).astype(BF16)
            moved = moved.astype(BF16)
            for a in (-1, 0, 1):
                d = e - 1 + a
                if d not in (0, 1):
                    continue
                for b in (-1, 0, 1):
                    piece = {-1: tall[:, 128:], 0: moved[:, :PLANE], 1: tall[:, :PLANE]}[b]
                    cim[pl.ds(tap_index(a, b, c) * OWN, OWN), pl.ds(d * PLANE, PLANE)] = piece

    near_lanes = (zh // 2) * 128

    def channels(half):
        return near_lanes if half == 0 else 128 - near_lanes

    def filter_products(half):
        grad[half, pl.ds(0, ROWS)] = lax.dot_general(
            cim[...], field[aligned(channels(half), 128, 128)],
            (((1,), (1,)), ((), ())), preferred_element_type=F32,
        )
        grad[half, pl.ds(ROWS, PADDED - ROWS)] = jnp.zeros((PADDED - ROWS, 128), F32)

    orders = ((px, along_x, py, along_y), (py, along_y, px, along_x))

    def unit_rows(r, i):
        return aligned(r * 4 * CHUNK + i * CHUNK, CHUNK, 16)

    def scatter(half):
        for r, (pos, along, _, _) in enumerate(orders):
            u = half * 2 + r
            sent = Group(grad_in.at[u])
            for k in (2, 1, 3):
                code = grad_code.at[u, k - 1]
                put_rows(code, grad[half, unit_rows(r, (pos + k) % 4)])
                sent.send(code, grad_in.at[u, k - 1], along(k))
            scattered[u] = sent

    def eight(pos, along):
        others = []
        for step in (5, 4, 3, 2, 7, 6, 1):
            k, row = step // 2, gy if step % 2 == 0 else side
            others.append((step - 1, along(k, row), ((pos + k) % 4) * 2 + row))
        return pos * 2 + gy, others

    def scatter_again(half):
        for r, (pos, _, pos2, along2) in enumerate(orders):
            u = half * 2 + r
            scattered[u].wait_recv()
            total = grad[half, unit_rows(r, pos)]
            for n in range(3):
                total = total + get_rows(grad_in.at[u, n])
            part[u, pl.ds(0, CHUNK)] = total
            part[u, pl.ds(CHUNK, 16)] = jnp.zeros((16, 128), F32)
            sent = Group(part_in.at[u])
            for n, device, there in eight(pos2, along2)[1]:
                sent.send(part.at[u, aligned(there * 16, 16, 16)], part_in.at[u, n], device)
            scattered_again[u] = sent

    def gather(half):
        for r, (_, _, pos2, along2) in enumerate(orders):
            u = half * 2 + r
            mine, others = eight(pos2, along2)
            rows = aligned(mine * 16, 16, 16)
            scattered_again[u].wait_recv()
            total = part[u, rows]
            for n in range(7):
                total = total + part_in[u, n]
            whole[u, rows] = total * (1.0 / math.sqrt(32768.0))
            sent = Group(part_in.at[u])
            for _, device, _ in others:
                sent.send(whole.at[u, rows], whole.at[u, rows], device)
            gathered[u] = sent

    def gather_again(half):
        lanes = aligned(channels(half), 128, 128)
        for r, (pos, along, _, _) in enumerate(orders):
            u = half * 2 + r
            gathered[u].wait_recv()
            code = whole_code.at[u]
            put_rows(code, whole[u, pl.ds(0, CHUNK)])
            sent = Group(whole_in.at[u])
            for k in (2, 1, 3):
                sent.send(code, whole_in.at[u, k - 1], along(k))
            grad_out[unit_rows(r, pos), lanes] = get_rows(code)
            gathered_again[u] = sent

    def finish(half):
        lanes = aligned(channels(half), 128, 128)
        for r, (pos, _, _, _) in enumerate(orders):
            u = half * 2 + r
            gathered_again[u].wait_recv()

            @pl.loop(0, 3)
            def _(n):
                grad_out[unit_rows(r, (pos + 3 - n) % 4), lanes] = get_rows(whole_in.at[u, n])

    scattered, scattered_again, gathered, gathered_again = {}, {}, {}, {}

    from_other.wait_recv()
    far_by_pair = pass_on(half_block(other, 16), along_z(pair))
    other_relay = pass_on(block(owner(other)), sibling)
    from_sibling.wait_recv()
    pair_relay.wait_recv()
    filter_products(0)
    scatter(0)

    far_by_other.wait_recv()
    far_by_pair.wait_recv()
    far_relay = pass_on(block(owner(far)), sibling)
    other_relay.wait_recv()
    far_relay.wait_recv()
    filter_products(1)
    scatter(1)

    @pl.loop(0, 4)
    def _(n):
        cols = aligned(n * 256, 256, 256)
        back[:, cols] = lax.dot_general(
            taps_t[...], cim[:, cols], (((1,), (0,)), ((), ())), preferred_element_type=F32
        )

    to_sibling = Group(back_in)
    for k in range(4):
        to_sibling.send(back.at[aligned((2 * k + 1 - core) * OWN, OWN, OWN)], back_in.at[k], sibling)

    @pl.loop(0, 4)
    def _(n):
        cols = aligned(n * 256, 256, 256)
        z[:, cols] = jnp.dot(taps[...], field[:, cols], preferred_element_type=F32)

    scatter_again(0)

    to_sibling.wait_recv()
    for k in range(4):
        back_sum[k] = back[aligned((2 * k + core) * OWN, OWN, OWN)] + back_in[k]

    ring = Ring(Group, back_sum, zh, along_z(1), along_z(3), back_code, back_first, back_both)
    ring.start()

    plane_lane = lane[:, :PLANE]
    plane_column = column[:, :PLANE]
    for e in range(4):
        rows_of = []
        for b in (-1, 0, 1):
            total = None
            for c in (-1, 0, 1):
                term = None
                for a in (-1, 0, 1):
                    d = e - 1 + a
                    if d in (0, 1):
                        value = z[pl.ds(tap_index(a, b, c) * OWN, OWN), pl.ds(d * PLANE, PLANE)]
                        term = value if term is None else term + value
                if c:
                    out = WIDTH - 1 if c == 1 else 0
                    term = jnp.where(plane_column == out, 0.0, roll(term, -c))
                total = term if total is None else total + term
            rows_of.append(roll(total, -b * WIDTH) if b else total)
        before, centre, after = rows_of
        core_sum[e] = (
            centre
            + jnp.where(plane_lane < PLANE - WIDTH, after, 0.0)
            + jnp.where(plane_lane >= WIDTH, before, 0.0)
        )
        outward = jnp.where(gy == 0, before[:, :128], after[:, PLANE - 128:])
        row_sum[e] = jnp.where(row_side, outward, 0.0)

    def resp_row(n):
        return resp_in.at[:, pl.ds(2 * PLANE + n * 128, 128)]

    outer = Group(resp_in)
    outer.send(core_sum.at[0], resp_in.at[:, pl.ds(PLANE, PLANE)], (d_prev, gy, af))
    outer.send(core_sum.at[3], resp_in.at[:, pl.ds(0, PLANE)], (d_next, gy, af))
    outer.send(row_sum.at[1], resp_row(0), (gz, side, af))
    outer.send(row_sum.at[2], resp_row(1), (gz, side, af))
    outer.send(row_sum.at[0], resp_row(3), (d_prev, side, af))
    outer.send(row_sum.at[3], resp_row(2), (d_next, side, af))

    scatter_again(1)
    gather(0)
    ring.middle()

    outer.wait_recv()
    for d, valid in ((0, gz > 0), (1, gz < 15)):
        total = core_sum[d + 1] + jnp.where(valid, resp_in[:, pl.ds(d * PLANE, PLANE)], 0.0)
        slab = resp_row(d)[...] + jnp.where(valid, resp_row(2 + d)[...], 0.0)
        slab = jnp.concatenate(
            [
                jnp.where(gy == 1, slab, 0.0),
                jnp.zeros((OWN, PLANE - 256), F32),
                jnp.where(gy == 0, slab, 0.0),
            ],
            axis=1,
        )
        resp_out[:, d, :] = (total + slab).astype(BF16)

    gather(1)
    gather_again(0)
    gather_again(1)
    for half, total in enumerate(ring.end()):
        for d in (0, 1):
            back_out[pl.ds(half * 16, 16), d, :] = total[:, d * PLANE:(d + 1) * PLANE].astype(BF16)
    finish(0)
    finish(1)
    for group in groups:
        group.wait_send()


def shards(features, filters, cotangent):
    vmem = pl.BlockSpec(memory_space=pltpu.VMEM)
    resp, back, grad = pl.pallas_call(
        kernel,
        out_shape=(
            pltpu.VMEM((OWN, 2, PLANE), BF16),
            pltpu.VMEM((OWN, 2, PLANE), BF16),
            pltpu.VMEM((PADDED, C), F32),
        ),
        in_specs=[pl.BlockSpec(memory_space=pl.ANY)] * 3,
        out_specs=(vmem,) * 3,
        scratch_shapes=[
            pltpu.VMEM((OWN, 2, PLANE), BF16),
            pltpu.VMEM((OWN, 2, PLANE), BF16),
            pltpu.VMEM((ROWS, C), BF16),
            pltpu.VMEM((C, ROWS), BF16),
            pltpu.VMEM((OWN, CELLS), BF16),
            pltpu.VMEM((OWN, CELLS), BF16),
            pltpu.VMEM((C, CELLS), BF16),
            pltpu.VMEM((OWN, 2 * PLANE + 4 * 128), BF16),
            pltpu.VMEM((ROWS, CELLS), BF16),
            pltpu.VMEM((C, CELLS), F32),
            pltpu.VMEM((4, OWN, CELLS), F32),
            pltpu.VMEM((4, OWN, CELLS), F32),
            pltpu.VMEM((6, 16, CELLS + 128), BF16),
            pltpu.VMEM((2, 16, CELLS + 128), BF16),
            pltpu.VMEM((2, 2, 16, CELLS + 128), BF16),
            pltpu.VMEM((ROWS, CELLS), F32),
            pltpu.VMEM((4, OWN, PLANE), F32),
            pltpu.VMEM((4, OWN, 128), F32),
            pltpu.VMEM((OWN, 2 * PLANE + 4 * 128), F32),
            pltpu.VMEM((2, PADDED, 128), F32),
            pltpu.VMEM((4, 3, CHUNK + 16, 128), BF16),
            pltpu.VMEM((4, 3, CHUNK + 16, 128), BF16),
            pltpu.VMEM((4, CHUNK + 16, 128), F32),
            pltpu.VMEM((4, 7, 16, 128), F32),
            pltpu.VMEM((4, CHUNK + 16, 128), F32),
            pltpu.VMEM((4, CHUNK + 16, 128), BF16),
            pltpu.VMEM((4, 3, CHUNK + 16, 128), BF16),
            pltpu.SemaphoreType.DMA((3,)),
            pltpu.SemaphoreType.DMA((N_GROUPS,)),
            pltpu.SemaphoreType.DMA((N_GROUPS,)),
        ],
        compiler_params=pltpu.CompilerParams(
            collective_id=0, has_side_effects=True, vmem_limit_bytes=60 * 1024 * 1024
        ),
    )(
        features,
        cotangent,
        filters.reshape(ROWS, C),
    )
    return resp, back, grad[:ROWS].reshape(filters.shape)


def solution(mesh):
    placed = (P("af", "gz", "gy"), P(None, None, None, "af", None), P("af", "gz", "gy"))
    return jax.shard_map(
        shards,
        mesh=mesh,
        in_specs=placed,
        out_specs=(P("af", "gz", "gy"), P("af", "gz", "gy"), P(None, None, None, "af", None)),
        check_vma=False,
    )
```

```python
import functools
import math

import jax
import jax.numpy as jnp
from jax import lax
from jax.experimental import pallas as pl
from jax.experimental.pallas import tpu as pltpu
from jax.sharding import PartitionSpec as P

MESH = pl.DeviceIdType.MESH
F32 = jnp.float32
BF16 = jnp.bfloat16
WIDTH = 64
PLANE = 512
CELLS = 1024
OWN = 32
C = 256
TAPS = 27
ROWS = TAPS * OWN
PADDED = 896
CHUNK = PADDED // 8
N_GROUPS = 32


def tap_index(a, b, c):
    return ((a + 1) * 3 + (b + 1)) * 3 + (c + 1)


def roll(x, shift):
    return pltpu.roll(x, shift % x.shape[1], 1)


def aligned(start, size, unit):
    return pl.ds(pl.multiple_of(start, unit), size)


def encode(blocks):
    top = functools.reduce(jnp.maximum, [jnp.abs(block) for block in blocks])
    scale = jnp.maximum(top * 2.0**-7.75, 1e-30).astype(BF16)
    inverse = 1.0 / scale.astype(F32)
    codes = []
    for block in blocks:
        power = block * inverse
        for _ in range(4):
            power = power * power
        codes.append(jnp.where(block < 0, -power, power).astype(BF16))
    return codes, scale


def decode(codes, scale):
    scale = scale.astype(F32)
    blocks = []
    for code in codes:
        code = code.astype(F32)
        root = jnp.maximum(jnp.abs(code), 2e-38)
        for _ in range(4):
            root = lax.rsqrt(root)
        root = jnp.where(code == 0, 0.0, root * scale)
        blocks.append(jnp.where(code < 0, -root, root))
    return blocks


def put_rows(ref, value):
    codes, scale = encode([value[i:i + 16] for i in range(0, CHUNK, 16)])
    ref[pl.ds(0, CHUNK)] = jnp.concatenate(codes, axis=0)
    ref[pl.ds(CHUNK, 16)] = scale


def get_rows(ref):
    codes = [ref[pl.ds(i, 16)] for i in range(0, CHUNK, 16)]
    return jnp.concatenate(decode(codes, ref[pl.ds(CHUNK, 16)]), axis=0)


def put_columns(ref, value):
    codes, scale = encode([value[:, i:i + 128] for i in range(0, CELLS, 128)])
    ref[:, pl.ds(0, CELLS)] = jnp.concatenate(codes, axis=1)
    ref[:, pl.ds(CELLS, 128)] = scale


def get_columns(ref):
    codes = [ref[:, pl.ds(i, 128)] for i in range(0, CELLS, 128)]
    return jnp.concatenate(decode(codes, ref[:, pl.ds(CELLS, 128)]), axis=1)


class Ring:
    def __init__(self, group, chunks, pos, nxt, prv, out, first, both):
        self.group, self.chunks, self.pos, self.nxt, self.prv = group, chunks, pos, nxt, prv
        self.out, self.first, self.both = out, first, both

    def part(self, k, half):
        return self.chunks[(self.pos + k) % 4, pl.ds(half * 16, 16)]

    def start(self):
        self.early, self.late = self.group(self.first), self.group(self.both)
        put_columns(self.out.at[0], self.part(2, 0))
        self.early.send(self.out.at[0], self.first.at[0], self.nxt)
        put_columns(self.out.at[1], self.part(2, 1))
        self.early.send(self.out.at[1], self.first.at[1], self.prv)
        put_columns(self.out.at[2], self.part(1, 1))
        self.late.send(self.out.at[2], self.both.at[0, 1], self.nxt)
        put_columns(self.out.at[3], self.part(3, 0))
        self.late.send(self.out.at[3], self.both.at[1, 0], self.prv)

    def middle(self):
        self.early.wait_recv()
        put_columns(self.out.at[4], self.part(1, 0) + get_columns(self.first.at[0]))
        self.late.send(self.out.at[4], self.both.at[0, 0], self.nxt)
        put_columns(self.out.at[5], self.part(3, 1) + get_columns(self.first.at[1]))
        self.late.send(self.out.at[5], self.both.at[1, 1], self.prv)

    def end(self):
        self.late.wait_recv()
        return [
            self.part(0, half) + get_columns(self.both.at[0, half]) + get_columns(self.both.at[1, half])
            for half in (0, 1)
        ]


def kernel(
    feat_hbm, cot_hbm, taps_hbm, resp_out, back_out, grad_out,
    feat_raw, cot_raw, taps, taps_t, feat, cot, field, cot_halo, cim,
    back, back_in, back_sum, back_code, back_first, back_both,
    z, core_sum, row_sum, resp_in,
    grad, grad_code, grad_in, part, part_in, whole, whole_code, whole_in,
    load_sem, send_sem, recv_sem,
):
    loads = [
        pltpu.make_async_copy(src, dst, load_sem.at[n])
        for n, (src, dst) in enumerate(((feat_hbm, feat_raw), (cot_hbm, cot_raw), (taps_hbm, taps)))
    ]
    for load in loads:
        load.start()
    gz = lax.axis_index("gz")
    gy = lax.axis_index("gy")
    af = lax.axis_index("af")
    py, px = gz // 4, gz % 4
    zh, core = af // 2, af % 2

    sibling = (gz, gy, zh * 2 + (1 - core))
    d_next, d_prev = (gz + 1) % 16, (gz + 15) % 16
    side = 1 - gy

    def along_x(k, row=gy):
        return (py * 4 + (px + k) % 4, row, af)

    def along_y(k, row=gy):
        return (((py + k) % 4) * 4 + px, row, af)

    def along_z(k):
        return (gz, gy, ((zh + k) % 4) * 2 + core)

    groups = []

    class Group:
        def __init__(self, size):
            self.index, self.size = len(groups), size
            groups.append(self)

        def send(self, src, dst, device):
            pltpu.make_async_remote_copy(
                src_ref=src, dst_ref=dst,
                send_sem=send_sem.at[self.index], recv_sem=recv_sem.at[self.index],
                device_id=device, device_id_type=MESH,
            ).start()
            return self

        def wait_recv(self):
            pltpu.make_async_copy(self.size, self.size, recv_sem.at[self.index]).wait()

        def wait_send(self):
            pltpu.make_async_copy(self.size, self.size, send_sem.at[self.index]).wait()

    partners = [sibling, (d_next, gy, af), (d_prev, gy, af)]
    partners += [(d_next, side, af), (d_prev, side, af), (gz, side, af)]
    partners += [along_z(1), along_z(3)]
    for k in (1, 2, 3):
        for along in (along_x, along_y):
            partners += [along(k), along(k, side)]
    barrier = pltpu.get_barrier_semaphore()
    for partner in partners:
        pl.semaphore_signal(barrier, inc=1, device_id=partner, device_id_type=MESH)

    def lay_flat(n, raw, flat):
        loads[n].wait()
        for d in (0, 1):
            flat[:, pl.ds(d * PLANE, PLANE)] = raw[:, d, :]

    lay_flat(0, feat_raw, feat)
    pl.semaphore_wait(barrier, len(partners))

    def block(channels_of):
        return field.at[aligned(channels_of * OWN, OWN, OWN)]

    pair = 1 + 2 * (zh % 2)
    other = 4 - pair
    far = 2

    def owner(k):
        return ((zh + k) % 4) * 2 + core

    def pass_on(rows, device):
        return Group(rows).send(rows, rows, device)

    def half_block(k, start):
        return field.at[aligned(owner(k) * OWN + start, 16, 16)]

    from_pair = Group(block(af)).send(feat, block(af), along_z(pair))
    from_other = Group(block(af)).send(feat, block(af), along_z(other))
    from_sibling = Group(block(af)).send(feat, block(af), sibling)
    lay_flat(1, cot_raw, cot)

    edge = (1 - gy) * (PLANE - 128)
    low_edge = cot.at[:, aligned(edge, 128, 128)]
    high_edge = cot.at[:, aligned(edge + PLANE, 128, 128)]

    def halo(n):
        return cot_halo.at[:, pl.ds(2 * PLANE + n * 128, 128)]

    halos = Group(cot_halo)
    halos.send(low_edge, halo(3), (d_prev, side, af))
    halos.send(high_edge, halo(0), (d_next, side, af))
    halos.send(cot.at[:, pl.ds(0, PLANE)], cot_halo.at[:, pl.ds(PLANE, PLANE)], (d_prev, gy, af))
    halos.send(cot.at[:, pl.ds(PLANE, PLANE)], cot_halo.at[:, pl.ds(0, PLANE)], (d_next, gy, af))
    halos.send(low_edge, halo(1), (gz, side, af))
    halos.send(high_edge, halo(2), (gz, side, af))
    block(af)[...] = feat[...]
    loads[2].wait()
    taps_t[...] = taps[...].T

    from_pair.wait_recv()
    far_by_other = pass_on(half_block(pair, 0), along_z(other))
    pair_relay = pass_on(block(owner(pair)), sibling)

    halos.wait_recv()
    lane = lax.broadcasted_iota(jnp.int32, (OWN, PLANE + 128), 1)
    column = lane % WIDTH
    slab_lane = lax.broadcasted_iota(jnp.int32, (OWN, 128), 1)
    row_side = (slab_lane < WIDTH) == (gy == 0)
    inside = (gz > 0, None, None, gz < 15)
    for e in range(4):
        if e in (1, 2):
            plane = cot[:, pl.ds((e - 1) * PLANE, PLANE)].astype(F32)
        else:
            plane = cot_halo[:, pl.ds((e // 3) * PLANE, PLANE)].astype(F32)
        rows = jnp.where(row_side, halo(e)[...].astype(F32), 0.0)
        base = jnp.concatenate([plane, rows], axis=1)
        if inside[e] is not None:
            base = jnp.where(inside[e], base, 0.0)
        for c in (-1, 0, 1):
            if c == 0:
                moved = base
            else:
                moved = jnp.where(column == (0 if c == 1 else WIDTH - 1), 0.0, roll(base, c))
            tall = roll(moved, WIDTH).astype(BF16)
            moved = moved.astype(BF16)
            for a in (-1, 0, 1):
                d = e - 1 + a
                if d not in (0, 1):
                    continue
                for b in (-1, 0, 1):
                    piece = {-1: tall[:, 128:], 0: moved[:, :PLANE], 1: tall[:, :PLANE]}[b]
                    cim[pl.ds(tap_index(a, b, c) * OWN, OWN), pl.ds(d * PLANE, PLANE)] = piece

    near_lanes = (zh // 2) * 128

    def channels(half):
        return near_lanes if half == 0 else 128 - near_lanes

    def filter_products(half):
        grad[half, pl.ds(0, ROWS)] = lax.dot_general(
            cim[...], field[aligned(channels(half), 128, 128)],
            (((1,), (1,)), ((), ())), preferred_element_type=F32,
        )
        grad[half, pl.ds(ROWS, PADDED - ROWS)] = jnp.zeros((PADDED - ROWS, 128), F32)

    orders = ((px, along_x, py, along_y), (py, along_y, px, along_x))

    def unit_rows(r, i):
        return aligned(r * 4 * CHUNK + i * CHUNK, CHUNK, 16)

    def scatter(half):
        for r, (pos, along, _, _) in enumerate(orders):
            u = half * 2 + r
            sent = Group(grad_in.at[u])
            for k in (2, 1, 3):
                code = grad_code.at[u, k - 1]
                put_rows(code, grad[half, unit_rows(r, (pos + k) % 4)])
                sent.send(code, grad_in.at[u, k - 1], along(k))
            scattered[u] = sent

    def eight(pos, along):
        others = []
        for step in (5, 4, 3, 2, 7, 6, 1):
            k, row = step // 2, gy if step % 2 == 0 else side
            others.append((step - 1, along(k, row), ((pos + k) % 4) * 2 + row))
        return pos * 2 + gy, others

    def scatter_again(half):
        for r, (pos, _, pos2, along2) in enumerate(orders):
            u = half * 2 + r
            scattered[u].wait_recv()
            total = grad[half, unit_rows(r, pos)]
            for n in range(3):
                total = total + get_rows(grad_in.at[u, n])
            part[u, pl.ds(0, CHUNK)] = total
            part[u, pl.ds(CHUNK, 16)] = jnp.zeros((16, 128), F32)
            sent = Group(part_in.at[u])
            for n, device, there in eight(pos2, along2)[1]:
                sent.send(part.at[u, aligned(there * 16, 16, 16)], part_in.at[u, n], device)
            scattered_again[u] = sent

    def gather(half):
        for r, (_, _, pos2, along2) in enumerate(orders):
            u = half * 2 + r
            mine, others = eight(pos2, along2)
            rows = aligned(mine * 16, 16, 16)
            scattered_again[u].wait_recv()
            total = part[u, rows]
            for n in range(7):
                total = total + part_in[u, n]
            whole[u, rows] = total * (1.0 / math.sqrt(32768.0))
            sent = Group(part_in.at[u])
            for _, device, _ in others:
                sent.send(whole.at[u, rows], whole.at[u, rows], device)
            gathered[u] = sent

    def gather_again(half):
        lanes = aligned(channels(half), 128, 128)
        for r, (pos, along, _, _) in enumerate(orders):
            u = half * 2 + r
            gathered[u].wait_recv()
            code = whole_code.at[u]
            put_rows(code, whole[u, pl.ds(0, CHUNK)])
            sent = Group(whole_in.at[u])
            for k in (2, 1, 3):
                sent.send(code, whole_in.at[u, k - 1], along(k))
            grad_out[unit_rows(r, pos), lanes] = get_rows(code)
            gathered_again[u] = sent

    def finish(half):
        lanes = aligned(channels(half), 128, 128)
        for r, (pos, _, _, _) in enumerate(orders):
            u = half * 2 + r
            gathered_again[u].wait_recv()

            @pl.loop(0, 3)
            def _(n):
                grad_out[unit_rows(r, (pos + 3 - n) % 4), lanes] = get_rows(whole_in.at[u, n])

    scattered, scattered_again, gathered, gathered_again = {}, {}, {}, {}

    from_other.wait_recv()
    far_by_pair = pass_on(half_block(other, 16), along_z(pair))
    other_relay = pass_on(block(owner(other)), sibling)
    from_sibling.wait_recv()
    pair_relay.wait_recv()
    filter_products(0)
    scatter(0)

    far_by_other.wait_recv()
    far_by_pair.wait_recv()
    far_relay = pass_on(block(owner(far)), sibling)
    other_relay.wait_recv()
    far_relay.wait_recv()
    filter_products(1)
    scatter(1)

    @pl.loop(0, 4)
    def _(n):
        cols = aligned(n * 256, 256, 256)
        back[:, cols] = lax.dot_general(
            taps_t[...], cim[:, cols], (((1,), (0,)), ((), ())), preferred_element_type=F32
        )

    to_sibling = Group(back_in)
    for k in range(4):
        to_sibling.send(back.at[aligned((2 * k + 1 - core) * OWN, OWN, OWN)], back_in.at[k], sibling)

    scatter_again(0)

    to_sibling.wait_recv()
    for k in range(4):
        back_sum[k] = back[aligned((2 * k + core) * OWN, OWN, OWN)] + back_in[k]

    ring = Ring(Group, back_sum, zh, along_z(1), along_z(3), back_code, back_first, back_both)
    ring.start()

    @pl.loop(0, 4)
    def _(n):
        cols = aligned(n * 256, 256, 256)
        z[:, cols] = jnp.dot(taps[...], field[:, cols], preferred_element_type=F32)

    scatter_again(1)

    plane_lane = lane[:, :PLANE]
    plane_column = column[:, :PLANE]
    for e in range(4):
        rows_of = []
        for b in (-1, 0, 1):
            total = None
            for c in (-1, 0, 1):
                term = None
                for a in (-1, 0, 1):
                    d = e - 1 + a
                    if d in (0, 1):
                        value = z[pl.ds(tap_index(a, b, c) * OWN, OWN), pl.ds(d * PLANE, PLANE)]
                        term = value if term is None else term + value
                if c:
                    out = WIDTH - 1 if c == 1 else 0
                    term = jnp.where(plane_column == out, 0.0, roll(term, -c))
                total = term if total is None else total + term
            rows_of.append(roll(total, -b * WIDTH) if b else total)
        before, centre, after = rows_of
        core_sum[e] = (
            centre
            + jnp.where(plane_lane < PLANE - WIDTH, after, 0.0)
            + jnp.where(plane_lane >= WIDTH, before, 0.0)
        )
        outward = jnp.where(gy == 0, before[:, :128], after[:, PLANE - 128:])
        row_sum[e] = jnp.where(row_side, outward, 0.0)

    def resp_row(n):
        return resp_in.at[:, pl.ds(2 * PLANE + n * 128, 128)]

    outer = Group(resp_in)
    outer.send(core_sum.at[0], resp_in.at[:, pl.ds(PLANE, PLANE)], (d_prev, gy, af))
    outer.send(core_sum.at[3], resp_in.at[:, pl.ds(0, PLANE)], (d_next, gy, af))
    outer.send(row_sum.at[1], resp_row(0), (gz, side, af))
    outer.send(row_sum.at[2], resp_row(1), (gz, side, af))
    outer.send(row_sum.at[0], resp_row(3), (d_prev, side, af))
    outer.send(row_sum.at[3], resp_row(2), (d_next, side, af))

    gather(0)
    ring.middle()

    gather(1)
    outer.wait_recv()
    for d, valid in ((0, gz > 0), (1, gz < 15)):
        total = core_sum[d + 1] + jnp.where(valid, resp_in[:, pl.ds(d * PLANE, PLANE)], 0.0)
        slab = resp_row(d)[...] + jnp.where(valid, resp_row(2 + d)[...], 0.0)
        slab = jnp.concatenate(
            [
                jnp.where(gy == 1, slab, 0.0),
                jnp.zeros((OWN, PLANE - 256), F32),
                jnp.where(gy == 0, slab, 0.0),
            ],
            axis=1,
        )
        resp_out[:, d, :] = (total + slab).astype(BF16)

    gather_again(0)
    for half, total in enumerate(ring.end()):
        for d in (0, 1):
            back_out[pl.ds(half * 16, 16), d, :] = total[:, d * PLANE:(d + 1) * PLANE].astype(BF16)
    gather_again(1)
    finish(0)
    finish(1)
    for group in groups:
        group.wait_send()


def copy_out(resp, back, grad, resp_out, back_out, grad_out, sem):
    copies = [
        pltpu.make_async_copy(src, dst, sem.at[n])
        for n, (src, dst) in enumerate(
            ((grad.at[pl.ds(0, ROWS)], grad_out), (resp, resp_out), (back, back_out))
        )
    ]
    for copy in copies:
        copy.start()
    for copy in copies:
        copy.wait()


def shards(features, filters, cotangent):
    vmem = pl.BlockSpec(memory_space=pltpu.VMEM)
    resp, back, grad = pl.pallas_call(
        kernel,
        out_shape=(
            pltpu.VMEM((OWN, 2, PLANE), BF16),
            pltpu.VMEM((OWN, 2, PLANE), BF16),
            pltpu.VMEM((PADDED, C), F32),
        ),
        in_specs=[pl.BlockSpec(memory_space=pl.ANY)] * 3,
        out_specs=(vmem,) * 3,
        scratch_shapes=[
            pltpu.VMEM((OWN, 2, PLANE), BF16),
            pltpu.VMEM((OWN, 2, PLANE), BF16),
            pltpu.VMEM((ROWS, C), BF16),
            pltpu.VMEM((C, ROWS), BF16),
            pltpu.VMEM((OWN, CELLS), BF16),
            pltpu.VMEM((OWN, CELLS), BF16),
            pltpu.VMEM((C, CELLS), BF16),
            pltpu.VMEM((OWN, 2 * PLANE + 4 * 128), BF16),
            pltpu.VMEM((ROWS, CELLS), BF16),
            pltpu.VMEM((C, CELLS), F32),
            pltpu.VMEM((4, OWN, CELLS), F32),
            pltpu.VMEM((4, OWN, CELLS), F32),
            pltpu.VMEM((6, 16, CELLS + 128), BF16),
            pltpu.VMEM((2, 16, CELLS + 128), BF16),
            pltpu.VMEM((2, 2, 16, CELLS + 128), BF16),
            pltpu.VMEM((ROWS, CELLS), F32),
            pltpu.VMEM((4, OWN, PLANE), F32),
            pltpu.VMEM((4, OWN, 128), F32),
            pltpu.VMEM((OWN, 2 * PLANE + 4 * 128), F32),
            pltpu.VMEM((2, PADDED, 128), F32),
            pltpu.VMEM((4, 3, CHUNK + 16, 128), BF16),
            pltpu.VMEM((4, 3, CHUNK + 16, 128), BF16),
            pltpu.VMEM((4, CHUNK + 16, 128), F32),
            pltpu.VMEM((4, 7, 16, 128), F32),
            pltpu.VMEM((4, CHUNK + 16, 128), F32),
            pltpu.VMEM((4, CHUNK + 16, 128), BF16),
            pltpu.VMEM((4, 3, CHUNK + 16, 128), BF16),
            pltpu.SemaphoreType.DMA((3,)),
            pltpu.SemaphoreType.DMA((N_GROUPS,)),
            pltpu.SemaphoreType.DMA((N_GROUPS,)),
        ],
        compiler_params=pltpu.CompilerParams(
            collective_id=0, has_side_effects=True, vmem_limit_bytes=60 * 1024 * 1024
        ),
    )(
        features,
        cotangent,
        filters.reshape(ROWS, C),
    )
    resp, back, grad = pl.pallas_call(
        copy_out,
        out_shape=(
            jax.ShapeDtypeStruct((OWN, 2, PLANE), BF16),
            jax.ShapeDtypeStruct((OWN, 2, PLANE), BF16),
            jax.ShapeDtypeStruct((ROWS, C), F32),
        ),
        in_specs=[vmem] * 3,
        out_specs=(pl.BlockSpec(memory_space=pl.ANY),) * 3,
        scratch_shapes=[pltpu.SemaphoreType.DMA((3,))],
    )(resp, back, grad)
    return resp, back, grad.reshape(filters.shape)


def solution(mesh):
    placed = (P("af", "gz", "gy"), P(None, None, None, "af", None), P("af", "gz", "gy"))
    return jax.shard_map(
        shards,
        mesh=mesh,
        in_specs=placed,
        out_specs=(P("af", "gz", "gy"), P("af", "gz", "gy"), P(None, None, None, "af", None)),
        check_vma=False,
    )
```

```python
import functools
import math

import jax
import jax.numpy as jnp
from jax import lax
from jax.experimental import pallas as pl
from jax.experimental.pallas import tpu as pltpu
from jax.sharding import PartitionSpec as P

MESH = pl.DeviceIdType.MESH
F32 = jnp.float32
BF16 = jnp.bfloat16
WIDTH = 64
PLANE = 512
CELLS = 1024
OWN = 32
C = 256
TAPS = 27
ROWS = TAPS * OWN
PADDED = 896
CHUNK = PADDED // 8
N_GROUPS = 32


def tap_index(a, b, c):
    return ((a + 1) * 3 + (b + 1)) * 3 + (c + 1)


def roll(x, shift):
    return pltpu.roll(x, shift % x.shape[1], 1)


def aligned(start, size, unit):
    return pl.ds(pl.multiple_of(start, unit), size)


def encode(blocks):
    top = functools.reduce(jnp.maximum, [jnp.abs(block) for block in blocks])
    scale = jnp.maximum(top * 2.0**-7.75, 1e-30).astype(BF16)
    inverse = 1.0 / scale.astype(F32)
    codes = []
    for block in blocks:
        power = block * inverse
        for _ in range(4):
            power = power * power
        codes.append(jnp.where(block < 0, -power, power).astype(BF16))
    return codes, scale


def decode(codes, scale):
    scale = scale.astype(F32)
    blocks = []
    for code in codes:
        code = code.astype(F32)
        root = jnp.maximum(jnp.abs(code), 2e-38)
        for _ in range(4):
            root = lax.rsqrt(root)
        root = jnp.where(code == 0, 0.0, root * scale)
        blocks.append(jnp.where(code < 0, -root, root))
    return blocks


def put_rows(ref, value):
    codes, scale = encode([value[i:i + 16] for i in range(0, CHUNK, 16)])
    ref[pl.ds(0, CHUNK)] = jnp.concatenate(codes, axis=0)
    ref[pl.ds(CHUNK, 16)] = scale


def get_rows(ref):
    codes = [ref[pl.ds(i, 16)] for i in range(0, CHUNK, 16)]
    return jnp.concatenate(decode(codes, ref[pl.ds(CHUNK, 16)]), axis=0)


def put_columns(ref, value):
    codes, scale = encode([value[:, i:i + 128] for i in range(0, CELLS, 128)])
    ref[:, pl.ds(0, CELLS)] = jnp.concatenate(codes, axis=1)
    ref[:, pl.ds(CELLS, 128)] = scale


def get_columns(ref):
    codes = [ref[:, pl.ds(i, 128)] for i in range(0, CELLS, 128)]
    return jnp.concatenate(decode(codes, ref[:, pl.ds(CELLS, 128)]), axis=1)


class Ring:
    def __init__(self, group, chunks, pos, nxt, prv, out, first, both):
        self.group, self.chunks, self.pos, self.nxt, self.prv = group, chunks, pos, nxt, prv
        self.out, self.first, self.both = out, first, both

    def part(self, k, half):
        return self.chunks[(self.pos + k) % 4, pl.ds(half * 16, 16)]

    def start(self):
        self.early, self.late = self.group(self.first), self.group(self.both)
        put_columns(self.out.at[0], self.part(2, 0))
        self.early.send(self.out.at[0], self.first.at[0], self.nxt)
        put_columns(self.out.at[1], self.part(2, 1))
        self.early.send(self.out.at[1], self.first.at[1], self.prv)
        put_columns(self.out.at[2], self.part(1, 1))
        self.late.send(self.out.at[2], self.both.at[0, 1], self.nxt)
        put_columns(self.out.at[3], self.part(3, 0))
        self.late.send(self.out.at[3], self.both.at[1, 0], self.prv)

    def middle(self):
        self.early.wait_recv()
        put_columns(self.out.at[4], self.part(1, 0) + get_columns(self.first.at[0]))
        self.late.send(self.out.at[4], self.both.at[0, 0], self.nxt)
        put_columns(self.out.at[5], self.part(3, 1) + get_columns(self.first.at[1]))
        self.late.send(self.out.at[5], self.both.at[1, 1], self.prv)

    def end(self):
        self.late.wait_recv()
        return [
            self.part(0, half) + get_columns(self.both.at[0, half]) + get_columns(self.both.at[1, half])
            for half in (0, 1)
        ]


def kernel(
    feat_hbm, cot_hbm, taps_hbm, resp_out, back_out, grad_out,
    feat_raw, cot_raw, taps, taps_t, feat, cot, field, cot_halo, cim,
    back, back_in, back_sum, back_code, back_first, back_both,
    z, core_sum, row_sum, resp_in,
    grad, grad_code, grad_in, part, part_in, whole, whole_code, whole_in,
    load_sem, send_sem, recv_sem,
):
    loads = [
        pltpu.make_async_copy(src, dst, load_sem.at[n])
        for n, (src, dst) in enumerate(((feat_hbm, feat_raw), (cot_hbm, cot_raw), (taps_hbm, taps)))
    ]
    for load in loads:
        load.start()
    gz = lax.axis_index("gz")
    gy = lax.axis_index("gy")
    af = lax.axis_index("af")
    py, px = gz // 4, gz % 4
    zh, core = af // 2, af % 2

    sibling = (gz, gy, zh * 2 + (1 - core))
    d_next, d_prev = (gz + 1) % 16, (gz + 15) % 16
    side = 1 - gy

    def along_x(k, row=gy):
        return (py * 4 + (px + k) % 4, row, af)

    def along_y(k, row=gy):
        return (((py + k) % 4) * 4 + px, row, af)

    def along_z(k):
        return (gz, gy, ((zh + k) % 4) * 2 + core)

    groups = []

    class Group:
        def __init__(self, size):
            self.index, self.size = len(groups), size
            groups.append(self)

        def send(self, src, dst, device):
            pltpu.make_async_remote_copy(
                src_ref=src, dst_ref=dst,
                send_sem=send_sem.at[self.index], recv_sem=recv_sem.at[self.index],
                device_id=device, device_id_type=MESH,
            ).start()
            return self

        def wait_recv(self):
            pltpu.make_async_copy(self.size, self.size, recv_sem.at[self.index]).wait()

        def wait_send(self):
            pltpu.make_async_copy(self.size, self.size, send_sem.at[self.index]).wait()

    partners = [sibling, (d_next, gy, af), (d_prev, gy, af)]
    partners += [(d_next, side, af), (d_prev, side, af), (gz, side, af)]
    partners += [along_z(1), along_z(3)]
    for k in (1, 2, 3):
        for along in (along_x, along_y):
            partners += [along(k), along(k, side)]
    barrier = pltpu.get_barrier_semaphore()
    for partner in partners:
        pl.semaphore_signal(barrier, inc=1, device_id=partner, device_id_type=MESH)

    def lay_flat(n, raw, flat):
        loads[n].wait()
        for d in (0, 1):
            flat[:, pl.ds(d * PLANE, PLANE)] = raw[:, d, :]

    lay_flat(0, feat_raw, feat)
    pl.semaphore_wait(barrier, len(partners))

    def block(channels_of):
        return field.at[aligned(channels_of * OWN, OWN, OWN)]

    pair = 1 + 2 * (zh % 2)
    other = 4 - pair
    far = 2

    def owner(k):
        return ((zh + k) % 4) * 2 + core

    def pass_on(rows, device):
        return Group(rows).send(rows, rows, device)

    def half_block(k, start):
        return field.at[aligned(owner(k) * OWN + start, 16, 16)]

    from_pair = Group(block(af)).send(feat, block(af), along_z(pair))
    from_other = Group(block(af)).send(feat, block(af), along_z(other))
    from_sibling = Group(block(af)).send(feat, block(af), sibling)
    lay_flat(1, cot_raw, cot)

    edge = (1 - gy) * (PLANE - 128)
    low_edge = cot.at[:, aligned(edge, 128, 128)]
    high_edge = cot.at[:, aligned(edge + PLANE, 128, 128)]

    def halo(n):
        return cot_halo.at[:, pl.ds(2 * PLANE + n * 128, 128)]

    halos = Group(cot_halo)
    halos.send(low_edge, halo(3), (d_prev, side, af))
    halos.send(high_edge, halo(0), (d_next, side, af))
    halos.send(cot.at[:, pl.ds(0, PLANE)], cot_halo.at[:, pl.ds(PLANE, PLANE)], (d_prev, gy, af))
    halos.send(cot.at[:, pl.ds(PLANE, PLANE)], cot_halo.at[:, pl.ds(0, PLANE)], (d_next, gy, af))
    halos.send(low_edge, halo(1), (gz, side, af))
    halos.send(high_edge, halo(2), (gz, side, af))
    block(af)[...] = feat[...]
    loads[2].wait()
    taps_t[...] = taps[...].T

    from_pair.wait_recv()
    far_by_other = pass_on(half_block(pair, 0), along_z(other))
    pair_relay = pass_on(block(owner(pair)), sibling)

    halos.wait_recv()
    lane = lax.broadcasted_iota(jnp.int32, (OWN, PLANE + 128), 1)
    column = lane % WIDTH
    slab_lane = lax.broadcasted_iota(jnp.int32, (OWN, 128), 1)
    row_side = (slab_lane < WIDTH) == (gy == 0)
    inside = (gz > 0, None, None, gz < 15)
    for e in range(4):
        if e in (1, 2):
            plane = cot[:, pl.ds((e - 1) * PLANE, PLANE)].astype(F32)
        else:
            plane = cot_halo[:, pl.ds((e // 3) * PLANE, PLANE)].astype(F32)
        rows = jnp.where(row_side, halo(e)[...].astype(F32), 0.0)
        base = jnp.concatenate([plane, rows], axis=1)
        if inside[e] is not None:
            base = jnp.where(inside[e], base, 0.0)
        for c in (-1, 0, 1):
            if c == 0:
                moved = base
            else:
                moved = jnp.where(column == (0 if c == 1 else WIDTH - 1), 0.0, roll(base, c))
            tall = roll(moved, WIDTH).astype(BF16)
            moved = moved.astype(BF16)
            for a in (-1, 0, 1):
                d = e - 1 + a
                if d not in (0, 1):
                    continue
                for b in (-1, 0, 1):
                    piece = {-1: tall[:, 128:], 0: moved[:, :PLANE], 1: tall[:, :PLANE]}[b]
                    cim[pl.ds(tap_index(a, b, c) * OWN, OWN), pl.ds(d * PLANE, PLANE)] = piece

    near_lanes = (zh // 2) * 128

    def channels(half):
        return near_lanes if half == 0 else 128 - near_lanes

    def filter_products(half):
        grad[half, pl.ds(0, ROWS)] = lax.dot_general(
            cim[...], field[aligned(channels(half), 128, 128)],
            (((1,), (1,)), ((), ())), preferred_element_type=F32,
        )
        grad[half, pl.ds(ROWS, PADDED - ROWS)] = jnp.zeros((PADDED - ROWS, 128), F32)

    orders = ((px, along_x, py, along_y), (py, along_y, px, along_x))

    def unit_rows(r, i):
        return aligned(r * 4 * CHUNK + i * CHUNK, CHUNK, 16)

    def scatter(half):
        for r, (pos, along, _, _) in enumerate(orders):
            u = half * 2 + r
            sent = Group(grad_in.at[u])
            for k in (2, 1, 3):
                code = grad_code.at[u, k - 1]
                put_rows(code, grad[half, unit_rows(r, (pos + k) % 4)])
                sent.send(code, grad_in.at[u, k - 1], along(k))
            scattered[u] = sent

    def eight(pos, along):
        others = []
        for step in (5, 4, 3, 2, 7, 6, 1):
            k, row = step // 2, gy if step % 2 == 0 else side
            others.append((step - 1, along(k, row), ((pos + k) % 4) * 2 + row))
        return pos * 2 + gy, others

    def scatter_again(half):
        for r, (pos, _, pos2, along2) in enumerate(orders):
            u = half * 2 + r
            scattered[u].wait_recv()
            total = grad[half, unit_rows(r, pos)]
            for n in range(3):
                total = total + get_rows(grad_in.at[u, n])
            part[u, pl.ds(0, CHUNK)] = total
            part[u, pl.ds(CHUNK, 16)] = jnp.zeros((16, 128), F32)
            sent = Group(part_in.at[u])
            for n, device, there in eight(pos2, along2)[1]:
                sent.send(part.at[u, aligned(there * 16, 16, 16)], part_in.at[u, n], device)
            scattered_again[u] = sent

    def gather(half):
        for r, (_, _, pos2, along2) in enumerate(orders):
            u = half * 2 + r
            mine, others = eight(pos2, along2)
            rows = aligned(mine * 16, 16, 16)
            scattered_again[u].wait_recv()
            total = part[u, rows]
            for n in range(7):
                total = total + part_in[u, n]
            whole[u, rows] = total * (1.0 / math.sqrt(32768.0))
            sent = Group(part_in.at[u])
            for _, device, _ in others:
                sent.send(whole.at[u, rows], whole.at[u, rows], device)
            gathered[u] = sent

    def gather_again(half):
        lanes = aligned(channels(half), 128, 128)
        for r, (pos, along, _, _) in enumerate(orders):
            u = half * 2 + r
            gathered[u].wait_recv()
            code = whole_code.at[u]
            put_rows(code, whole[u, pl.ds(0, CHUNK)])
            sent = Group(whole_in.at[u])
            for k in (2, 1, 3):
                sent.send(code, whole_in.at[u, k - 1], along(k))
            grad_out[unit_rows(r, pos), lanes] = get_rows(code)
            gathered_again[u] = sent

    def finish(half):
        lanes = aligned(channels(half), 128, 128)
        for r, (pos, _, _, _) in enumerate(orders):
            u = half * 2 + r
            gathered_again[u].wait_recv()

            @pl.loop(0, 3)
            def _(n):
                grad_out[unit_rows(r, (pos + 3 - n) % 4), lanes] = get_rows(whole_in.at[u, n])

    scattered, scattered_again, gathered, gathered_again = {}, {}, {}, {}

    from_other.wait_recv()
    far_by_pair = pass_on(half_block(other, 16), along_z(pair))
    other_relay = pass_on(block(owner(other)), sibling)
    from_sibling.wait_recv()
    pair_relay.wait_recv()
    filter_products(0)
    scatter(0)

    @pl.loop(0, 4)
    def _(n):
        cols = aligned(n * 256, 256, 256)
        back[:, cols] = lax.dot_general(
            taps_t[...], cim[:, cols], (((1,), (0,)), ((), ())), preferred_element_type=F32
        )

    to_sibling = Group(back_in)
    for k in range(4):
        to_sibling.send(back.at[aligned((2 * k + 1 - core) * OWN, OWN, OWN)], back_in.at[k], sibling)

    to_sibling.wait_recv()
    for k in range(4):
        back_sum[k] = back[aligned((2 * k + core) * OWN, OWN, OWN)] + back_in[k]

    ring = Ring(Group, back_sum, zh, along_z(1), along_z(3), back_code, back_first, back_both)
    ring.start()

    far_by_other.wait_recv()
    far_by_pair.wait_recv()
    far_relay = pass_on(block(owner(far)), sibling)
    other_relay.wait_recv()
    far_relay.wait_recv()
    filter_products(1)
    scatter(1)

    scatter_again(0)

    scatter_again(1)

    gather(0)
    ring.middle()

    @pl.loop(0, 4)
    def _(n):
        cols = aligned(n * 256, 256, 256)
        z[:, cols] = jnp.dot(taps[...], field[:, cols], preferred_element_type=F32)

    gather(1)
    plane_lane = lane[:, :PLANE]
    plane_column = column[:, :PLANE]
    for e in range(4):
        rows_of = []
        for b in (-1, 0, 1):
            total = None
            for c in (-1, 0, 1):
                term = None
                for a in (-1, 0, 1):
                    d = e - 1 + a
                    if d in (0, 1):
                        value = z[pl.ds(tap_index(a, b, c) * OWN, OWN), pl.ds(d * PLANE, PLANE)]
                        term = value if term is None else term + value
                if c:
                    out = WIDTH - 1 if c == 1 else 0
                    term = jnp.where(plane_column == out, 0.0, roll(term, -c))
                total = term if total is None else total + term
            rows_of.append(roll(total, -b * WIDTH) if b else total)
        before, centre, after = rows_of
        core_sum[e] = (
            centre
            + jnp.where(plane_lane < PLANE - WIDTH, after, 0.0)
            + jnp.where(plane_lane >= WIDTH, before, 0.0)
        )
        outward = jnp.where(gy == 0, before[:, :128], after[:, PLANE - 128:])
        row_sum[e] = jnp.where(row_side, outward, 0.0)

    def resp_row(n):
        return resp_in.at[:, pl.ds(2 * PLANE + n * 128, 128)]

    outer = Group(resp_in)
    outer.send(core_sum.at[0], resp_in.at[:, pl.ds(PLANE, PLANE)], (d_prev, gy, af))
    outer.send(core_sum.at[3], resp_in.at[:, pl.ds(0, PLANE)], (d_next, gy, af))
    outer.send(row_sum.at[1], resp_row(0), (gz, side, af))
    outer.send(row_sum.at[2], resp_row(1), (gz, side, af))
    outer.send(row_sum.at[0], resp_row(3), (d_prev, side, af))
    outer.send(row_sum.at[3], resp_row(2), (d_next, side, af))

    gather_again(0)
    gather_again(1)
    outer.wait_recv()
    for d, valid in ((0, gz > 0), (1, gz < 15)):
        total = core_sum[d + 1] + jnp.where(valid, resp_in[:, pl.ds(d * PLANE, PLANE)], 0.0)
        slab = resp_row(d)[...] + jnp.where(valid, resp_row(2 + d)[...], 0.0)
        slab = jnp.concatenate(
            [
                jnp.where(gy == 1, slab, 0.0),
                jnp.zeros((OWN, PLANE - 256), F32),
                jnp.where(gy == 0, slab, 0.0),
            ],
            axis=1,
        )
        resp_out[:, d, :] = (total + slab).astype(BF16)

    for half, total in enumerate(ring.end()):
        for d in (0, 1):
            back_out[pl.ds(half * 16, 16), d, :] = total[:, d * PLANE:(d + 1) * PLANE].astype(BF16)
    finish(0)
    finish(1)
    for group in groups:
        group.wait_send()


def shards(features, filters, cotangent):
    vmem = pl.BlockSpec(memory_space=pltpu.VMEM)
    resp, back, grad = pl.pallas_call(
        kernel,
        out_shape=(
            pltpu.VMEM((OWN, 2, PLANE), BF16),
            pltpu.VMEM((OWN, 2, PLANE), BF16),
            pltpu.VMEM((PADDED, C), F32),
        ),
        in_specs=[pl.BlockSpec(memory_space=pl.ANY)] * 3,
        out_specs=(vmem,) * 3,
        scratch_shapes=[
            pltpu.VMEM((OWN, 2, PLANE), BF16),
            pltpu.VMEM((OWN, 2, PLANE), BF16),
            pltpu.VMEM((ROWS, C), BF16),
            pltpu.VMEM((C, ROWS), BF16),
            pltpu.VMEM((OWN, CELLS), BF16),
            pltpu.VMEM((OWN, CELLS), BF16),
            pltpu.VMEM((C, CELLS), BF16),
            pltpu.VMEM((OWN, 2 * PLANE + 4 * 128), BF16),
            pltpu.VMEM((ROWS, CELLS), BF16),
            pltpu.VMEM((C, CELLS), F32),
            pltpu.VMEM((4, OWN, CELLS), F32),
            pltpu.VMEM((4, OWN, CELLS), F32),
            pltpu.VMEM((6, 16, CELLS + 128), BF16),
            pltpu.VMEM((2, 16, CELLS + 128), BF16),
            pltpu.VMEM((2, 2, 16, CELLS + 128), BF16),
            pltpu.VMEM((ROWS, CELLS), F32),
            pltpu.VMEM((4, OWN, PLANE), F32),
            pltpu.VMEM((4, OWN, 128), F32),
            pltpu.VMEM((OWN, 2 * PLANE + 4 * 128), F32),
            pltpu.VMEM((2, PADDED, 128), F32),
            pltpu.VMEM((4, 3, CHUNK + 16, 128), BF16),
            pltpu.VMEM((4, 3, CHUNK + 16, 128), BF16),
            pltpu.VMEM((4, CHUNK + 16, 128), F32),
            pltpu.VMEM((4, 7, 16, 128), F32),
            pltpu.VMEM((4, CHUNK + 16, 128), F32),
            pltpu.VMEM((4, CHUNK + 16, 128), BF16),
            pltpu.VMEM((4, 3, CHUNK + 16, 128), BF16),
            pltpu.SemaphoreType.DMA((3,)),
            pltpu.SemaphoreType.DMA((N_GROUPS,)),
            pltpu.SemaphoreType.DMA((N_GROUPS,)),
        ],
        compiler_params=pltpu.CompilerParams(
            collective_id=0, has_side_effects=True, vmem_limit_bytes=60 * 1024 * 1024
        ),
    )(
        features,
        cotangent,
        filters.reshape(ROWS, C),
    )
    return resp, back, grad[:ROWS].reshape(filters.shape)


def solution(mesh):
    placed = (P("af", "gz", "gy"), P(None, None, None, "af", None), P("af", "gz", "gy"))
    return jax.shard_map(
        shards,
        mesh=mesh,
        in_specs=placed,
        out_specs=(P("af", "gz", "gy"), P("af", "gz", "gy"), P(None, None, None, "af", None)),
        check_vma=False,
    )
```

```python
import functools
import math

import jax
import jax.numpy as jnp
from jax import lax
from jax.experimental import pallas as pl
from jax.experimental.pallas import tpu as pltpu
from jax.sharding import PartitionSpec as P

MESH = pl.DeviceIdType.MESH
F32 = jnp.float32
BF16 = jnp.bfloat16
WIDTH = 64
PLANE = 512
CELLS = 1024
OWN = 32
C = 256
TAPS = 27
ROWS = TAPS * OWN
PADDED = 896
CHUNK = PADDED // 8
SUB = CHUNK // 8
N_GROUPS = 31


def tap_index(a, b, c):
    return ((a + 1) * 3 + (b + 1)) * 3 + (c + 1)


def roll(x, shift):
    return pltpu.roll(x, shift % x.shape[1], 1)


def aligned(start, size, unit):
    return pl.ds(pl.multiple_of(start, unit), size)


def encode(blocks):
    top = functools.reduce(jnp.maximum, [jnp.abs(block) for block in blocks])
    scale = jnp.maximum(top * 2.0**-7.75, 1e-30).astype(BF16)
    inverse = 1.0 / scale.astype(F32)
    codes = []
    for block in blocks:
        power = block * inverse
        for _ in range(4):
            power = power * power
        codes.append(jnp.where(block < 0, -power, power).astype(BF16))
    return codes, scale


def decode(codes, scale):
    scale = scale.astype(F32)
    blocks = []
    for code in codes:
        code = code.astype(F32)
        root = jnp.maximum(jnp.abs(code), 2e-38)
        for _ in range(4):
            root = lax.rsqrt(root)
        root = jnp.where(code == 0, 0.0, root * scale)
        blocks.append(jnp.where(code < 0, -root, root))
    return blocks


def put_rows(ref, value):
    codes, scale = encode([value[i:i + 16] for i in range(0, CHUNK, 16)])
    ref[pl.ds(0, CHUNK)] = jnp.concatenate(codes, axis=0)
    ref[pl.ds(CHUNK, 16)] = scale


def get_rows(ref):
    codes = [ref[pl.ds(i, 16)] for i in range(0, CHUNK, 16)]
    return jnp.concatenate(decode(codes, ref[pl.ds(CHUNK, 16)]), axis=0)


def encode_sub(value):
    valid = lax.broadcasted_iota(jnp.int32, value.shape, 0) < SUB
    top = jnp.max(jnp.where(valid, jnp.abs(value), 0.0), axis=0, keepdims=True)
    scale = jnp.maximum(jnp.broadcast_to(top, value.shape) * 2.0**-7.75, 1e-30)
    scale = scale.astype(BF16).astype(F32)
    power = value * (1.0 / scale)
    for _ in range(4):
        power = power * power
    return jnp.where(valid, jnp.where(value < 0, -power, power), scale).astype(BF16)


def decode_sub(code):
    scale = jnp.broadcast_to(code.astype(F32)[SUB:SUB + 1], code.shape)
    return decode([code], scale)[0]


def get_subs(ref, rows):
    for j in range(8):
        rows[pl.ds(j * SUB, 16)] = decode_sub(ref[j])
    return rows[pl.ds(0, CHUNK)]


def put_columns(ref, value):
    codes, scale = encode([value[:, i:i + 128] for i in range(0, CELLS, 128)])
    ref[:, pl.ds(0, CELLS)] = jnp.concatenate(codes, axis=1)
    ref[:, pl.ds(CELLS, 128)] = scale


def get_columns(ref):
    codes = [ref[:, pl.ds(i, 128)] for i in range(0, CELLS, 128)]
    return jnp.concatenate(decode(codes, ref[:, pl.ds(CELLS, 128)]), axis=1)


class Ring:
    def __init__(self, group, chunks, pos, nxt, prv, out, first, both):
        self.group, self.chunks, self.pos, self.nxt, self.prv = group, chunks, pos, nxt, prv
        self.out, self.first, self.both = out, first, both

    def part(self, k, half):
        return self.chunks[(self.pos + k) % 4, pl.ds(half * 16, 16)]

    def start(self):
        self.early, self.late = self.group(self.first), self.group(self.both)
        put_columns(self.out.at[0], self.part(2, 0))
        self.early.send(self.out.at[0], self.first.at[0], self.nxt)
        put_columns(self.out.at[1], self.part(2, 1))
        self.early.send(self.out.at[1], self.first.at[1], self.prv)
        put_columns(self.out.at[2], self.part(1, 1))
        self.late.send(self.out.at[2], self.both.at[0, 1], self.nxt)
        put_columns(self.out.at[3], self.part(3, 0))
        self.late.send(self.out.at[3], self.both.at[1, 0], self.prv)

    def middle(self):
        self.early.wait_recv()
        put_columns(self.out.at[4], self.part(1, 0) + get_columns(self.first.at[0]))
        self.late.send(self.out.at[4], self.both.at[0, 0], self.nxt)
        put_columns(self.out.at[5], self.part(3, 1) + get_columns(self.first.at[1]))
        self.late.send(self.out.at[5], self.both.at[1, 1], self.prv)

    def end(self):
        self.late.wait_recv()
        return [
            self.part(0, half) + get_columns(self.both.at[0, half]) + get_columns(self.both.at[1, half])
            for half in (0, 1)
        ]


def kernel(
    feat_hbm, cot_hbm, taps_hbm, resp_out, back_out, grad_out,
    feat_raw, cot_raw, taps, taps_t, feat, cot, field, cot_halo, cim,
    back, back_in, back_sum, back_code, back_first, back_both,
    z, core_sum, row_sum, resp_in,
    grad, grad_code, grad_in, part, part_code, part_in, rows_here, whole_code, whole_in,
    load_sem, send_sem, recv_sem,
):
    loads = [
        pltpu.make_async_copy(src, dst, load_sem.at[n])
        for n, (src, dst) in enumerate(((feat_hbm, feat_raw), (cot_hbm, cot_raw), (taps_hbm, taps)))
    ]
    for load in loads:
        load.start()
    gz = lax.axis_index("gz")
    gy = lax.axis_index("gy")
    af = lax.axis_index("af")
    py, px = gz // 4, gz % 4
    zh, core = af // 2, af % 2

    sibling = (gz, gy, zh * 2 + (1 - core))
    d_next, d_prev = (gz + 1) % 16, (gz + 15) % 16
    side = 1 - gy

    def along_x(k, row=gy):
        return (py * 4 + (px + k) % 4, row, af)

    def along_y(k, row=gy):
        return (((py + k) % 4) * 4 + px, row, af)

    def along_z(k):
        return (gz, gy, ((zh + k) % 4) * 2 + core)

    groups = []

    class Group:
        def __init__(self, size):
            self.index, self.size = len(groups), size
            groups.append(self)

        def send(self, src, dst, device):
            pltpu.make_async_remote_copy(
                src_ref=src, dst_ref=dst,
                send_sem=send_sem.at[self.index], recv_sem=recv_sem.at[self.index],
                device_id=device, device_id_type=MESH,
            ).start()
            return self

        def wait_recv(self):
            pltpu.make_async_copy(self.size, self.size, recv_sem.at[self.index]).wait()

        def wait_send(self):
            pltpu.make_async_copy(self.size, self.size, send_sem.at[self.index]).wait()

    partners = [sibling, (d_next, gy, af), (d_prev, gy, af)]
    partners += [(d_next, side, af), (d_prev, side, af), (gz, side, af)]
    partners += [along_z(1), along_z(3)]
    for k in (1, 2, 3):
        for along in (along_x, along_y):
            partners += [along(k), along(k, side)]
    barrier = pltpu.get_barrier_semaphore()
    for partner in partners:
        pl.semaphore_signal(barrier, inc=1, device_id=partner, device_id_type=MESH)

    def lay_flat(n, raw, flat):
        loads[n].wait()
        for d in (0, 1):
            flat[:, pl.ds(d * PLANE, PLANE)] = raw[:, d, :]

    lay_flat(0, feat_raw, feat)
    pl.semaphore_wait(barrier, len(partners))

    def block(channels_of):
        return field.at[aligned(channels_of * OWN, OWN, OWN)]

    pair = 1 + 2 * (zh % 2)
    other = 4 - pair
    far = 2

    def owner(k):
        return ((zh + k) % 4) * 2 + core

    def pass_on(rows, device):
        return Group(rows).send(rows, rows, device)

    def half_block(k, start):
        return field.at[aligned(owner(k) * OWN + start, 16, 16)]

    low, high = feat.at[pl.ds(0, 16)], feat.at[pl.ds(16, 16)]
    low_here, high_here = half_block(0, 0), half_block(0, 16)
    pair_low = Group(low).send(low, low_here, along_z(pair))
    other_high = Group(high).send(high, high_here, along_z(other))
    pair_high = Group(high).send(high, high_here, along_z(pair))
    other_low = Group(low).send(low, low_here, along_z(other))
    from_sibling = Group(block(af)).send(feat, block(af), sibling)
    lay_flat(1, cot_raw, cot)

    edge = (1 - gy) * (PLANE - 128)
    low_edge = cot.at[:, aligned(edge, 128, 128)]
    high_edge = cot.at[:, aligned(edge + PLANE, 128, 128)]

    def halo(n):
        return cot_halo.at[:, pl.ds(2 * PLANE + n * 128, 128)]

    halos = Group(cot_halo)
    halos.send(low_edge, halo(3), (d_prev, side, af))
    halos.send(high_edge, halo(0), (d_next, side, af))
    halos.send(cot.at[:, pl.ds(0, PLANE)], cot_halo.at[:, pl.ds(PLANE, PLANE)], (d_prev, gy, af))
    halos.send(cot.at[:, pl.ds(PLANE, PLANE)], cot_halo.at[:, pl.ds(0, PLANE)], (d_next, gy, af))
    halos.send(low_edge, halo(1), (gz, side, af))
    halos.send(high_edge, halo(2), (gz, side, af))
    block(af)[...] = feat[...]
    loads[2].wait()
    taps_t[...] = taps[...].T

    pair_low.wait_recv()
    far_by_other = pass_on(half_block(pair, 0), along_z(other))
    other_high.wait_recv()
    far_by_pair = pass_on(half_block(other, 16), along_z(pair))
    pair_high.wait_recv()
    pair_relay = pass_on(block(owner(pair)), sibling)

    halos.wait_recv()
    lane = lax.broadcasted_iota(jnp.int32, (OWN, PLANE + 128), 1)
    column = lane % WIDTH
    slab_lane = lax.broadcasted_iota(jnp.int32, (OWN, 128), 1)
    row_side = (slab_lane < WIDTH) == (gy == 0)
    inside = (gz > 0, None, None, gz < 15)
    for e in range(4):
        if e in (1, 2):
            plane = cot[:, pl.ds((e - 1) * PLANE, PLANE)].astype(F32)
        else:
            plane = cot_halo[:, pl.ds((e // 3) * PLANE, PLANE)].astype(F32)
        rows = jnp.where(row_side, halo(e)[...].astype(F32), 0.0)
        base = jnp.concatenate([plane, rows], axis=1)
        if inside[e] is not None:
            base = jnp.where(inside[e], base, 0.0)
        for c in (-1, 0, 1):
            if c == 0:
                moved = base
            else:
                moved = jnp.where(column == (0 if c == 1 else WIDTH - 1), 0.0, roll(base, c))
            tall = roll(moved, WIDTH).astype(BF16)
            moved = moved.astype(BF16)
            for a in (-1, 0, 1):
                d = e - 1 + a
                if d not in (0, 1):
                    continue
                for b in (-1, 0, 1):
                    piece = {-1: tall[:, 128:], 0: moved[:, :PLANE], 1: tall[:, :PLANE]}[b]
                    cim[pl.ds(tap_index(a, b, c) * OWN, OWN), pl.ds(d * PLANE, PLANE)] = piece

    near_lanes = (zh // 2) * 128

    def channels(half):
        return near_lanes if half == 0 else 128 - near_lanes

    def filter_products(half):
        grad[half, pl.ds(0, ROWS)] = lax.dot_general(
            cim[...], field[aligned(channels(half), 128, 128)],
            (((1,), (1,)), ((), ())), preferred_element_type=F32,
        )
        grad[half, pl.ds(ROWS, PADDED - ROWS)] = jnp.zeros((PADDED - ROWS, 128), F32)

    orders = ((px, along_x, py, along_y), (py, along_y, px, along_x))

    def unit_rows(r, i):
        return aligned(r * 4 * CHUNK + i * CHUNK, CHUNK, 16)

    def scatter(half):
        for r, (pos, along, _, _) in enumerate(orders):
            u = half * 2 + r
            sent = Group(grad_in.at[u])
            for k in (2, 1, 3):
                code = grad_code.at[u, k - 1]
                put_rows(code, grad[half, unit_rows(r, (pos + k) % 4)])
                sent.send(code, grad_in.at[u, k - 1], along(k))
            scattered[u] = sent

    def eight(pos, along):
        others = []
        for step in (5, 4, 3, 2, 7, 6, 1):
            k, row = step // 2, gy if step % 2 == 0 else side
            others.append((step - 1, along(k, row), ((pos + k) % 4) * 2 + row))
        return pos * 2 + gy, others

    def scatter_again(half):
        for r, (pos, _, pos2, along2) in enumerate(orders):
            u = half * 2 + r
            scattered[u].wait_recv()
            total = grad[half, unit_rows(r, pos)]
            for n in range(3):
                total = total + get_rows(grad_in.at[u, n])
            total = jnp.concatenate([total, jnp.zeros((8, 128), F32)], axis=0)
            for j in range(8):
                value = total[j * SUB:j * SUB + 16]
                part[u, j] = value
                part_code[u, j] = encode_sub(value)
            sent = Group(part_in.at[u])
            for n, device, there in eight(pos2, along2)[1]:
                sent.send(part_code.at[u, there], part_in.at[u, n], device)
            scattered_again[u] = sent

    def gather(half):
        for r, (_, _, pos2, along2) in enumerate(orders):
            u = half * 2 + r
            mine, others = eight(pos2, along2)
            scattered_again[u].wait_recv()
            total = part[u, mine]
            for n in range(7):
                total = total + decode_sub(part_in[u, n])
            whole_code[u, mine] = encode_sub(total * (1.0 / math.sqrt(32768.0)))
            sent = Group(part_in.at[u])
            for _, device, _ in others:
                sent.send(whole_code.at[u, mine], whole_code.at[u, mine], device)
            gathered[u] = sent

    def gather_again(half):
        lanes = aligned(channels(half), 128, 128)
        for r, (pos, along, _, _) in enumerate(orders):
            u = half * 2 + r
            gathered[u].wait_recv()
            sent = Group(whole_in.at[u])
            for k in (2, 1, 3):
                sent.send(whole_code.at[u], whole_in.at[u, k - 1], along(k))
            gathered_again[u] = sent
        for r, (pos, along, _, _) in enumerate(orders):
            grad_out[unit_rows(r, pos), lanes] = get_subs(whole_code.at[half * 2 + r], rows_here)

    def finish(half):
        lanes = aligned(channels(half), 128, 128)
        for r, (pos, _, _, _) in enumerate(orders):
            u = half * 2 + r
            gathered_again[u].wait_recv()
            for n in range(3):
                grad_out[unit_rows(r, (pos + 3 - n) % 4), lanes] = get_subs(whole_in.at[u, n], rows_here)

    scattered, scattered_again, gathered, gathered_again = {}, {}, {}, {}

    other_low.wait_recv()
    other_relay = pass_on(block(owner(other)), sibling)
    from_sibling.wait_recv()
    pair_relay.wait_recv()
    filter_products(0)
    scatter(0)

    @pl.loop(0, 4)
    def _(n):
        cols = aligned(n * 256, 256, 256)
        back[:, cols] = lax.dot_general(
            taps_t[...], cim[:, cols], (((1,), (0,)), ((), ())), preferred_element_type=F32
        )

    to_sibling = Group(back_in)
    for k in range(4):
        to_sibling.send(back.at[aligned((2 * k + 1 - core) * OWN, OWN, OWN)], back_in.at[k], sibling)

    to_sibling.wait_recv()
    for k in range(4):
        back_sum[k] = back[aligned((2 * k + core) * OWN, OWN, OWN)] + back_in[k]

    ring = Ring(Group, back_sum, zh, along_z(1), along_z(3), back_code, back_first, back_both)
    ring.start()

    far_by_other.wait_recv()
    far_by_pair.wait_recv()
    far_relay = pass_on(block(owner(far)), sibling)
    other_relay.wait_recv()
    far_relay.wait_recv()
    filter_products(1)
    scatter(1)

    scatter_again(0)

    scatter_again(1)

    gather(0)
    ring.middle()

    @pl.loop(0, 4)
    def _(n):
        cols = aligned(n * 256, 256, 256)
        z[:, cols] = jnp.dot(taps[...], field[:, cols], preferred_element_type=F32)

    gather(1)
    plane_lane = lane[:, :PLANE]
    plane_column = column[:, :PLANE]
    for e in range(4):
        rows_of = []
        for b in (-1, 0, 1):
            total = None
            for c in (-1, 0, 1):
                term = None
                for a in (-1, 0, 1):
                    d = e - 1 + a
                    if d in (0, 1):
                        value = z[pl.ds(tap_index(a, b, c) * OWN, OWN), pl.ds(d * PLANE, PLANE)]
                        term = value if term is None else term + value
                if c:
                    out = WIDTH - 1 if c == 1 else 0
                    term = jnp.where(plane_column == out, 0.0, roll(term, -c))
                total = term if total is None else total + term
            rows_of.append(roll(total, -b * WIDTH) if b else total)
        before, centre, after = rows_of
        core_sum[e] = (
            centre
            + jnp.where(plane_lane < PLANE - WIDTH, after, 0.0)
            + jnp.where(plane_lane >= WIDTH, before, 0.0)
        )
        outward = jnp.where(gy == 0, before[:, :128], after[:, PLANE - 128:])
        row_sum[e] = jnp.where(row_side, outward, 0.0)

    def resp_row(n):
        return resp_in.at[:, pl.ds(2 * PLANE + n * 128, 128)]

    outer = Group(resp_in)
    outer.send(core_sum.at[0], resp_in.at[:, pl.ds(PLANE, PLANE)], (d_prev, gy, af))
    outer.send(core_sum.at[3], resp_in.at[:, pl.ds(0, PLANE)], (d_next, gy, af))
    outer.send(row_sum.at[1], resp_row(0), (gz, side, af))
    outer.send(row_sum.at[2], resp_row(1), (gz, side, af))
    outer.send(row_sum.at[0], resp_row(3), (d_prev, side, af))
    outer.send(row_sum.at[3], resp_row(2), (d_next, side, af))

    gather_again(0)
    gather_again(1)
    outer.wait_recv()
    for d, valid in ((0, gz > 0), (1, gz < 15)):
        total = core_sum[d + 1] + jnp.where(valid, resp_in[:, pl.ds(d * PLANE, PLANE)], 0.0)
        slab = resp_row(d)[...] + jnp.where(valid, resp_row(2 + d)[...], 0.0)
        slab = jnp.concatenate(
            [
                jnp.where(gy == 1, slab, 0.0),
                jnp.zeros((OWN, PLANE - 256), F32),
                jnp.where(gy == 0, slab, 0.0),
            ],
            axis=1,
        )
        resp_out[:, d, :] = (total + slab).astype(BF16)

    for half, total in enumerate(ring.end()):
        for d in (0, 1):
            back_out[pl.ds(half * 16, 16), d, :] = total[:, d * PLANE:(d + 1) * PLANE].astype(BF16)
    finish(0)
    finish(1)
    for group in groups:
        group.wait_send()


def shards(features, filters, cotangent):
    vmem = pl.BlockSpec(memory_space=pltpu.VMEM)
    resp, back, grad = pl.pallas_call(
        kernel,
        out_shape=(
            pltpu.VMEM((OWN, 2, PLANE), BF16),
            pltpu.VMEM((OWN, 2, PLANE), BF16),
            pltpu.VMEM((PADDED, C), F32),
        ),
        in_specs=[pl.BlockSpec(memory_space=pl.ANY)] * 3,
        out_specs=(vmem,) * 3,
        scratch_shapes=[
            pltpu.VMEM((OWN, 2, PLANE), BF16),
            pltpu.VMEM((OWN, 2, PLANE), BF16),
            pltpu.VMEM((ROWS, C), BF16),
            pltpu.VMEM((C, ROWS), BF16),
            pltpu.VMEM((OWN, CELLS), BF16),
            pltpu.VMEM((OWN, CELLS), BF16),
            pltpu.VMEM((C, CELLS), BF16),
            pltpu.VMEM((OWN, 2 * PLANE + 4 * 128), BF16),
            pltpu.VMEM((ROWS, CELLS), BF16),
            pltpu.VMEM((C, CELLS), F32),
            pltpu.VMEM((4, OWN, CELLS), F32),
            pltpu.VMEM((4, OWN, CELLS), F32),
            pltpu.VMEM((6, 16, CELLS + 128), BF16),
            pltpu.VMEM((2, 16, CELLS + 128), BF16),
            pltpu.VMEM((2, 2, 16, CELLS + 128), BF16),
            pltpu.VMEM((ROWS, CELLS), F32),
            pltpu.VMEM((4, OWN, PLANE), F32),
            pltpu.VMEM((4, OWN, 128), F32),
            pltpu.VMEM((OWN, 2 * PLANE + 4 * 128), F32),
            pltpu.VMEM((2, PADDED, 128), F32),
            pltpu.VMEM((4, 3, CHUNK + 16, 128), BF16),
            pltpu.VMEM((4, 3, CHUNK + 16, 128), BF16),
            pltpu.VMEM((4, 8, 16, 128), F32),
            pltpu.VMEM((4, 8, 16, 128), BF16),
            pltpu.VMEM((4, 7, 16, 128), BF16),
            pltpu.VMEM((CHUNK + 16, 128), F32),
            pltpu.VMEM((4, 8, 16, 128), BF16),
            pltpu.VMEM((4, 3, 8, 16, 128), BF16),
            pltpu.SemaphoreType.DMA((3,)),
            pltpu.SemaphoreType.DMA((N_GROUPS,)),
            pltpu.SemaphoreType.DMA((N_GROUPS,)),
        ],
        compiler_params=pltpu.CompilerParams(
            collective_id=0, has_side_effects=True, vmem_limit_bytes=60 * 1024 * 1024
        ),
    )(
        features,
        cotangent,
        filters.reshape(ROWS, C),
    )
    return resp, back, grad[:ROWS].reshape(filters.shape)


def solution(mesh):
    placed = (P("af", "gz", "gy"), P(None, None, None, "af", None), P("af", "gz", "gy"))
    return jax.shard_map(
        shards,
        mesh=mesh,
        in_specs=placed,
        out_specs=(P("af", "gz", "gy"), P("af", "gz", "gy"), P(None, None, None, "af", None)),
        check_vma=False,
    )
```

```python
import functools
import math

import jax
import jax.numpy as jnp
from jax import lax
from jax.experimental import pallas as pl
from jax.experimental.pallas import tpu as pltpu
from jax.sharding import PartitionSpec as P

MESH = pl.DeviceIdType.MESH
F32 = jnp.float32
BF16 = jnp.bfloat16
WIDTH = 64
PLANE = 512
CELLS = 1024
OWN = 32
C = 256
TAPS = 27
ROWS = TAPS * OWN
PADDED = 896
CHUNK = PADDED // 8
SUB = CHUNK // 8
N_GROUPS = 35


def tap_index(a, b, c):
    return ((a + 1) * 3 + (b + 1)) * 3 + (c + 1)


def roll(x, shift):
    return pltpu.roll(x, shift % x.shape[1], 1)


def aligned(start, size, unit):
    return pl.ds(pl.multiple_of(start, unit), size)


def encode(blocks):
    top = functools.reduce(jnp.maximum, [jnp.abs(block) for block in blocks])
    scale = jnp.maximum(top * 2.0**-7.75, 1e-30).astype(BF16)
    inverse = 1.0 / scale.astype(F32)
    codes = []
    for block in blocks:
        power = block * inverse
        for _ in range(4):
            power = power * power
        codes.append(jnp.where(block < 0, -power, power).astype(BF16))
    return codes, scale


def decode(codes, scale):
    scale = scale.astype(F32)
    blocks = []
    for code in codes:
        code = code.astype(F32)
        root = jnp.maximum(jnp.abs(code), 2e-38)
        for _ in range(4):
            root = lax.rsqrt(root)
        root = jnp.where(code == 0, 0.0, root * scale)
        blocks.append(jnp.where(code < 0, -root, root))
    return blocks


def put_rows(ref, value):
    codes, scale = encode([value[i:i + 16] for i in range(0, CHUNK, 16)])
    ref[pl.ds(0, CHUNK)] = jnp.concatenate(codes, axis=0)
    ref[pl.ds(CHUNK, 16)] = scale


def get_rows(ref):
    codes = [ref[pl.ds(i, 16)] for i in range(0, CHUNK, 16)]
    return jnp.concatenate(decode(codes, ref[pl.ds(CHUNK, 16)]), axis=0)


def encode_sub(value):
    valid = lax.broadcasted_iota(jnp.int32, value.shape, 0) < SUB
    top = jnp.max(jnp.where(valid, jnp.abs(value), 0.0), axis=0, keepdims=True)
    scale = jnp.maximum(jnp.broadcast_to(top, value.shape) * 2.0**-7.75, 1e-30)
    scale = scale.astype(BF16).astype(F32)
    power = value * (1.0 / scale)
    for _ in range(4):
        power = power * power
    return jnp.where(valid, jnp.where(value < 0, -power, power), scale).astype(BF16)


def decode_sub(code):
    scale = jnp.broadcast_to(code.astype(F32)[SUB:SUB + 1], code.shape)
    return decode([code], scale)[0]


def get_subs(ref, rows):
    for j in range(8):
        rows[pl.ds(j * SUB, 16)] = decode_sub(ref[j])
    return rows[pl.ds(0, CHUNK)]


def put_columns(ref, value):
    codes, scale = encode([value[:, i:i + 128] for i in range(0, CELLS, 128)])
    ref[:, pl.ds(0, CELLS)] = jnp.concatenate(codes, axis=1)
    ref[:, pl.ds(CELLS, 128)] = scale


def get_columns(ref):
    codes = [ref[:, pl.ds(i, 128)] for i in range(0, CELLS, 128)]
    return jnp.concatenate(decode(codes, ref[:, pl.ds(CELLS, 128)]), axis=1)


class Ring:
    def __init__(self, group, chunks, pos, nxt, prv, out, first, both):
        self.group, self.chunks, self.pos, self.nxt, self.prv = group, chunks, pos, nxt, prv
        self.out, self.first, self.both = out, first, both

    def part(self, k, half):
        return self.chunks[(self.pos + k) % 4, pl.ds(half * 16, 16)]

    def start(self):
        self.early, self.late = self.group(self.first), self.group(self.both)
        put_columns(self.out.at[0], self.part(2, 0))
        self.early.send(self.out.at[0], self.first.at[0], self.nxt)
        put_columns(self.out.at[1], self.part(2, 1))
        self.early.send(self.out.at[1], self.first.at[1], self.prv)
        put_columns(self.out.at[2], self.part(1, 1))
        self.late.send(self.out.at[2], self.both.at[0, 1], self.nxt)
        put_columns(self.out.at[3], self.part(3, 0))
        self.late.send(self.out.at[3], self.both.at[1, 0], self.prv)

    def middle(self):
        self.early.wait_recv()
        put_columns(self.out.at[4], self.part(1, 0) + get_columns(self.first.at[0]))
        self.late.send(self.out.at[4], self.both.at[0, 0], self.nxt)
        put_columns(self.out.at[5], self.part(3, 1) + get_columns(self.first.at[1]))
        self.late.send(self.out.at[5], self.both.at[1, 1], self.prv)

    def end(self):
        self.late.wait_recv()
        return [
            self.part(0, half) + get_columns(self.both.at[0, half]) + get_columns(self.both.at[1, half])
            for half in (0, 1)
        ]


def kernel(
    feat_hbm, cot_hbm, taps_hbm, resp_out, back_out, grad_out,
    feat_raw, cot_raw, taps, taps_t, feat, cot, field, cot_halo, cim,
    back, back_in, back_sum, back_code, back_first, back_both,
    z, core_sum, row_sum, resp_in,
    grad, grad_code, grad_in, part, part_code, part_in, rows_here, whole_code, whole_in,
    load_sem, send_sem, recv_sem,
):
    loads = [
        pltpu.make_async_copy(src, dst, load_sem.at[n])
        for n, (src, dst) in enumerate(((feat_hbm, feat_raw), (cot_hbm, cot_raw), (taps_hbm, taps)))
    ]
    for load in loads:
        load.start()
    gz = lax.axis_index("gz")
    gy = lax.axis_index("gy")
    af = lax.axis_index("af")
    py, px = gz // 4, gz % 4
    zh, core = af // 2, af % 2

    sibling = (gz, gy, zh * 2 + (1 - core))
    d_next, d_prev = (gz + 1) % 16, (gz + 15) % 16
    side = 1 - gy

    def along_x(k, row=gy, to=core):
        return (py * 4 + (px + k) % 4, row, zh * 2 + to)

    def along_y(k, row=gy, to=core):
        return (((py + k) % 4) * 4 + px, row, zh * 2 + to)

    def along_z(k, to=core):
        return (gz, gy, ((zh + k) % 4) * 2 + to)

    groups = []

    class Group:
        def __init__(self, size):
            self.index, self.size = len(groups), size
            groups.append(self)

        def send(self, src, dst, device, there=None):
            there = self.index if there is None else there
            pltpu.make_async_remote_copy(
                src_ref=src, dst_ref=dst,
                send_sem=send_sem.at[self.index], recv_sem=recv_sem.at[there],
                device_id=device, device_id_type=MESH,
            ).start()
            return self

        def wait_recv(self, size=None):
            size = self.size if size is None else size
            pltpu.make_async_copy(size, size, recv_sem.at[self.index]).wait()

        def wait_send(self):
            pltpu.make_async_copy(self.size, self.size, send_sem.at[self.index]).wait()

    partners = [sibling, (d_next, gy, af), (d_prev, gy, af)]
    partners += [(d_next, side, af), (d_prev, side, af), (gz, side, af)]
    for k in (1, 3):
        partners += [along_z(k), along_z(k, 1 - core)]
    for k in (1, 2, 3):
        for along in (along_x, along_y):
            partners += [along(k), along(k, side), along(k, gy, 1 - core)]
    barrier = pltpu.get_barrier_semaphore()
    for partner in partners:
        pl.semaphore_signal(barrier, inc=1, device_id=partner, device_id_type=MESH)

    def lay_flat(n, raw, flat):
        loads[n].wait()
        for d in (0, 1):
            flat[:, pl.ds(d * PLANE, PLANE)] = raw[:, d, :]

    lay_flat(0, feat_raw, feat)
    pl.semaphore_wait(barrier, len(partners))

    def block(channels_of):
        return field.at[aligned(channels_of * OWN, OWN, OWN)]

    pair = 1 + 2 * (zh % 2)
    other = 4 - pair
    far = 2

    def of_chip(k, number):
        return block(((zh + k) % 4) * 2 + number)

    early = [Group(feat), Group(feat)]
    late = [Group(feat), Group(feat)]
    from_far = [Group(feat), Group(feat)]
    relays = [Group(field.at[pl.ds(0, 2 * OWN)]) for _ in range(3)]
    k_early = pair + core * (other - pair)
    early[0].send(feat, block(af), along_z(k_early, 1), early[0].index + core)
    late[0].send(feat, block(af), along_z(4 - k_early, 1), late[0].index + core)
    from_sibling = Group(block(af)).send(feat, block(af), sibling)
    lay_flat(1, cot_raw, cot)

    edge = (1 - gy) * (PLANE - 128)
    low_edge = cot.at[:, aligned(edge, 128, 128)]
    high_edge = cot.at[:, aligned(edge + PLANE, 128, 128)]

    def halo(n):
        return cot_halo.at[:, pl.ds(2 * PLANE + n * 128, 128)]

    halos = Group(cot_halo)
    halos.send(low_edge, halo(3), (d_prev, side, af))
    halos.send(high_edge, halo(0), (d_next, side, af))
    halos.send(cot.at[:, pl.ds(0, PLANE)], cot_halo.at[:, pl.ds(PLANE, PLANE)], (d_prev, gy, af))
    halos.send(cot.at[:, pl.ds(PLANE, PLANE)], cot_halo.at[:, pl.ds(0, PLANE)], (d_next, gy, af))
    halos.send(low_edge, halo(1), (gz, side, af))
    halos.send(high_edge, halo(2), (gz, side, af))
    block(af)[...] = feat[...]
    loads[2].wait()
    taps_t[...] = taps[...].T

    def relay(n, k, number):
        rows = of_chip(k, number)
        relays[n].send(rows, rows, sibling)

    @pl.when(core == 1)
    def _():
        for n, k, back in ((0, pair, other), (1, other, pair)):
            early[n].wait_recv()
            rows = of_chip(k, n)
            from_far[n].send(rows, rows, along_z(back))
            relay(n, k, n)
        late[1].wait_recv()
        relay(0, pair, 1)

    halos.wait_recv()
    lane = lax.broadcasted_iota(jnp.int32, (OWN, PLANE + 128), 1)
    column = lane % WIDTH
    slab_lane = lax.broadcasted_iota(jnp.int32, (OWN, 128), 1)
    row_side = (slab_lane < WIDTH) == (gy == 0)
    inside = (gz > 0, None, None, gz < 15)
    for e in range(4):
        if e in (1, 2):
            plane = cot[:, pl.ds((e - 1) * PLANE, PLANE)].astype(F32)
        else:
            plane = cot_halo[:, pl.ds((e // 3) * PLANE, PLANE)].astype(F32)
        rows = jnp.where(row_side, halo(e)[...].astype(F32), 0.0)
        base = jnp.concatenate([plane, rows], axis=1)
        if inside[e] is not None:
            base = jnp.where(inside[e], base, 0.0)
        for c in (-1, 0, 1):
            if c == 0:
                moved = base
            else:
                moved = jnp.where(column == (0 if c == 1 else WIDTH - 1), 0.0, roll(base, c))
            tall = roll(moved, WIDTH).astype(BF16)
            moved = moved.astype(BF16)
            for a in (-1, 0, 1):
                d = e - 1 + a
                if d not in (0, 1):
                    continue
                for b in (-1, 0, 1):
                    piece = {-1: tall[:, 128:], 0: moved[:, :PLANE], 1: tall[:, :PLANE]}[b]
                    cim[pl.ds(tap_index(a, b, c) * OWN, OWN), pl.ds(d * PLANE, PLANE)] = piece

    def channels(half):
        return ((zh // 2 + half) % 2) * 128

    def filter_products(half):
        grad[half, pl.ds(0, ROWS)] = lax.dot_general(
            cim[...], field[aligned(channels(half), 128, 128)],
            (((1,), (1,)), ((), ())), preferred_element_type=F32,
        )
        grad[half, pl.ds(ROWS, PADDED - ROWS)] = jnp.zeros((PADDED - ROWS, 128), F32)

    orders = ((px, along_x, py, along_y), (py, along_y, px, along_x))

    def unit_rows(r, i):
        return aligned(r * 4 * CHUNK + i * CHUNK, CHUNK, 16)

    units = [(mine, r) for mine in (0, 1) for r in (0, 1)]
    first = [Group(grad_in.at[0, r, pl.ds(1, 3)]) for half, r in units]
    from_here = [Group(grad_code.at[0, 0]) for half, r in units]

    def scatter(half):
        relation = (core + half) % 2
        for r, (pos, along, _, _) in enumerate(orders):
            n = half * 2 + r
            there = first[0].index + relation * 2 + r
            for k in (2, 1, 3):
                code = grad_code.at[n, k]
                put_rows(code, grad[half, unit_rows(r, (pos + k) % 4)])
                first[n].send(code, grad_in.at[relation, r, k], along(k, gy, half), there)

            @pl.when(core != half)
            def _():
                code = grad_code.at[n, 0]
                put_rows(code, grad[half, unit_rows(r, pos)])
                from_here[n].send(code, grad_in.at[1, r, 0], sibling, there)

    def eight(pos, along):
        others = []
        for step in (5, 4, 3, 2, 7, 6, 1):
            k, row = step // 2, gy if step % 2 == 0 else side
            others.append((step - 1, along(k, row), ((pos + k) % 4) * 2 + row))
        return pos * 2 + gy, others

    def received(ref, mine, r):
        return ref.at[1, r] if mine else ref.at[0, r, pl.ds(1, 3)]

    def scatter_again():
        for u, (mine, r) in enumerate(units):
            pos, _, pos2, along2 = orders[r]
            first[u].wait_recv(received(grad_in, mine, r))
            total = get_rows(grad_in.at[mine, r, 0]) if mine else grad[core, unit_rows(r, pos)]
            for k in (1, 2, 3):
                total = total + get_rows(grad_in.at[mine, r, k])
            total = jnp.concatenate([total, jnp.zeros((8, 128), F32)], axis=0)
            for j in range(8):
                value = total[j * SUB:j * SUB + 16]
                part[u, j] = value
                part_code[u, j] = encode_sub(value)
            sent = Group(part_in.at[u])
            for n, device, there in eight(pos2, along2)[1]:
                sent.send(part_code.at[u, there], part_in.at[u, n], device)
            scattered_again[u] = sent

    def gather():
        for u, (mine, r) in enumerate(units):
            _, _, pos2, along2 = orders[r]
            place, others = eight(pos2, along2)
            scattered_again[u].wait_recv()
            total = part[u, place]
            for n in range(7):
                total = total + decode_sub(part_in[u, n])
            whole_code[u, place] = encode_sub(total * (1.0 / math.sqrt(32768.0)))
            sent = Group(part_in.at[u])
            for _, device, _ in others:
                sent.send(whole_code.at[u, place], whole_code.at[u, place], device)
            gathered[u] = sent

    def gather_again():
        for u, (mine, r) in enumerate(units):
            along = orders[r][1]
            gathered[u].wait_recv()
            sent = Group(received(whole_in, mine, r))
            for k in (2, 1, 3):
                sent.send(whole_code.at[u], whole_in.at[mine, r, k], along(k, gy, (core + mine) % 2))
            if mine:
                sent.send(whole_code.at[u], whole_in.at[1, r, 0], sibling)
            gathered_again[u] = sent

    def store(mine, r, k, ref):
        lanes = aligned(channels((core + mine) % 2), 128, 128)
        grad_out[unit_rows(r, (orders[r][0] + 4 - k) % 4), lanes] = get_subs(ref, rows_here)

    def finish():
        for r in (0, 1):
            store(0, r, 0, whole_code.at[r])
        for u, (mine, r) in enumerate(units):
            gathered_again[u].wait_recv()
            for k in range(1 - mine, 4):
                store(mine, r, k, whole_in.at[mine, r, k])

    scattered_again, gathered, gathered_again = {}, {}, {}

    @pl.when(core == 1)
    def _():
        late[0].wait_recv()
        relay(1, other, 0)

    pl.when(core == 0)(relays[0].wait_recv)
    from_sibling.wait_recv()
    filter_products(0)
    scatter(0)

    @pl.loop(0, 4)
    def _(n):
        cols = aligned(n * 256, 256, 256)
        back[:, cols] = lax.dot_general(
            taps_t[...], cim[:, cols], (((1,), (0,)), ((), ())), preferred_element_type=F32
        )

    to_sibling = Group(back_in)
    for k in range(4):
        to_sibling.send(back.at[aligned((2 * k + 1 - core) * OWN, OWN, OWN)], back_in.at[k], sibling)

    @pl.when(core == 1)
    def _():
        for n in (0, 1):
            from_far[n].wait_recv()
            relay(2, far, n)

    @pl.when(core == 0)
    def _():
        relays[1].wait_recv()
        relays[2].wait_recv()

    filter_products(1)
    scatter(1)

    to_sibling.wait_recv()
    for k in range(4):
        back_sum[k] = back[aligned((2 * k + core) * OWN, OWN, OWN)] + back_in[k]

    ring = Ring(Group, back_sum, zh, along_z(1), along_z(3), back_code, back_first, back_both)
    ring.start()

    scatter_again()

    @pl.loop(0, 4)
    def _(n):
        cols = aligned(n * 256, 256, 256)
        z[:, cols] = jnp.dot(taps[...], field[:, cols], preferred_element_type=F32)

    plane_lane = lane[:, :PLANE]
    plane_column = column[:, :PLANE]
    for e in range(4):
        rows_of = []
        for b in (-1, 0, 1):
            total = None
            for c in (-1, 0, 1):
                term = None
                for a in (-1, 0, 1):
                    d = e - 1 + a
                    if d in (0, 1):
                        value = z[pl.ds(tap_index(a, b, c) * OWN, OWN), pl.ds(d * PLANE, PLANE)]
                        term = value if term is None else term + value
                if c:
                    out = WIDTH - 1 if c == 1 else 0
                    term = jnp.where(plane_column == out, 0.0, roll(term, -c))
                total = term if total is None else total + term
            rows_of.append(roll(total, -b * WIDTH) if b else total)
        before, centre, after = rows_of
        core_sum[e] = (
            centre
            + jnp.where(plane_lane < PLANE - WIDTH, after, 0.0)
            + jnp.where(plane_lane >= WIDTH, before, 0.0)
        )
        outward = jnp.where(gy == 0, before[:, :128], after[:, PLANE - 128:])
        row_sum[e] = jnp.where(row_side, outward, 0.0)

    def resp_row(n):
        return resp_in.at[:, pl.ds(2 * PLANE + n * 128, 128)]

    outer = Group(resp_in)
    outer.send(core_sum.at[0], resp_in.at[:, pl.ds(PLANE, PLANE)], (d_prev, gy, af))
    outer.send(core_sum.at[3], resp_in.at[:, pl.ds(0, PLANE)], (d_next, gy, af))
    outer.send(row_sum.at[1], resp_row(0), (gz, side, af))
    outer.send(row_sum.at[2], resp_row(1), (gz, side, af))
    outer.send(row_sum.at[0], resp_row(3), (d_prev, side, af))
    outer.send(row_sum.at[3], resp_row(2), (d_next, side, af))

    gather()

    ring.middle()

    gather_again()

    outer.wait_recv()
    for d, valid in ((0, gz > 0), (1, gz < 15)):
        total = core_sum[d + 1] + jnp.where(valid, resp_in[:, pl.ds(d * PLANE, PLANE)], 0.0)
        slab = resp_row(d)[...] + jnp.where(valid, resp_row(2 + d)[...], 0.0)
        slab = jnp.concatenate(
            [
                jnp.where(gy == 1, slab, 0.0),
                jnp.zeros((OWN, PLANE - 256), F32),
                jnp.where(gy == 0, slab, 0.0),
            ],
            axis=1,
        )
        resp_out[:, d, :] = (total + slab).astype(BF16)

    for half, total in enumerate(ring.end()):
        for d in (0, 1):
            back_out[pl.ds(half * 16, 16), d, :] = total[:, d * PLANE:(d + 1) * PLANE].astype(BF16)

    finish()

    for n, (half, r) in enumerate(units):
        pl.when(core != half)(from_here[n].wait_send)
    @pl.when(core == 1)
    def _():
        for group in from_far + relays:
            group.wait_send()

    for group in groups:
        if group not in from_here + from_far + relays + [early[1], late[1]]:
            group.wait_send()


def shards(features, filters, cotangent):
    vmem = pl.BlockSpec(memory_space=pltpu.VMEM)
    resp, back, grad = pl.pallas_call(
        kernel,
        out_shape=(
            pltpu.VMEM((OWN, 2, PLANE), BF16),
            pltpu.VMEM((OWN, 2, PLANE), BF16),
            pltpu.VMEM((PADDED, C), F32),
        ),
        in_specs=[pl.BlockSpec(memory_space=pl.ANY)] * 3,
        out_specs=(vmem,) * 3,
        scratch_shapes=[
            pltpu.VMEM((OWN, 2, PLANE), BF16),
            pltpu.VMEM((OWN, 2, PLANE), BF16),
            pltpu.VMEM((ROWS, C), BF16),
            pltpu.VMEM((C, ROWS), BF16),
            pltpu.VMEM((OWN, CELLS), BF16),
            pltpu.VMEM((OWN, CELLS), BF16),
            pltpu.VMEM((C, CELLS), BF16),
            pltpu.VMEM((OWN, 2 * PLANE + 4 * 128), BF16),
            pltpu.VMEM((ROWS, CELLS), BF16),
            pltpu.VMEM((C, CELLS), F32),
            pltpu.VMEM((4, OWN, CELLS), F32),
            pltpu.VMEM((4, OWN, CELLS), F32),
            pltpu.VMEM((6, 16, CELLS + 128), BF16),
            pltpu.VMEM((2, 16, CELLS + 128), BF16),
            pltpu.VMEM((2, 2, 16, CELLS + 128), BF16),
            pltpu.VMEM((ROWS, CELLS), F32),
            pltpu.VMEM((4, OWN, PLANE), F32),
            pltpu.VMEM((4, OWN, 128), F32),
            pltpu.VMEM((OWN, 2 * PLANE + 4 * 128), F32),
            pltpu.VMEM((2, PADDED, 128), F32),
            pltpu.VMEM((4, 4, CHUNK + 16, 128), BF16),
            pltpu.VMEM((2, 2, 4, CHUNK + 16, 128), BF16),
            pltpu.VMEM((4, 8, 16, 128), F32),
            pltpu.VMEM((4, 8, 16, 128), BF16),
            pltpu.VMEM((4, 7, 16, 128), BF16),
            pltpu.VMEM((CHUNK + 16, 128), F32),
            pltpu.VMEM((4, 8, 16, 128), BF16),
            pltpu.VMEM((2, 2, 4, 8, 16, 128), BF16),
            pltpu.SemaphoreType.DMA((3,)),
            pltpu.SemaphoreType.DMA((N_GROUPS,)),
            pltpu.SemaphoreType.DMA((N_GROUPS,)),
        ],
        compiler_params=pltpu.CompilerParams(
            collective_id=0, has_side_effects=True, vmem_limit_bytes=60 * 1024 * 1024
        ),
    )(
        features,
        cotangent,
        filters.reshape(ROWS, C),
    )
    return resp, back, grad[:ROWS].reshape(filters.shape)


def solution(mesh):
    placed = (P("af", "gz", "gy"), P(None, None, None, "af", None), P("af", "gz", "gy"))
    return jax.shard_map(
        shards,
        mesh=mesh,
        in_specs=placed,
        out_specs=(P("af", "gz", "gy"), P("af", "gz", "gy"), P(None, None, None, "af", None)),
        check_vma=False,
    )
```

```python
import functools
import math

import jax
import jax.numpy as jnp
from jax import lax
from jax.experimental import pallas as pl
from jax.experimental.pallas import tpu as pltpu
from jax.sharding import PartitionSpec as P

MESH = pl.DeviceIdType.MESH
F32 = jnp.float32
BF16 = jnp.bfloat16
WIDTH = 64
PLANE = 512
CELLS = 1024
OWN = 32
C = 256
TAPS = 27
ROWS = TAPS * OWN
PADDED = 896
CHUNK = PADDED // 8
SUB = CHUNK // 8
N_GROUPS = 35


def tap_index(a, b, c):
    return ((a + 1) * 3 + (b + 1)) * 3 + (c + 1)


def roll(x, shift):
    return pltpu.roll(x, shift % x.shape[1], 1)


def aligned(start, size, unit):
    return pl.ds(pl.multiple_of(start, unit), size)


def encode(blocks):
    top = functools.reduce(jnp.maximum, [jnp.abs(block) for block in blocks])
    scale = jnp.maximum(top * 2.0**-7.75, 1e-30).astype(BF16)
    inverse = 1.0 / scale.astype(F32)
    codes = []
    for block in blocks:
        power = block * inverse
        for _ in range(4):
            power = power * power
        codes.append(jnp.where(block < 0, -power, power).astype(BF16))
    return codes, scale


def decode(codes, scale):
    scale = scale.astype(F32)
    blocks = []
    for code in codes:
        code = code.astype(F32)
        root = jnp.maximum(jnp.abs(code), 2e-38)
        for _ in range(4):
            root = lax.rsqrt(root)
        root = jnp.where(code == 0, 0.0, root * scale)
        blocks.append(jnp.where(code < 0, -root, root))
    return blocks


def put_rows(ref, value):
    codes, scale = encode([value[i:i + 16] for i in range(0, CHUNK, 16)])
    ref[pl.ds(0, CHUNK)] = jnp.concatenate(codes, axis=0)
    ref[pl.ds(CHUNK, 16)] = scale


def get_rows(ref):
    codes = [ref[pl.ds(i, 16)] for i in range(0, CHUNK, 16)]
    return jnp.concatenate(decode(codes, ref[pl.ds(CHUNK, 16)]), axis=0)


def encode_sub(value):
    valid = lax.broadcasted_iota(jnp.int32, value.shape, 0) < SUB
    top = jnp.max(jnp.where(valid, jnp.abs(value), 0.0), axis=0, keepdims=True)
    scale = jnp.maximum(jnp.broadcast_to(top, value.shape) * 2.0**-7.75, 1e-30)
    scale = scale.astype(BF16).astype(F32)
    power = value * (1.0 / scale)
    for _ in range(4):
        power = power * power
    return jnp.where(valid, jnp.where(value < 0, -power, power), scale).astype(BF16)


def decode_sub(code):
    scale = jnp.broadcast_to(code.astype(F32)[SUB:SUB + 1], code.shape)
    return decode([code], scale)[0]


def get_subs(ref, rows):
    for j in range(8):
        rows[pl.ds(j * SUB, 16)] = decode_sub(ref[j])
    return rows[pl.ds(0, CHUNK)]


def put_columns(ref, value):
    codes, scale = encode([value[:, i:i + 128] for i in range(0, CELLS, 128)])
    ref[:, pl.ds(0, CELLS)] = jnp.concatenate(codes, axis=1)
    ref[:, pl.ds(CELLS, 128)] = scale


def get_columns(ref):
    codes = [ref[:, pl.ds(i, 128)] for i in range(0, CELLS, 128)]
    return jnp.concatenate(decode(codes, ref[:, pl.ds(CELLS, 128)]), axis=1)


class Ring:
    def __init__(self, group, chunks, pos, nxt, prv, out, first, both):
        self.group, self.chunks, self.pos, self.nxt, self.prv = group, chunks, pos, nxt, prv
        self.out, self.first, self.both = out, first, both

    def part(self, k, half):
        return self.chunks[(self.pos + k) % 4, pl.ds(half * 16, 16)]

    def start(self):
        self.early, self.late = self.group(self.first), self.group(self.both)
        put_columns(self.out.at[0], self.part(2, 0))
        self.early.send(self.out.at[0], self.first.at[0], self.nxt)
        put_columns(self.out.at[1], self.part(2, 1))
        self.early.send(self.out.at[1], self.first.at[1], self.prv)
        put_columns(self.out.at[2], self.part(1, 1))
        self.late.send(self.out.at[2], self.both.at[0, 1], self.nxt)
        put_columns(self.out.at[3], self.part(3, 0))
        self.late.send(self.out.at[3], self.both.at[1, 0], self.prv)

    def middle(self):
        self.early.wait_recv()
        put_columns(self.out.at[4], self.part(1, 0) + get_columns(self.first.at[0]))
        self.late.send(self.out.at[4], self.both.at[0, 0], self.nxt)
        put_columns(self.out.at[5], self.part(3, 1) + get_columns(self.first.at[1]))
        self.late.send(self.out.at[5], self.both.at[1, 1], self.prv)

    def end(self):
        self.late.wait_recv()
        return [
            self.part(0, half) + get_columns(self.both.at[0, half]) + get_columns(self.both.at[1, half])
            for half in (0, 1)
        ]


def kernel(
    feat_hbm, cot_hbm, taps_hbm, both_out, grad_out,
    feat_raw, cot_raw, taps, taps_t, feat, cot, field, cot_halo, cim,
    back, back_in, back_sum, back_code, back_first, back_both,
    z, core_sum, row_sum, resp_in,
    grad, grad_code, grad_in, part, part_code, part_in, rows_here, whole_code, whole_in,
    load_sem, send_sem, recv_sem,
):
    loads = [
        pltpu.make_async_copy(src, dst, load_sem.at[n])
        for n, (src, dst) in enumerate(((feat_hbm, feat_raw), (cot_hbm, cot_raw), (taps_hbm, taps)))
    ]
    for load in loads:
        load.start()
    gz = lax.axis_index("gz")
    gy = lax.axis_index("gy")
    af = lax.axis_index("af")
    py, px = gz // 4, gz % 4
    zh, core = af // 2, af % 2

    sibling = (gz, gy, zh * 2 + (1 - core))
    d_next, d_prev = (gz + 1) % 16, (gz + 15) % 16
    side = 1 - gy

    def along_x(k, row=gy, to=core):
        return (py * 4 + (px + k) % 4, row, zh * 2 + to)

    def along_y(k, row=gy, to=core):
        return (((py + k) % 4) * 4 + px, row, zh * 2 + to)

    def along_z(k, to=core):
        return (gz, gy, ((zh + k) % 4) * 2 + to)

    groups = []

    class Group:
        def __init__(self, size):
            self.index, self.size = len(groups), size
            groups.append(self)

        def send(self, src, dst, device, there=None):
            there = self.index if there is None else there
            pltpu.make_async_remote_copy(
                src_ref=src, dst_ref=dst,
                send_sem=send_sem.at[self.index], recv_sem=recv_sem.at[there],
                device_id=device, device_id_type=MESH,
            ).start()
            return self

        def wait_recv(self, size=None):
            size = self.size if size is None else size
            pltpu.make_async_copy(size, size, recv_sem.at[self.index]).wait()

        def wait_send(self):
            pltpu.make_async_copy(self.size, self.size, send_sem.at[self.index]).wait()

    partners = [sibling, (d_next, gy, af), (d_prev, gy, af)]
    partners += [(d_next, side, af), (d_prev, side, af), (gz, side, af)]
    for k in (1, 3):
        partners += [along_z(k), along_z(k, 1 - core)]
    for k in (1, 2, 3):
        for along in (along_x, along_y):
            partners += [along(k), along(k, side), along(k, gy, 1 - core)]
    barrier = pltpu.get_barrier_semaphore()
    for partner in partners:
        pl.semaphore_signal(barrier, inc=1, device_id=partner, device_id_type=MESH)

    def lay_flat(n, raw, flat):
        loads[n].wait()
        for d in (0, 1):
            flat[:, pl.ds(d * PLANE, PLANE)] = raw[:, d, :]

    lay_flat(0, feat_raw, feat)
    pl.semaphore_wait(barrier, len(partners))

    def block(channels_of):
        return field.at[aligned(channels_of * OWN, OWN, OWN)]

    pair = 1 + 2 * (zh % 2)
    other = 4 - pair
    far = 2

    def of_chip(k, number):
        return block(((zh + k) % 4) * 2 + number)

    early = [Group(feat), Group(feat)]
    late = [Group(feat), Group(feat)]
    from_far = [Group(feat), Group(feat)]
    relays = [Group(field.at[pl.ds(0, 2 * OWN)]) for _ in range(3)]
    k_early = pair + core * (other - pair)
    early[0].send(feat, block(af), along_z(k_early, 1), early[0].index + core)
    late[0].send(feat, block(af), along_z(4 - k_early, 1), late[0].index + core)
    from_sibling = Group(block(af)).send(feat, block(af), sibling)
    lay_flat(1, cot_raw, cot)

    edge = (1 - gy) * (PLANE - 128)
    low_edge = cot.at[:, aligned(edge, 128, 128)]
    high_edge = cot.at[:, aligned(edge + PLANE, 128, 128)]

    def halo(n):
        return cot_halo.at[:, pl.ds(2 * PLANE + n * 128, 128)]

    halos = Group(cot_halo)
    halos.send(low_edge, halo(3), (d_prev, side, af))
    halos.send(high_edge, halo(0), (d_next, side, af))
    halos.send(cot.at[:, pl.ds(0, PLANE)], cot_halo.at[:, pl.ds(PLANE, PLANE)], (d_prev, gy, af))
    halos.send(cot.at[:, pl.ds(PLANE, PLANE)], cot_halo.at[:, pl.ds(0, PLANE)], (d_next, gy, af))
    halos.send(low_edge, halo(1), (gz, side, af))
    halos.send(high_edge, halo(2), (gz, side, af))
    block(af)[...] = feat[...]
    loads[2].wait()
    taps_t[...] = taps[...].T

    def relay(n, k, number):
        rows = of_chip(k, number)
        relays[n].send(rows, rows, sibling)

    @pl.when(core == 1)
    def _():
        for n, k, back in ((0, pair, other), (1, other, pair)):
            early[n].wait_recv()
            rows = of_chip(k, n)
            from_far[n].send(rows, rows, along_z(back))
            relay(n, k, n)
        late[1].wait_recv()
        relay(0, pair, 1)

    halos.wait_recv()
    lane = lax.broadcasted_iota(jnp.int32, (OWN, PLANE + 128), 1)
    column = lane % WIDTH
    slab_lane = lax.broadcasted_iota(jnp.int32, (OWN, 128), 1)
    row_side = (slab_lane < WIDTH) == (gy == 0)
    inside = (gz > 0, None, None, gz < 15)
    for e in range(4):
        if e in (1, 2):
            plane = cot[:, pl.ds((e - 1) * PLANE, PLANE)].astype(F32)
        else:
            plane = cot_halo[:, pl.ds((e // 3) * PLANE, PLANE)].astype(F32)
        rows = jnp.where(row_side, halo(e)[...].astype(F32), 0.0)
        base = jnp.concatenate([plane, rows], axis=1)
        if inside[e] is not None:
            base = jnp.where(inside[e], base, 0.0)
        for c in (-1, 0, 1):
            if c == 0:
                moved = base
            else:
                moved = jnp.where(column == (0 if c == 1 else WIDTH - 1), 0.0, roll(base, c))
            tall = roll(moved, WIDTH).astype(BF16)
            moved = moved.astype(BF16)
            for a in (-1, 0, 1):
                d = e - 1 + a
                if d not in (0, 1):
                    continue
                for b in (-1, 0, 1):
                    piece = {-1: tall[:, 128:], 0: moved[:, :PLANE], 1: tall[:, :PLANE]}[b]
                    cim[pl.ds(tap_index(a, b, c) * OWN, OWN), pl.ds(d * PLANE, PLANE)] = piece

    def channels(half):
        return ((zh // 2 + half) % 2) * 128

    def filter_products(half):
        grad[half, pl.ds(0, ROWS)] = lax.dot_general(
            cim[...], field[aligned(channels(half), 128, 128)],
            (((1,), (1,)), ((), ())), preferred_element_type=F32,
        )
        grad[half, pl.ds(ROWS, PADDED - ROWS)] = jnp.zeros((PADDED - ROWS, 128), F32)

    orders = ((px, along_x, py, along_y), (py, along_y, px, along_x))

    def unit_rows(r, i):
        return aligned(r * 4 * CHUNK + i * CHUNK, CHUNK, 16)

    units = [(mine, r) for mine in (0, 1) for r in (0, 1)]
    first = [Group(grad_in.at[0, r, pl.ds(1, 3)]) for half, r in units]
    from_here = [Group(grad_code.at[0, 0]) for half, r in units]

    def scatter(half):
        relation = (core + half) % 2
        for r, (pos, along, _, _) in enumerate(orders):
            n = half * 2 + r
            there = first[0].index + relation * 2 + r
            for k in (2, 1, 3):
                code = grad_code.at[n, k]
                put_rows(code, grad[half, unit_rows(r, (pos + k) % 4)])
                first[n].send(code, grad_in.at[relation, r, k], along(k, gy, half), there)

            @pl.when(core != half)
            def _():
                code = grad_code.at[n, 0]
                put_rows(code, grad[half, unit_rows(r, pos)])
                from_here[n].send(code, grad_in.at[1, r, 0], sibling, there)

    def eight(pos, along):
        others = []
        for step in (5, 4, 3, 2, 7, 6, 1):
            k, row = step // 2, gy if step % 2 == 0 else side
            others.append((step - 1, along(k, row), ((pos + k) % 4) * 2 + row))
        return pos * 2 + gy, others

    def received(ref, mine, r):
        return ref.at[1, r] if mine else ref.at[0, r, pl.ds(1, 3)]

    def scatter_again():
        for u, (mine, r) in enumerate(units):
            pos, _, pos2, along2 = orders[r]
            first[u].wait_recv(received(grad_in, mine, r))
            total = get_rows(grad_in.at[mine, r, 0]) if mine else grad[core, unit_rows(r, pos)]
            for k in (1, 2, 3):
                total = total + get_rows(grad_in.at[mine, r, k])
            total = jnp.concatenate([total, jnp.zeros((8, 128), F32)], axis=0)
            for j in range(8):
                value = total[j * SUB:j * SUB + 16]
                part[u, j] = value
                part_code[u, j] = encode_sub(value)
            sent = Group(part_in.at[u])
            for n, device, there in eight(pos2, along2)[1]:
                sent.send(part_code.at[u, there], part_in.at[u, n], device)
            scattered_again[u] = sent

    def gather():
        for u, (mine, r) in enumerate(units):
            _, _, pos2, along2 = orders[r]
            place, others = eight(pos2, along2)
            scattered_again[u].wait_recv()
            total = part[u, place]
            for n in range(7):
                total = total + decode_sub(part_in[u, n])
            whole_code[u, place] = encode_sub(total * (1.0 / math.sqrt(32768.0)))
            sent = Group(part_in.at[u])
            for _, device, _ in others:
                sent.send(whole_code.at[u, place], whole_code.at[u, place], device)
            gathered[u] = sent

    def gather_again():
        for u, (mine, r) in enumerate(units):
            along = orders[r][1]
            gathered[u].wait_recv()
            sent = Group(received(whole_in, mine, r))
            for k in (2, 1, 3):
                sent.send(whole_code.at[u], whole_in.at[mine, r, k], along(k, gy, (core + mine) % 2))
            if mine:
                sent.send(whole_code.at[u], whole_in.at[1, r, 0], sibling)
            gathered_again[u] = sent

    def store(mine, r, k, ref):
        lanes = aligned(channels((core + mine) % 2), 128, 128)
        grad_out[unit_rows(r, (orders[r][0] + 4 - k) % 4), lanes] = get_subs(ref, rows_here)

    def finish():
        for r in (0, 1):
            store(0, r, 0, whole_code.at[r])
        for u, (mine, r) in enumerate(units):
            gathered_again[u].wait_recv()
            for k in range(1 - mine, 4):
                store(mine, r, k, whole_in.at[mine, r, k])

    scattered_again, gathered, gathered_again = {}, {}, {}

    @pl.when(core == 1)
    def _():
        late[0].wait_recv()
        relay(1, other, 0)

    pl.when(core == 0)(relays[0].wait_recv)
    from_sibling.wait_recv()
    filter_products(0)
    scatter(0)

    @pl.loop(0, 4)
    def _(n):
        cols = aligned(n * 256, 256, 256)
        back[:, cols] = lax.dot_general(
            taps_t[...], cim[:, cols], (((1,), (0,)), ((), ())), preferred_element_type=F32
        )

    to_sibling = Group(back_in)
    for k in range(4):
        to_sibling.send(back.at[aligned((2 * k + 1 - core) * OWN, OWN, OWN)], back_in.at[k], sibling)

    @pl.when(core == 1)
    def _():
        for n in (0, 1):
            from_far[n].wait_recv()
            relay(2, far, n)

    @pl.when(core == 0)
    def _():
        relays[1].wait_recv()
        relays[2].wait_recv()

    filter_products(1)
    scatter(1)

    to_sibling.wait_recv()
    for k in range(4):
        back_sum[k] = back[aligned((2 * k + core) * OWN, OWN, OWN)] + back_in[k]

    ring = Ring(Group, back_sum, zh, along_z(1), along_z(3), back_code, back_first, back_both)
    ring.start()

    scatter_again()

    @pl.loop(0, 4)
    def _(n):
        cols = aligned(n * 256, 256, 256)
        z[:, cols] = jnp.dot(taps[...], field[:, cols], preferred_element_type=F32)

    plane_lane = lane[:, :PLANE]
    plane_column = column[:, :PLANE]
    for e in range(4):
        rows_of = []
        for b in (-1, 0, 1):
            total = None
            for c in (-1, 0, 1):
                term = None
                for a in (-1, 0, 1):
                    d = e - 1 + a
                    if d in (0, 1):
                        value = z[pl.ds(tap_index(a, b, c) * OWN, OWN), pl.ds(d * PLANE, PLANE)]
                        term = value if term is None else term + value
                if c:
                    out = WIDTH - 1 if c == 1 else 0
                    term = jnp.where(plane_column == out, 0.0, roll(term, -c))
                total = term if total is None else total + term
            rows_of.append(roll(total, -b * WIDTH) if b else total)
        before, centre, after = rows_of
        core_sum[e] = (
            centre
            + jnp.where(plane_lane < PLANE - WIDTH, after, 0.0)
            + jnp.where(plane_lane >= WIDTH, before, 0.0)
        )
        outward = jnp.where(gy == 0, before[:, :128], after[:, PLANE - 128:])
        row_sum[e] = jnp.where(row_side, outward, 0.0)

    def resp_row(n):
        return resp_in.at[:, pl.ds(2 * PLANE + n * 128, 128)]

    outer = Group(resp_in)
    outer.send(core_sum.at[0], resp_in.at[:, pl.ds(PLANE, PLANE)], (d_prev, gy, af))
    outer.send(core_sum.at[3], resp_in.at[:, pl.ds(0, PLANE)], (d_next, gy, af))
    outer.send(row_sum.at[1], resp_row(0), (gz, side, af))
    outer.send(row_sum.at[2], resp_row(1), (gz, side, af))
    outer.send(row_sum.at[0], resp_row(3), (d_prev, side, af))
    outer.send(row_sum.at[3], resp_row(2), (d_next, side, af))

    gather()

    ring.middle()

    gather_again()

    outer.wait_recv()
    for d, valid in ((0, gz > 0), (1, gz < 15)):
        total = core_sum[d + 1] + jnp.where(valid, resp_in[:, pl.ds(d * PLANE, PLANE)], 0.0)
        slab = resp_row(d)[...] + jnp.where(valid, resp_row(2 + d)[...], 0.0)
        slab = jnp.concatenate(
            [
                jnp.where(gy == 1, slab, 0.0),
                jnp.zeros((OWN, PLANE - 256), F32),
                jnp.where(gy == 0, slab, 0.0),
            ],
            axis=1,
        )
        both_out[0, :, d, :] = (total + slab).astype(BF16)

    for half, total in enumerate(ring.end()):
        for d in (0, 1):
            both_out[1, pl.ds(half * 16, 16), d, :] = total[:, d * PLANE:(d + 1) * PLANE].astype(BF16)

    finish()

    for n, (half, r) in enumerate(units):
        pl.when(core != half)(from_here[n].wait_send)
    @pl.when(core == 1)
    def _():
        for group in from_far + relays:
            group.wait_send()

    for group in groups:
        if group not in from_here + from_far + relays + [early[1], late[1]]:
            group.wait_send()


def shards(features, filters, cotangent):
    vmem = pl.BlockSpec(memory_space=pltpu.VMEM)
    both, grad = pl.pallas_call(
        kernel,
        out_shape=(
            pltpu.VMEM((2, OWN, 2, PLANE), BF16),
            pltpu.VMEM((PADDED, C), F32),
        ),
        in_specs=[pl.BlockSpec(memory_space=pl.ANY)] * 3,
        out_specs=(vmem,) * 2,
        scratch_shapes=[
            pltpu.VMEM((OWN, 2, PLANE), BF16),
            pltpu.VMEM((OWN, 2, PLANE), BF16),
            pltpu.VMEM((ROWS, C), BF16),
            pltpu.VMEM((C, ROWS), BF16),
            pltpu.VMEM((OWN, CELLS), BF16),
            pltpu.VMEM((OWN, CELLS), BF16),
            pltpu.VMEM((C, CELLS), BF16),
            pltpu.VMEM((OWN, 2 * PLANE + 4 * 128), BF16),
            pltpu.VMEM((ROWS, CELLS), BF16),
            pltpu.VMEM((C, CELLS), F32),
            pltpu.VMEM((4, OWN, CELLS), F32),
            pltpu.VMEM((4, OWN, CELLS), F32),
            pltpu.VMEM((6, 16, CELLS + 128), BF16),
            pltpu.VMEM((2, 16, CELLS + 128), BF16),
            pltpu.VMEM((2, 2, 16, CELLS + 128), BF16),
            pltpu.VMEM((ROWS, CELLS), F32),
            pltpu.VMEM((4, OWN, PLANE), F32),
            pltpu.VMEM((4, OWN, 128), F32),
            pltpu.VMEM((OWN, 2 * PLANE + 4 * 128), F32),
            pltpu.VMEM((2, PADDED, 128), F32),
            pltpu.VMEM((4, 4, CHUNK + 16, 128), BF16),
            pltpu.VMEM((2, 2, 4, CHUNK + 16, 128), BF16),
            pltpu.VMEM((4, 8, 16, 128), F32),
            pltpu.VMEM((4, 8, 16, 128), BF16),
            pltpu.VMEM((4, 7, 16, 128), BF16),
            pltpu.VMEM((CHUNK + 16, 128), F32),
            pltpu.VMEM((4, 8, 16, 128), BF16),
            pltpu.VMEM((2, 2, 4, 8, 16, 128), BF16),
            pltpu.SemaphoreType.DMA((3,)),
            pltpu.SemaphoreType.DMA((N_GROUPS,)),
            pltpu.SemaphoreType.DMA((N_GROUPS,)),
        ],
        compiler_params=pltpu.CompilerParams(
            collective_id=0, has_side_effects=True, vmem_limit_bytes=60 * 1024 * 1024
        ),
    )(
        features,
        cotangent,
        filters.reshape(ROWS, C),
    )
    return both[0], both[1], grad[:ROWS].reshape(filters.shape)


def solution(mesh):
    placed = (P("af", "gz", "gy"), P(None, None, None, "af", None), P("af", "gz", "gy"))
    return jax.shard_map(
        shards,
        mesh=mesh,
        in_specs=placed,
        out_specs=(P("af", "gz", "gy"), P("af", "gz", "gy"), P(None, None, None, "af", None)),
        check_vma=False,
    )
```

```python
import functools
import math

import jax
import jax.numpy as jnp
from jax import lax
from jax.experimental import pallas as pl
from jax.experimental.pallas import tpu as pltpu
from jax.sharding import PartitionSpec as P

MESH = pl.DeviceIdType.MESH
F32 = jnp.float32
BF16 = jnp.bfloat16
WIDTH = 64
PLANE = 512
CELLS = 1024
OWN = 32
C = 256
TAPS = 27
ROWS = TAPS * OWN
PADDED = 896
CHUNK = PADDED // 8
SUB = CHUNK // 8
N_GROUPS = 35


def tap_index(a, b, c):
    return ((a + 1) * 3 + (b + 1)) * 3 + (c + 1)


def roll(x, shift):
    return pltpu.roll(x, shift % x.shape[1], 1)


def aligned(start, size, unit):
    return pl.ds(pl.multiple_of(start, unit), size)


def encode(blocks):
    top = functools.reduce(jnp.maximum, [jnp.abs(block) for block in blocks])
    scale = jnp.maximum(top * 2.0**-7.75, 1e-30).astype(BF16)
    inverse = 1.0 / scale.astype(F32)
    codes = []
    for block in blocks:
        power = block * inverse
        for _ in range(4):
            power = power * power
        codes.append(jnp.where(block < 0, -power, power).astype(BF16))
    return codes, scale


def decode(codes, scale):
    scale = scale.astype(F32)
    blocks = []
    for code in codes:
        code = code.astype(F32)
        root = jnp.exp2(jnp.log2(jnp.maximum(jnp.abs(code), 2e-38)) * (1 / 16))
        root = jnp.where(code == 0, 0.0, root * scale)
        blocks.append(jnp.where(code < 0, -root, root))
    return blocks


def put_rows(ref, value):
    codes, scale = encode([value[i:i + 16] for i in range(0, CHUNK, 16)])
    ref[pl.ds(0, CHUNK)] = jnp.concatenate(codes, axis=0)
    ref[pl.ds(CHUNK, 16)] = scale


def get_rows(ref):
    codes = [ref[pl.ds(i, 16)] for i in range(0, CHUNK, 16)]
    return jnp.concatenate(decode(codes, ref[pl.ds(CHUNK, 16)]), axis=0)


def encode_sub(value):
    valid = lax.broadcasted_iota(jnp.int32, value.shape, 0) < SUB
    top = jnp.max(jnp.where(valid, jnp.abs(value), 0.0), axis=0, keepdims=True)
    scale = jnp.maximum(jnp.broadcast_to(top, value.shape) * 2.0**-7.75, 1e-30)
    scale = scale.astype(BF16).astype(F32)
    power = value * (1.0 / scale)
    for _ in range(4):
        power = power * power
    return jnp.where(valid, jnp.where(value < 0, -power, power), scale).astype(BF16)


def decode_sub(code):
    scale = jnp.broadcast_to(code.astype(F32)[SUB:SUB + 1], code.shape)
    return decode([code], scale)[0]


def get_subs(ref, rows):
    for j in range(8):
        rows[pl.ds(j * SUB, 16)] = decode_sub(ref[j])
    return rows[pl.ds(0, CHUNK)]


def put_columns(ref, value):
    codes, scale = encode([value[:, i:i + 128] for i in range(0, CELLS, 128)])
    ref[:, pl.ds(0, CELLS)] = jnp.concatenate(codes, axis=1)
    ref[:, pl.ds(CELLS, 128)] = scale


def get_columns(ref):
    codes = [ref[:, pl.ds(i, 128)] for i in range(0, CELLS, 128)]
    return jnp.concatenate(decode(codes, ref[:, pl.ds(CELLS, 128)]), axis=1)


class Ring:
    def __init__(self, group, chunks, pos, nxt, prv, out, first, both):
        self.group, self.chunks, self.pos, self.nxt, self.prv = group, chunks, pos, nxt, prv
        self.out, self.first, self.both = out, first, both
        self.early, self.late = group(first), group(both)

    def part(self, k, half):
        return self.chunks[(self.pos + k) % 4, pl.ds(half * 16, 16)]

    def start(self):
        put_columns(self.out.at[0], self.part(2, 0))
        self.early.send(self.out.at[0], self.first.at[0], self.nxt)
        put_columns(self.out.at[1], self.part(2, 1))
        self.early.send(self.out.at[1], self.first.at[1], self.prv)
        put_columns(self.out.at[2], self.part(1, 1))
        self.late.send(self.out.at[2], self.both.at[0, 1], self.nxt)
        put_columns(self.out.at[3], self.part(3, 0))
        self.late.send(self.out.at[3], self.both.at[1, 0], self.prv)

    def middle(self):
        self.early.wait_recv()
        put_columns(self.out.at[4], self.part(1, 0) + get_columns(self.first.at[0]))
        self.late.send(self.out.at[4], self.both.at[0, 0], self.nxt)
        put_columns(self.out.at[5], self.part(3, 1) + get_columns(self.first.at[1]))
        self.late.send(self.out.at[5], self.both.at[1, 1], self.prv)

    def end(self):
        self.late.wait_recv()
        return [
            self.part(0, half) + get_columns(self.both.at[0, half]) + get_columns(self.both.at[1, half])
            for half in (0, 1)
        ]


def kernel(
    feat_hbm, cot_hbm, taps_hbm, both_out, grad_out,
    feat_raw, cot_raw, taps, taps_t, feat, cot, field, cot_halo, cim,
    back, back_in, back_sum, back_code, back_first, back_both,
    z, core_sum, row_sum, resp_in,
    grad, grad_code, grad_in, part, part_code, part_in, rows_here, whole_code, whole_in,
    load_sem, send_sem, recv_sem,
):
    loads = [
        pltpu.make_async_copy(src, dst, load_sem.at[n])
        for n, (src, dst) in enumerate(((feat_hbm, feat_raw), (cot_hbm, cot_raw), (taps_hbm, taps)))
    ]
    for load in loads:
        load.start()
    gz = lax.axis_index("gz")
    gy = lax.axis_index("gy")
    af = lax.axis_index("af")
    py, px = gz // 4, gz % 4
    zh, core = af // 2, af % 2

    sibling = (gz, gy, zh * 2 + (1 - core))
    d_next, d_prev = (gz + 1) % 16, (gz + 15) % 16
    side = 1 - gy

    def along_x(k, row=gy, to=core):
        return (py * 4 + (px + k) % 4, row, zh * 2 + to)

    def along_y(k, row=gy, to=core):
        return (((py + k) % 4) * 4 + px, row, zh * 2 + to)

    def along_z(k, to=core):
        return (gz, gy, ((zh + k) % 4) * 2 + to)

    groups = []

    class Group:
        def __init__(self, size):
            self.index, self.size = len(groups), size
            groups.append(self)

        def send(self, src, dst, device, there=None):
            there = self.index if there is None else there
            pltpu.make_async_remote_copy(
                src_ref=src, dst_ref=dst,
                send_sem=send_sem.at[self.index], recv_sem=recv_sem.at[there],
                device_id=device, device_id_type=MESH,
            ).start()
            return self

        def wait_recv(self, size=None):
            size = self.size if size is None else size
            pltpu.make_async_copy(size, size, recv_sem.at[self.index]).wait()

        def wait_send(self):
            pltpu.make_async_copy(self.size, self.size, send_sem.at[self.index]).wait()

    partners = [sibling, (d_next, gy, af), (d_prev, gy, af)]
    partners += [(d_next, side, af), (d_prev, side, af), (gz, side, af)]
    for k in (1, 3):
        partners += [along_z(k), along_z(k, 1 - core)]
    for k in (1, 2, 3):
        for along in (along_x, along_y):
            partners += [along(k), along(k, side), along(k, gy, 1 - core)]
    barrier = pltpu.get_barrier_semaphore()
    for partner in partners:
        pl.semaphore_signal(barrier, inc=1, device_id=partner, device_id_type=MESH)

    def lay_flat(n, raw, flat):
        loads[n].wait()
        for d in (0, 1):
            flat[:, pl.ds(d * PLANE, PLANE)] = raw[:, d, :]

    lay_flat(0, feat_raw, feat)
    pl.semaphore_wait(barrier, len(partners))

    def block(channels_of):
        return field.at[aligned(channels_of * OWN, OWN, OWN)]

    pair = 1 + 2 * (zh % 2)
    other = 4 - pair
    far = 2

    def of_chip(k, number):
        return block(((zh + k) % 4) * 2 + number)

    early = [Group(feat), Group(feat)]
    late = [Group(feat), Group(feat)]
    from_far = [Group(feat), Group(feat)]
    relays = [Group(field.at[pl.ds(0, 2 * OWN)]) for _ in range(3)]
    k_early = pair + core * (other - pair)
    early[0].send(feat, block(af), along_z(k_early, 1), early[0].index + core)
    late[0].send(feat, block(af), along_z(4 - k_early, 1), late[0].index + core)
    from_sibling = Group(block(af)).send(feat, block(af), sibling)
    lay_flat(1, cot_raw, cot)

    edge = (1 - gy) * (PLANE - 128)
    low_edge = cot.at[:, aligned(edge, 128, 128)]
    high_edge = cot.at[:, aligned(edge + PLANE, 128, 128)]

    def halo(n):
        return cot_halo.at[:, pl.ds(2 * PLANE + n * 128, 128)]

    halos = Group(cot_halo)
    halos.send(low_edge, halo(3), (d_prev, side, af))
    halos.send(high_edge, halo(0), (d_next, side, af))
    halos.send(cot.at[:, pl.ds(0, PLANE)], cot_halo.at[:, pl.ds(PLANE, PLANE)], (d_prev, gy, af))
    halos.send(cot.at[:, pl.ds(PLANE, PLANE)], cot_halo.at[:, pl.ds(0, PLANE)], (d_next, gy, af))
    halos.send(low_edge, halo(1), (gz, side, af))
    halos.send(high_edge, halo(2), (gz, side, af))
    block(af)[...] = feat[...]
    loads[2].wait()
    taps_t[...] = taps[...].T

    def relay(n, k, number):
        rows = of_chip(k, number)
        relays[n].send(rows, rows, sibling)

    @pl.when(core == 1)
    def _():
        for n, k, back in ((0, pair, other), (1, other, pair)):
            early[n].wait_recv()
            rows = of_chip(k, n)
            from_far[n].send(rows, rows, along_z(back))
            relay(n, k, n)
        late[1].wait_recv()
        relay(0, pair, 1)

    halos.wait_recv()
    lane = lax.broadcasted_iota(jnp.int32, (OWN, PLANE + 128), 1)
    column = lane % WIDTH
    slab_lane = lax.broadcasted_iota(jnp.int32, (OWN, 128), 1)
    row_side = (slab_lane < WIDTH) == (gy == 0)
    inside = (gz > 0, None, None, gz < 15)
    for e in range(4):
        if e in (1, 2):
            plane = cot[:, pl.ds((e - 1) * PLANE, PLANE)].astype(F32)
        else:
            plane = cot_halo[:, pl.ds((e // 3) * PLANE, PLANE)].astype(F32)
        rows = jnp.where(row_side, halo(e)[...].astype(F32), 0.0)
        base = jnp.concatenate([plane, rows], axis=1)
        if inside[e] is not None:
            base = jnp.where(inside[e], base, 0.0)
        for c in (-1, 0, 1):
            if c == 0:
                moved = base
            else:
                moved = jnp.where(column == (0 if c == 1 else WIDTH - 1), 0.0, roll(base, c))
            tall = roll(moved, WIDTH).astype(BF16)
            moved = moved.astype(BF16)
            for a in (-1, 0, 1):
                d = e - 1 + a
                if d not in (0, 1):
                    continue
                for b in (-1, 0, 1):
                    piece = {-1: tall[:, 128:], 0: moved[:, :PLANE], 1: tall[:, :PLANE]}[b]
                    cim[pl.ds(tap_index(a, b, c) * OWN, OWN), pl.ds(d * PLANE, PLANE)] = piece

    def channels(half):
        return ((zh // 2 + half) % 2) * 128

    def filter_products(half):
        grad[half, pl.ds(0, ROWS)] = lax.dot_general(
            cim[...], field[aligned(channels(half), 128, 128)],
            (((1,), (1,)), ((), ())), preferred_element_type=F32,
        )
        grad[half, pl.ds(ROWS, PADDED - ROWS)] = jnp.zeros((PADDED - ROWS, 128), F32)

    orders = ((px, along_x, py, along_y), (py, along_y, px, along_x))

    def unit_rows(r, i):
        return aligned(r * 4 * CHUNK + i * CHUNK, CHUNK, 16)

    units = [(mine, r) for mine in (0, 1) for r in (0, 1)]
    first = [Group(grad_in.at[0, r, pl.ds(1, 3)]) for half, r in units]
    from_here = [Group(grad_code.at[0, 0]) for half, r in units]

    def scatter(half):
        relation = (core + half) % 2
        for r, (pos, along, _, _) in enumerate(orders):
            n = half * 2 + r
            there = first[0].index + relation * 2 + r
            for k in (2, 1, 3):
                code = grad_code.at[n, k]
                put_rows(code, grad[half, unit_rows(r, (pos + k) % 4)])
                first[n].send(code, grad_in.at[relation, r, k], along(k, gy, half), there)

            @pl.when(core != half)
            def _():
                code = grad_code.at[n, 0]
                put_rows(code, grad[half, unit_rows(r, pos)])
                from_here[n].send(code, grad_in.at[1, r, 0], sibling, there)

    def eight(pos, along):
        others = []
        for step in (5, 4, 3, 2, 7, 6, 1):
            k, row = step // 2, gy if step % 2 == 0 else side
            others.append((step - 1, along(k, row), ((pos + k) % 4) * 2 + row))
        return pos * 2 + gy, others

    def received(ref, mine, r):
        return ref.at[1, r] if mine else ref.at[0, r, pl.ds(1, 3)]

    def scatter_again():
        for u, (mine, r) in enumerate(units):
            pos, _, pos2, along2 = orders[r]
            first[u].wait_recv(received(grad_in, mine, r))
            total = get_rows(grad_in.at[mine, r, 0]) if mine else grad[core, unit_rows(r, pos)]
            for k in (1, 2, 3):
                total = total + get_rows(grad_in.at[mine, r, k])
            total = jnp.concatenate([total, jnp.zeros((8, 128), F32)], axis=0)
            for j in range(8):
                value = total[j * SUB:j * SUB + 16]
                part[u, j] = value
                part_code[u, j] = encode_sub(value)
            sent = Group(part_in.at[u])
            for n, device, there in eight(pos2, along2)[1]:
                sent.send(part_code.at[u, there], part_in.at[u, n], device)
            scattered_again[u] = sent

    def gather():
        for u, (mine, r) in enumerate(units):
            _, _, pos2, along2 = orders[r]
            place, others = eight(pos2, along2)
            scattered_again[u].wait_recv()
            total = part[u, place]
            for n in range(7):
                total = total + decode_sub(part_in[u, n])
            whole_code[u, place] = encode_sub(total * (1.0 / math.sqrt(32768.0)))
            sent = Group(part_in.at[u])
            for _, device, _ in others:
                sent.send(whole_code.at[u, place], whole_code.at[u, place], device)
            gathered[u] = sent

    def gather_again():
        for u, (mine, r) in enumerate(units):
            along = orders[r][1]
            gathered[u].wait_recv()
            sent = Group(received(whole_in, mine, r))
            for k in (2, 1, 3):
                sent.send(whole_code.at[u], whole_in.at[mine, r, k], along(k, gy, (core + mine) % 2))
            if mine:
                sent.send(whole_code.at[u], whole_in.at[1, r, 0], sibling)
            gathered_again[u] = sent

    def store(mine, r, k, ref):
        lanes = aligned(channels((core + mine) % 2), 128, 128)
        grad_out[unit_rows(r, (orders[r][0] + 4 - k) % 4), lanes] = get_subs(ref, rows_here)

    def finish():
        for r in (0, 1):
            store(0, r, 0, whole_code.at[r])
        for u, (mine, r) in enumerate(units):
            gathered_again[u].wait_recv()
            for k in range(1 - mine, 4):
                store(mine, r, k, whole_in.at[mine, r, k])

    scattered_again, gathered, gathered_again = {}, {}, {}

    @pl.when(core == 1)
    def _():
        late[0].wait_recv()
        relay(1, other, 0)

    pl.when(core == 0)(relays[0].wait_recv)
    from_sibling.wait_recv()
    filter_products(0)
    scatter(0)

    @pl.loop(0, 4)
    def _(n):
        cols = aligned(n * 256, 256, 256)
        back[:, cols] = lax.dot_general(
            taps_t[...], cim[:, cols], (((1,), (0,)), ((), ())), preferred_element_type=F32
        )

    to_sibling = Group(back_in)
    for k in range(4):
        to_sibling.send(back.at[aligned((2 * k + 1 - core) * OWN, OWN, OWN)], back_in.at[k], sibling)

    @pl.when(core == 1)
    def _():
        for n in (0, 1):
            from_far[n].wait_recv()
            relay(2, far, n)

    @pl.when(core == 0)
    def _():
        relays[1].wait_recv()
        relays[2].wait_recv()

    filter_products(1)
    scatter(1)

    ring = Ring(Group, back_sum, zh, along_z(1), along_z(3), back_code, back_first, back_both)

    def start_ring():
        to_sibling.wait_recv()
        for k in range(4):
            back_sum[k] = back[aligned((2 * k + core) * OWN, OWN, OWN)] + back_in[k]
        ring.start()

    pl.when(core == 1)(start_ring)
    scatter_again()
    pl.when(core == 0)(start_ring)

    @pl.loop(0, 4)
    def _(n):
        cols = aligned(n * 256, 256, 256)
        z[:, cols] = jnp.dot(taps[...], field[:, cols], preferred_element_type=F32)

    plane_lane = lane[:, :PLANE]
    plane_column = column[:, :PLANE]
    for e in range(4):
        rows_of = []
        for b in (-1, 0, 1):
            total = None
            for c in (-1, 0, 1):
                term = None
                for a in (-1, 0, 1):
                    d = e - 1 + a
                    if d in (0, 1):
                        value = z[pl.ds(tap_index(a, b, c) * OWN, OWN), pl.ds(d * PLANE, PLANE)]
                        term = value if term is None else term + value
                if c:
                    out = WIDTH - 1 if c == 1 else 0
                    term = jnp.where(plane_column == out, 0.0, roll(term, -c))
                total = term if total is None else total + term
            rows_of.append(roll(total, -b * WIDTH) if b else total)
        before, centre, after = rows_of
        core_sum[e] = (
            centre
            + jnp.where(plane_lane < PLANE - WIDTH, after, 0.0)
            + jnp.where(plane_lane >= WIDTH, before, 0.0)
        )
        outward = jnp.where(gy == 0, before[:, :128], after[:, PLANE - 128:])
        row_sum[e] = jnp.where(row_side, outward, 0.0)

    def resp_row(n):
        return resp_in.at[:, pl.ds(2 * PLANE + n * 128, 128)]

    outer = Group(resp_in)
    outer.send(core_sum.at[0], resp_in.at[:, pl.ds(PLANE, PLANE)], (d_prev, gy, af))
    outer.send(core_sum.at[3], resp_in.at[:, pl.ds(0, PLANE)], (d_next, gy, af))
    outer.send(row_sum.at[1], resp_row(0), (gz, side, af))
    outer.send(row_sum.at[2], resp_row(1), (gz, side, af))
    outer.send(row_sum.at[0], resp_row(3), (d_prev, side, af))
    outer.send(row_sum.at[3], resp_row(2), (d_next, side, af))

    gather()

    ring.middle()

    gather_again()

    outer.wait_recv()
    for d, valid in ((0, gz > 0), (1, gz < 15)):
        total = core_sum[d + 1] + jnp.where(valid, resp_in[:, pl.ds(d * PLANE, PLANE)], 0.0)
        slab = resp_row(d)[...] + jnp.where(valid, resp_row(2 + d)[...], 0.0)
        slab = jnp.concatenate(
            [
                jnp.where(gy == 1, slab, 0.0),
                jnp.zeros((OWN, PLANE - 256), F32),
                jnp.where(gy == 0, slab, 0.0),
            ],
            axis=1,
        )
        both_out[0, :, d, :] = (total + slab).astype(BF16)

    for half, total in enumerate(ring.end()):
        for d in (0, 1):
            both_out[1, pl.ds(half * 16, 16), d, :] = total[:, d * PLANE:(d + 1) * PLANE].astype(BF16)

    finish()

    for n, (half, r) in enumerate(units):
        pl.when(core != half)(from_here[n].wait_send)
    @pl.when(core == 1)
    def _():
        for group in from_far + relays:
            group.wait_send()

    for group in groups:
        if group not in from_here + from_far + relays + [early[1], late[1]]:
            group.wait_send()


def shards(features, filters, cotangent):
    vmem = pl.BlockSpec(memory_space=pltpu.VMEM)
    both, grad = pl.pallas_call(
        kernel,
        out_shape=(
            pltpu.VMEM((2, OWN, 2, PLANE), BF16),
            pltpu.VMEM((PADDED, C), F32),
        ),
        in_specs=[pl.BlockSpec(memory_space=pl.ANY)] * 3,
        out_specs=(vmem,) * 2,
        scratch_shapes=[
            pltpu.VMEM((OWN, 2, PLANE), BF16),
            pltpu.VMEM((OWN, 2, PLANE), BF16),
            pltpu.VMEM((ROWS, C), BF16),
            pltpu.VMEM((C, ROWS), BF16),
            pltpu.VMEM((OWN, CELLS), BF16),
            pltpu.VMEM((OWN, CELLS), BF16),
            pltpu.VMEM((C, CELLS), BF16),
            pltpu.VMEM((OWN, 2 * PLANE + 4 * 128), BF16),
            pltpu.VMEM((ROWS, CELLS), BF16),
            pltpu.VMEM((C, CELLS), F32),
            pltpu.VMEM((4, OWN, CELLS), F32),
            pltpu.VMEM((4, OWN, CELLS), F32),
            pltpu.VMEM((6, 16, CELLS + 128), BF16),
            pltpu.VMEM((2, 16, CELLS + 128), BF16),
            pltpu.VMEM((2, 2, 16, CELLS + 128), BF16),
            pltpu.VMEM((ROWS, CELLS), F32),
            pltpu.VMEM((4, OWN, PLANE), F32),
            pltpu.VMEM((4, OWN, 128), F32),
            pltpu.VMEM((OWN, 2 * PLANE + 4 * 128), F32),
            pltpu.VMEM((2, PADDED, 128), F32),
            pltpu.VMEM((4, 4, CHUNK + 16, 128), BF16),
            pltpu.VMEM((2, 2, 4, CHUNK + 16, 128), BF16),
            pltpu.VMEM((4, 8, 16, 128), F32),
            pltpu.VMEM((4, 8, 16, 128), BF16),
            pltpu.VMEM((4, 7, 16, 128), BF16),
            pltpu.VMEM((CHUNK + 16, 128), F32),
            pltpu.VMEM((4, 8, 16, 128), BF16),
            pltpu.VMEM((2, 2, 4, 8, 16, 128), BF16),
            pltpu.SemaphoreType.DMA((3,)),
            pltpu.SemaphoreType.DMA((N_GROUPS,)),
            pltpu.SemaphoreType.DMA((N_GROUPS,)),
        ],
        compiler_params=pltpu.CompilerParams(
            collective_id=0, has_side_effects=True, vmem_limit_bytes=60 * 1024 * 1024
        ),
    )(
        features,
        cotangent,
        filters.reshape(ROWS, C),
    )
    return both[0], both[1], grad[:ROWS].reshape(filters.shape)


def solution(mesh):
    placed = (P("af", "gz", "gy"), P(None, None, None, "af", None), P("af", "gz", "gy"))
    return jax.shard_map(
        shards,
        mesh=mesh,
        in_specs=placed,
        out_specs=(P("af", "gz", "gy"), P("af", "gz", "gy"), P(None, None, None, "af", None)),
        check_vma=False,
    )
```

```python
import functools
import math

import jax
import jax.numpy as jnp
from jax import lax
from jax.experimental import pallas as pl
from jax.experimental.pallas import tpu as pltpu
from jax.sharding import PartitionSpec as P

MESH = pl.DeviceIdType.MESH
F32 = jnp.float32
BF16 = jnp.bfloat16
WIDTH = 64
PLANE = 512
CELLS = 1024
OWN = 32
C = 256
TAPS = 27
ROWS = TAPS * OWN
PADDED = 896
CHUNK = PADDED // 8
SUB = CHUNK // 8
N_GROUPS = 35


def tap_index(a, b, c):
    return ((a + 1) * 3 + (b + 1)) * 3 + (c + 1)


def roll(x, shift):
    return pltpu.roll(x, shift % x.shape[1], 1)


def aligned(start, size, unit):
    return pl.ds(pl.multiple_of(start, unit), size)


def encode(blocks):
    top = functools.reduce(jnp.maximum, [jnp.abs(block) for block in blocks])
    scale = jnp.maximum(top * 2.0**-7.75, 1e-30).astype(BF16)
    inverse = 1.0 / scale.astype(F32)
    codes = []
    for block in blocks:
        power = block * inverse
        for _ in range(4):
            power = power * power
        codes.append(jnp.where(block < 0, -power, power).astype(BF16))
    return codes, scale


def decode(codes, scale):
    scale = scale.astype(F32)
    blocks = []
    for code in codes:
        code = code.astype(F32)
        root = jnp.exp2(jnp.log2(jnp.maximum(jnp.abs(code), 2e-38)) * (1 / 16))
        root = jnp.where(code == 0, 0.0, root * scale)
        blocks.append(jnp.where(code < 0, -root, root))
    return blocks


def put_rows(ref, value):
    codes, scale = encode([value[i:i + 16] for i in range(0, CHUNK, 16)])
    ref[pl.ds(0, CHUNK)] = jnp.concatenate(codes, axis=0)
    ref[pl.ds(CHUNK, 16)] = scale


def get_rows(ref):
    codes = [ref[pl.ds(i, 16)] for i in range(0, CHUNK, 16)]
    return jnp.concatenate(decode(codes, ref[pl.ds(CHUNK, 16)]), axis=0)


def encode_sub(value):
    valid = lax.broadcasted_iota(jnp.int32, value.shape, 0) < SUB
    top = jnp.max(jnp.where(valid, jnp.abs(value), 0.0), axis=0, keepdims=True)
    scale = jnp.maximum(jnp.broadcast_to(top, value.shape) * 2.0**-7.75, 1e-30)
    scale = scale.astype(BF16).astype(F32)
    power = value * (1.0 / scale)
    for _ in range(4):
        power = power * power
    return jnp.where(valid, jnp.where(value < 0, -power, power), scale).astype(BF16)


def decode_sub(code):
    scale = jnp.broadcast_to(code.astype(F32)[SUB:SUB + 1], code.shape)
    return decode([code], scale)[0]


def get_subs(ref, rows):
    for j in range(8):
        rows[pl.ds(j * SUB, 16)] = decode_sub(ref[j])
    return rows[pl.ds(0, CHUNK)]


def put_columns(ref, value):
    codes, scale = encode([value[:, i:i + 128] for i in range(0, CELLS, 128)])
    ref[:, pl.ds(0, CELLS)] = jnp.concatenate(codes, axis=1)
    ref[:, pl.ds(CELLS, 128)] = scale


def get_columns(ref):
    codes = [ref[:, pl.ds(i, 128)] for i in range(0, CELLS, 128)]
    return jnp.concatenate(decode(codes, ref[:, pl.ds(CELLS, 128)]), axis=1)


class Ring:
    def __init__(self, group, chunks, pos, nxt, prv, out, first, both):
        self.group, self.chunks, self.pos, self.nxt, self.prv = group, chunks, pos, nxt, prv
        self.out, self.first, self.both = out, first, both
        self.early, self.late = group(first), group(both)

    def part(self, k, half):
        return self.chunks[(self.pos + k) % 4, pl.ds(half * 16, 16)]

    def start(self):
        put_columns(self.out.at[0], self.part(2, 0))
        self.early.send(self.out.at[0], self.first.at[0], self.nxt)
        put_columns(self.out.at[1], self.part(2, 1))
        self.early.send(self.out.at[1], self.first.at[1], self.prv)
        put_columns(self.out.at[2], self.part(1, 1))
        self.late.send(self.out.at[2], self.both.at[0, 1], self.nxt)
        put_columns(self.out.at[3], self.part(3, 0))
        self.late.send(self.out.at[3], self.both.at[1, 0], self.prv)

    def middle(self):
        self.early.wait_recv()
        put_columns(self.out.at[4], self.part(1, 0) + get_columns(self.first.at[0]))
        self.late.send(self.out.at[4], self.both.at[0, 0], self.nxt)
        put_columns(self.out.at[5], self.part(3, 1) + get_columns(self.first.at[1]))
        self.late.send(self.out.at[5], self.both.at[1, 1], self.prv)

    def end(self):
        self.late.wait_recv()
        return [
            self.part(0, half) + get_columns(self.both.at[0, half]) + get_columns(self.both.at[1, half])
            for half in (0, 1)
        ]


def kernel(
    feat_hbm, cot_hbm, taps_hbm, both_out, grad_out,
    feat_raw, cot_raw, taps, taps_t, feat, cot, field, cot_halo, cim,
    back, back_in, back_sum, back_code, back_first, back_both,
    z, core_sum, row_sum, resp_in,
    grad, grad_code, grad_in, part, part_code, part_in, rows_here, whole_code, whole_in,
    load_sem, send_sem, recv_sem,
):
    loads = [
        pltpu.make_async_copy(src, dst, load_sem.at[n])
        for n, (src, dst) in enumerate(((feat_hbm, feat_raw), (cot_hbm, cot_raw), (taps_hbm, taps)))
    ]
    for load in loads:
        load.start()
    gz = lax.axis_index("gz")
    gy = lax.axis_index("gy")
    af = lax.axis_index("af")
    py, px = gz // 4, gz % 4
    zh, core = af // 2, af % 2

    sibling = (gz, gy, zh * 2 + (1 - core))
    d_next, d_prev = (gz + 1) % 16, (gz + 15) % 16
    side = 1 - gy

    def along_x(k, row=gy, to=core):
        return (py * 4 + (px + k) % 4, row, zh * 2 + to)

    def along_y(k, row=gy, to=core):
        return (((py + k) % 4) * 4 + px, row, zh * 2 + to)

    def along_z(k, to=core):
        return (gz, gy, ((zh + k) % 4) * 2 + to)

    groups = []

    class Group:
        def __init__(self, size):
            self.index, self.size = len(groups), size
            groups.append(self)

        def send(self, src, dst, device, there=None):
            there = self.index if there is None else there
            pltpu.make_async_remote_copy(
                src_ref=src, dst_ref=dst,
                send_sem=send_sem.at[self.index], recv_sem=recv_sem.at[there],
                device_id=device, device_id_type=MESH,
            ).start()
            return self

        def wait_recv(self, size=None):
            size = self.size if size is None else size
            pltpu.make_async_copy(size, size, recv_sem.at[self.index]).wait()

        def wait_send(self):
            pltpu.make_async_copy(self.size, self.size, send_sem.at[self.index]).wait()

    partners = [sibling, (d_next, gy, af), (d_prev, gy, af)]
    partners += [(d_next, side, af), (d_prev, side, af), (gz, side, af)]
    for k in (1, 3):
        partners += [along_z(k), along_z(k, 1 - core)]
    for k in (1, 2, 3):
        for along in (along_x, along_y):
            partners += [along(k), along(k, side), along(k, gy, 1 - core)]
    barrier = pltpu.get_barrier_semaphore()
    for partner in partners:
        pl.semaphore_signal(barrier, inc=1, device_id=partner, device_id_type=MESH)

    def lay_flat(n, raw, flat):
        loads[n].wait()
        for d in (0, 1):
            flat[:, pl.ds(d * PLANE, PLANE)] = raw[:, d, :]

    lay_flat(0, feat_raw, feat)
    pl.semaphore_wait(barrier, len(partners))

    def block(channels_of):
        return field.at[aligned(channels_of * OWN, OWN, OWN)]

    pair = 1 + 2 * (zh % 2)
    other = 4 - pair
    far = 2

    def of_chip(k, number):
        return block(((zh + k) % 4) * 2 + number)

    early = [Group(feat), Group(feat)]
    late = [Group(feat), Group(feat)]
    from_far = [Group(feat), Group(feat)]
    relays = [Group(field.at[pl.ds(0, 2 * OWN)]) for _ in range(3)]
    k_early = pair + core * (other - pair)
    early[0].send(feat, block(af), along_z(k_early, 1), early[0].index + core)
    late[0].send(feat, block(af), along_z(4 - k_early, 1), late[0].index + core)
    from_sibling = Group(block(af)).send(feat, block(af), sibling)
    lay_flat(1, cot_raw, cot)

    edge = (1 - gy) * (PLANE - 128)
    low_edge = cot.at[:, aligned(edge, 128, 128)]
    high_edge = cot.at[:, aligned(edge + PLANE, 128, 128)]

    def halo(n):
        return cot_halo.at[:, pl.ds(2 * PLANE + n * 128, 128)]

    halos = Group(cot_halo)
    halos.send(low_edge, halo(3), (d_prev, side, af))
    halos.send(high_edge, halo(0), (d_next, side, af))
    halos.send(cot.at[:, pl.ds(0, PLANE)], cot_halo.at[:, pl.ds(PLANE, PLANE)], (d_prev, gy, af))
    halos.send(cot.at[:, pl.ds(PLANE, PLANE)], cot_halo.at[:, pl.ds(0, PLANE)], (d_next, gy, af))
    halos.send(low_edge, halo(1), (gz, side, af))
    halos.send(high_edge, halo(2), (gz, side, af))
    block(af)[...] = feat[...]
    loads[2].wait()
    taps_t[...] = taps[...].T

    def relay(n, k, number):
        rows = of_chip(k, number)
        relays[n].send(rows, rows, sibling)

    @pl.when(core == 1)
    def _():
        for n, k, back in ((0, pair, other), (1, other, pair)):
            early[n].wait_recv()
            rows = of_chip(k, n)
            from_far[n].send(rows, rows, along_z(back))
            relay(n, k, n)
        late[1].wait_recv()
        relay(0, pair, 1)

    halos.wait_recv()
    lane = lax.broadcasted_iota(jnp.int32, (OWN, PLANE + 128), 1)
    column = lane % WIDTH
    slab_lane = lax.broadcasted_iota(jnp.int32, (OWN, 128), 1)
    row_side = (slab_lane < WIDTH) == (gy == 0)
    inside = (gz > 0, None, None, gz < 15)
    for e in range(4):
        if e in (1, 2):
            plane = cot[:, pl.ds((e - 1) * PLANE, PLANE)].astype(F32)
        else:
            plane = cot_halo[:, pl.ds((e // 3) * PLANE, PLANE)].astype(F32)
        rows = jnp.where(row_side, halo(e)[...].astype(F32), 0.0)
        base = jnp.concatenate([plane, rows], axis=1)
        if inside[e] is not None:
            base = jnp.where(inside[e], base, 0.0)
        for c in (-1, 0, 1):
            if c == 0:
                moved = base
            else:
                moved = jnp.where(column == (0 if c == 1 else WIDTH - 1), 0.0, roll(base, c))
            tall = roll(moved, WIDTH).astype(BF16)
            moved = moved.astype(BF16)
            for a in (-1, 0, 1):
                d = e - 1 + a
                if d not in (0, 1):
                    continue
                for b in (-1, 0, 1):
                    piece = {-1: tall[:, 128:], 0: moved[:, :PLANE], 1: tall[:, :PLANE]}[b]
                    cim[pl.ds(tap_index(a, b, c) * OWN, OWN), pl.ds(d * PLANE, PLANE)] = piece

    def channels(half):
        return ((zh // 2 + half) % 2) * 128

    def filter_products(half):
        grad[half, pl.ds(0, ROWS)] = lax.dot_general(
            cim[...], field[aligned(channels(half), 128, 128)],
            (((1,), (1,)), ((), ())), preferred_element_type=F32,
        )
        grad[half, pl.ds(ROWS, PADDED - ROWS)] = jnp.zeros((PADDED - ROWS, 128), F32)

    orders = ((px, along_x, py, along_y), (py, along_y, px, along_x))

    def unit_rows(r, i):
        return aligned(r * 4 * CHUNK + i * CHUNK, CHUNK, 16)

    units = [(mine, r) for mine in (0, 1) for r in (0, 1)]
    first = [Group(grad_in.at[0, r, pl.ds(1, 3)]) for half, r in units]
    from_here = [Group(grad_code.at[0, 0]) for half, r in units]

    def scatter(half):
        relation = (core + half) % 2
        for r, (pos, along, _, _) in enumerate(orders):
            n = half * 2 + r
            there = first[0].index + relation * 2 + r
            for k in (2, 1, 3):
                code = grad_code.at[n, k]
                put_rows(code, grad[half, unit_rows(r, (pos + k) % 4)])
                first[n].send(code, grad_in.at[relation, r, k], along(k, gy, half), there)

            @pl.when(core != half)
            def _():
                code = grad_code.at[n, 0]
                put_rows(code, grad[half, unit_rows(r, pos)])
                from_here[n].send(code, grad_in.at[1, r, 0], sibling, there)

    def eight(pos, along):
        others = []
        for step in (5, 4, 3, 2, 7, 6, 1):
            k, row = step // 2, gy if step % 2 == 0 else side
            others.append((step - 1, along(k, row), ((pos + k) % 4) * 2 + row))
        return pos * 2 + gy, others

    def received(ref, mine, r):
        return ref.at[1, r] if mine else ref.at[0, r, pl.ds(1, 3)]

    def scatter_again():
        for u, (mine, r) in enumerate(units):
            pos, _, pos2, along2 = orders[r]
            first[u].wait_recv(received(grad_in, mine, r))
            total = get_rows(grad_in.at[mine, r, 0]) if mine else grad[core, unit_rows(r, pos)]
            for k in (1, 2, 3):
                total = total + get_rows(grad_in.at[mine, r, k])
            total = jnp.concatenate([total, jnp.zeros((8, 128), F32)], axis=0)
            for j in range(8):
                value = total[j * SUB:j * SUB + 16]
                part[u, j] = value
                part_code[u, j] = encode_sub(value)
            sent = Group(part_in.at[u])
            for n, device, there in eight(pos2, along2)[1]:
                sent.send(part_code.at[u, there], part_in.at[u, n], device)
            scattered_again[u] = sent

    def gather():
        for u, (mine, r) in enumerate(units):
            _, _, pos2, along2 = orders[r]
            place, others = eight(pos2, along2)
            scattered_again[u].wait_recv()
            total = part[u, place]
            for n in range(7):
                total = total + decode_sub(part_in[u, n])
            whole_code[u, place] = encode_sub(total * (1.0 / math.sqrt(32768.0)))
            sent = Group(part_in.at[u])
            for _, device, _ in others:
                sent.send(whole_code.at[u, place], whole_code.at[u, place], device)
            gathered[u] = sent

    def gather_again():
        for u, (mine, r) in enumerate(units):
            along = orders[r][1]
            gathered[u].wait_recv()
            sent = Group(received(whole_in, mine, r))
            for k in (2, 1, 3):
                sent.send(whole_code.at[u], whole_in.at[mine, r, k], along(k, gy, (core + mine) % 2))
            if mine:
                sent.send(whole_code.at[u], whole_in.at[1, r, 0], sibling)
            else:
                whole_in[0, r, 0] = whole_code[u]
            gathered_again[u] = sent

    def finish():
        for half in (1, 0):
            mine = (core + half) % 2
            lanes = aligned(channels(half), 128, 128)
            for r in (0, 1):
                for n in (0, 1):
                    pl.when(mine == n)(gathered_again[2 * n + r].wait_recv)
                for k in range(4):
                    rows = unit_rows(r, (orders[r][0] + 4 - k) % 4)
                    grad_out[rows, lanes] = get_subs(whole_in.at[mine, r, k], rows_here)

    scattered_again, gathered, gathered_again = {}, {}, {}

    @pl.when(core == 1)
    def _():
        late[0].wait_recv()
        relay(1, other, 0)

    pl.when(core == 0)(relays[0].wait_recv)
    from_sibling.wait_recv()
    filter_products(0)
    scatter(0)

    @pl.loop(0, 4)
    def _(n):
        cols = aligned(n * 256, 256, 256)
        back[:, cols] = lax.dot_general(
            taps_t[...], cim[:, cols], (((1,), (0,)), ((), ())), preferred_element_type=F32
        )

    to_sibling = Group(back_in)
    for k in range(4):
        to_sibling.send(back.at[aligned((2 * k + 1 - core) * OWN, OWN, OWN)], back_in.at[k], sibling)

    @pl.when(core == 1)
    def _():
        for n in (0, 1):
            from_far[n].wait_recv()
            relay(2, far, n)

    @pl.when(core == 0)
    def _():
        relays[1].wait_recv()
        relays[2].wait_recv()

    filter_products(1)
    scatter(1)

    ring = Ring(Group, back_sum, zh, along_z(1), along_z(3), back_code, back_first, back_both)

    def start_ring():
        to_sibling.wait_recv()
        for k in range(4):
            back_sum[k] = back[aligned((2 * k + core) * OWN, OWN, OWN)] + back_in[k]
        ring.start()

    pl.when(core == 1)(start_ring)
    scatter_again()
    pl.when(core == 0)(start_ring)

    @pl.loop(0, 4)
    def _(n):
        cols = aligned(n * 256, 256, 256)
        z[:, cols] = jnp.dot(taps[...], field[:, cols], preferred_element_type=F32)

    plane_lane = lane[:, :PLANE]
    plane_column = column[:, :PLANE]
    for e in range(4):
        rows_of = []
        for b in (-1, 0, 1):
            total = None
            for c in (-1, 0, 1):
                term = None
                for a in (-1, 0, 1):
                    d = e - 1 + a
                    if d in (0, 1):
                        value = z[pl.ds(tap_index(a, b, c) * OWN, OWN), pl.ds(d * PLANE, PLANE)]
                        term = value if term is None else term + value
                if c:
                    out = WIDTH - 1 if c == 1 else 0
                    term = jnp.where(plane_column == out, 0.0, roll(term, -c))
                total = term if total is None else total + term
            rows_of.append(roll(total, -b * WIDTH) if b else total)
        before, centre, after = rows_of
        core_sum[e] = (
            centre
            + jnp.where(plane_lane < PLANE - WIDTH, after, 0.0)
            + jnp.where(plane_lane >= WIDTH, before, 0.0)
        )
        outward = jnp.where(gy == 0, before[:, :128], after[:, PLANE - 128:])
        row_sum[e] = jnp.where(row_side, outward, 0.0)

    def resp_row(n):
        return resp_in.at[:, pl.ds(2 * PLANE + n * 128, 128)]

    outer = Group(resp_in)
    outer.send(core_sum.at[0], resp_in.at[:, pl.ds(PLANE, PLANE)], (d_prev, gy, af))
    outer.send(core_sum.at[3], resp_in.at[:, pl.ds(0, PLANE)], (d_next, gy, af))
    outer.send(row_sum.at[1], resp_row(0), (gz, side, af))
    outer.send(row_sum.at[2], resp_row(1), (gz, side, af))
    outer.send(row_sum.at[0], resp_row(3), (d_prev, side, af))
    outer.send(row_sum.at[3], resp_row(2), (d_next, side, af))

    gather()

    ring.middle()

    gather_again()

    outer.wait_recv()
    for d, valid in ((0, gz > 0), (1, gz < 15)):
        total = core_sum[d + 1] + jnp.where(valid, resp_in[:, pl.ds(d * PLANE, PLANE)], 0.0)
        slab = resp_row(d)[...] + jnp.where(valid, resp_row(2 + d)[...], 0.0)
        slab = jnp.concatenate(
            [
                jnp.where(gy == 1, slab, 0.0),
                jnp.zeros((OWN, PLANE - 256), F32),
                jnp.where(gy == 0, slab, 0.0),
            ],
            axis=1,
        )
        both_out[0, :, d, :] = (total + slab).astype(BF16)

    for half, total in enumerate(ring.end()):
        for d in (0, 1):
            both_out[1, pl.ds(half * 16, 16), d, :] = total[:, d * PLANE:(d + 1) * PLANE].astype(BF16)

    finish()

    for n, (half, r) in enumerate(units):
        pl.when(core != half)(from_here[n].wait_send)
    @pl.when(core == 1)
    def _():
        for group in from_far + relays:
            group.wait_send()

    for group in groups:
        if group not in from_here + from_far + relays + [early[1], late[1]]:
            group.wait_send()


def shards(features, filters, cotangent):
    vmem = pl.BlockSpec(memory_space=pltpu.VMEM)
    both, grad = pl.pallas_call(
        kernel,
        out_shape=(
            pltpu.VMEM((2, OWN, 2, PLANE), BF16),
            pltpu.VMEM((PADDED, C), F32),
        ),
        in_specs=[pl.BlockSpec(memory_space=pl.ANY)] * 3,
        out_specs=(vmem,) * 2,
        scratch_shapes=[
            pltpu.VMEM((OWN, 2, PLANE), BF16),
            pltpu.VMEM((OWN, 2, PLANE), BF16),
            pltpu.VMEM((ROWS, C), BF16),
            pltpu.VMEM((C, ROWS), BF16),
            pltpu.VMEM((OWN, CELLS), BF16),
            pltpu.VMEM((OWN, CELLS), BF16),
            pltpu.VMEM((C, CELLS), BF16),
            pltpu.VMEM((OWN, 2 * PLANE + 4 * 128), BF16),
            pltpu.VMEM((ROWS, CELLS), BF16),
            pltpu.VMEM((C, CELLS), F32),
            pltpu.VMEM((4, OWN, CELLS), F32),
            pltpu.VMEM((4, OWN, CELLS), F32),
            pltpu.VMEM((6, 16, CELLS + 128), BF16),
            pltpu.VMEM((2, 16, CELLS + 128), BF16),
            pltpu.VMEM((2, 2, 16, CELLS + 128), BF16),
            pltpu.VMEM((ROWS, CELLS), F32),
            pltpu.VMEM((4, OWN, PLANE), F32),
            pltpu.VMEM((4, OWN, 128), F32),
            pltpu.VMEM((OWN, 2 * PLANE + 4 * 128), F32),
            pltpu.VMEM((2, PADDED, 128), F32),
            pltpu.VMEM((4, 4, CHUNK + 16, 128), BF16),
            pltpu.VMEM((2, 2, 4, CHUNK + 16, 128), BF16),
            pltpu.VMEM((4, 8, 16, 128), F32),
            pltpu.VMEM((4, 8, 16, 128), BF16),
            pltpu.VMEM((4, 7, 16, 128), BF16),
            pltpu.VMEM((CHUNK + 16, 128), F32),
            pltpu.VMEM((4, 8, 16, 128), BF16),
            pltpu.VMEM((2, 2, 4, 8, 16, 128), BF16),
            pltpu.SemaphoreType.DMA((3,)),
            pltpu.SemaphoreType.DMA((N_GROUPS,)),
            pltpu.SemaphoreType.DMA((N_GROUPS,)),
        ],
        compiler_params=pltpu.CompilerParams(
            collective_id=0, has_side_effects=True, vmem_limit_bytes=60 * 1024 * 1024
        ),
    )(
        features,
        cotangent,
        filters.reshape(ROWS, C),
    )
    return both[0], both[1], grad[:ROWS].reshape(filters.shape)


def solution(mesh):
    placed = (P("af", "gz", "gy"), P(None, None, None, "af", None), P("af", "gz", "gy"))
    return jax.shard_map(
        shards,
        mesh=mesh,
        in_specs=placed,
        out_specs=(P("af", "gz", "gy"), P("af", "gz", "gy"), P(None, None, None, "af", None)),
        check_vma=False,
    )
```
